32 devices in a mesh: groups: 2 (over y), gx: 4 (over x, core), gy: 4 (over z).
Axes of the slice: x: 2, y: 2, z: 4, core: 2. Of those that a mesh axis runs over, the one named last changes fastest.
Arguments:
- layer_class: int32 [64, 64, 128], P(('groups', 'gx'), 'gy'), parts along dimension 0, may hold values from 0 to 5
- permittivity: float32 [6], replicated, may hold values from 2 to 8
- mobility: float32 [6], replicated, may hold values from 0.1 to 10
- capture: float32 [6], replicated, may hold values from 0.02 to 0.4
- potential: float32 [64, 64, 128], P(('groups', 'gx'), 'gy'), parts along dimension 0, may hold values from -2.4 to 2.4
- rhs_psi: float32 [64, 64, 128], P(('groups', 'gx'), 'gy'), parts along dimension 0, may hold values from -48 to 48
- rhs_n: float32 [64, 64, 128], P(('groups', 'gx'), 'gy'), parts along dimension 0, may hold values from -24 to 24
Outputs:
- potential_update: float32 [64, 64, 128], P(('groups', 'gx'), 'gy'), parts along dimension 0
- density_update: float32 [64, 64, 128], P(('groups', 'gx'), 'gy'), parts along dimension 0
The draws below stay inside these ranges and needn't reach their ends.
There are 2 independent parts, one for each index of `groups`. The reference program is written for one: setup_inputs(seed, part) draws one part's arguments, and reference() takes and returns one part's arrays. A program takes and returns all parts, laid end to end along the dimension named above; an argument that names none is the same for every part. Nothing has to cross between parts.
All inputs are finite; a program needn't handle non-finite values.
Results may differ from the reference program's by a relative error of at most 0.0003.
Values sent between devices are 32-bit elements; how exact they have to be, the bound alone decides.
No kernel may reach another device: no remote copies, remote signals or barrier semaphores. Data moves between devices by JAX's collectives and lax.ppermute only.
A program may use at most 64 MiB of HBM per device.

```python
import math
import jax
import jax.numpy as jnp

NZ = 128
LEVELS = 4
COARSE_ITERS = 20
MATERIALS = 6
NX = 32
NY = 64


def touch_ends(values, key, low, largest):
    spot = [jax.random.randint(jax.random.fold_in(key, axis), (), 0, length) for axis, length in enumerate(values.shape)]
    main_axis = values.shape.index(max(values.shape))
    next_to = spot[:main_axis] + [(spot[main_axis] + 1) % values.shape[main_axis]] + spot[main_axis + 1:]
    return values.at[tuple(spot)].set(low).at[tuple(next_to)].set(largest)


def levels(rng, shape, cuts, low, high):
    def one(axis_at, shards_of):
        steps = jax.random.uniform(jax.random.fold_in(jax.random.fold_in(rng, 6), axis_at), (shards_of,), jnp.float32, low / len(cuts), high / len(cuts))
        return jnp.repeat(jnp.exp(steps), shape[axis_at] // shards_of).reshape((-1,) + (1,) * (len(shape) - axis_at - 1))

    factor_of = one(*cuts[0])
    for cut in cuts[1:]:
        factor_of = factor_of * one(*cut)
    return factor_of


def gaussian(key, dims, deviation, limit, pieces=(), kind=jnp.bfloat16):
    values = jax.random.normal(key, dims, jnp.float32) * deviation
    if len(pieces) > 0:
        values = levels(key, dims, pieces, -0.22, 0.18) * values
    return jnp.clip(values, min=-limit, max=limit).astype(kind)


def setup_inputs(seed: int = 0, part: int = 0) -> dict:
    key_of = jax.random.split(jax.random.key(seed), 8)
    part_keys = jax.random.split(jax.random.fold_in(key_of[7], part), 8)
    return {
        "layer_class": touch_ends(jax.random.randint(part_keys[0], (NX, NY, NZ), 0, MATERIALS), jax.random.fold_in(part_keys[0], 1), 0, MATERIALS - 1).astype(jnp.int32),
        "permittivity": jnp.clip(jnp.exp(jax.random.uniform(key_of[1], (MATERIALS,), jnp.float32, math.log(2.0), math.log(8.0))), 2.0, 8.0),
        "mobility": jnp.clip(jnp.exp(jax.random.uniform(key_of[2], (MATERIALS,), jnp.float32, math.log(0.1), math.log(10.0))), 0.1, 10.0),
        "capture": jnp.clip(jnp.exp(jax.random.uniform(key_of[3], (MATERIALS,), jnp.float32, math.log(0.02), math.log(0.4))), 0.02, 0.4),
        "potential": gaussian(part_keys[4], (NX, NY, NZ), 0.4, 2.4, ((0, 4), (1, 4)), jnp.float32),
        "rhs_psi": gaussian(part_keys[5], (NX, NY, NZ), 8.0, 48.0, ((0, 4), (1, 4)), jnp.float32),
        "rhs_n": gaussian(part_keys[6], (NX, NY, NZ), 4.0, 24.0, ((0, 4), (1, 4)), jnp.float32),
    }


OMEGA = 0.8


def bernoulli(values):
    nearly_zero = jnp.abs(values) < 1e-3
    guarded = jnp.where(nearly_zero, 1.0, values)
    return jnp.where(nearly_zero, 1.0 - 0.5 * values + values * values / 12.0, guarded / jnp.expm1(guarded))


def neighbours(array):
    center = array[..., 1:-1, 1:-1, :]
    pad_widths = [(0, 0)] * (array.ndim - 1) + [(1, 1)]
    vertical = jnp.pad(center, pad_widths)
    return center, [array[..., 2:, 1:-1, :], array[..., :-2, 1:-1, :], array[..., 1:-1, 2:, :], array[..., 1:-1, :-2, :], vertical[..., 2:], vertical[..., :-2]]


def assemble_operator(coefficients, factor):
    center, beside = neighbours(coefficients)
    diag_poisson = jnp.zeros_like(center[0])
    diag_density = center[3]
    couplings = []
    for other in beside:
        conduct = 0.5 * (center[0] + other[0]) * factor
        motion = 0.5 * (center[1] + other[1]) * factor
        gradient = other[2] - center[2]
        diag_poisson = diag_poisson + conduct
        diag_density = diag_density + motion * bernoulli(-gradient)
        couplings.append(jnp.stack([conduct, motion * bernoulli(gradient)]))
    return jnp.stack([diag_poisson, diag_density]), jnp.stack(couplings)


def apply_operator(operator, field):
    diagonal, couplings = operator
    center, beside = neighbours(field)
    result = diagonal * center
    for position in range(6):
        result = result - couplings[position] * beside[position]
    return result


def jacobi_sweep(operator, field, source):
    center = field[..., 1:-1, 1:-1, :]
    return center + OMEGA * (source - apply_operator(operator, field)) / operator[0]


def pad_lateral(array):
    return jnp.pad(array, [(0, 0)] * (array.ndim - 3) + [(1, 1), (1, 1), (0, 0)])


def restrict_mean(array):
    leading = array.shape[:-3]
    rows, columns, layers = array.shape[-3], array.shape[-2], array.shape[-1]
    blocks = array.reshape(leading + (rows // 2, 2, columns // 2, 2, layers // 2, 2))
    return jnp.sum(blocks, axis=(-5, -3, -1)) * 0.125


def prolong(array):
    return jnp.repeat(jnp.repeat(jnp.repeat(array, 2, axis=-3), 2, axis=-2), 2, axis=-1)


def material_fields(layer_class, permittivity, mobility, capture, potential):
    classes = jnp.arange(permittivity.shape[0], dtype=jnp.int32)
    same_class = layer_class[None] == classes[:, None, None, None]

    def select_table(table):
        return jnp.sum(jnp.where(same_class, table[:, None, None, None], 0.0), axis=0)

    return jnp.stack([select_table(permittivity), select_table(mobility), potential, select_table(capture)])


def reference(layer_class, permittivity, mobility, capture, potential, rhs_psi, rhs_n):
    hierarchy = [material_fields(layer_class, permittivity, mobility, capture, potential)]
    for grid_level in range(1, LEVELS):
        hierarchy.append(restrict_mean(hierarchy[-1]))

    def descend(grid_level, source):
        operator = assemble_operator(pad_lateral(hierarchy[grid_level]), 0.25 ** grid_level)
        iterate = OMEGA * source / operator[0]
        if grid_level == LEVELS - 1:
            for iteration in range(COARSE_ITERS - 1):
                iterate = jacobi_sweep(operator, pad_lateral(iterate), source)
            return iterate
        iterate = jacobi_sweep(operator, pad_lateral(iterate), source)
        residual = source - apply_operator(operator, pad_lateral(iterate))
        iterate = iterate + prolong(descend(grid_level + 1, restrict_mean(residual)))
        for iteration in range(2):
            iterate = jacobi_sweep(operator, pad_lateral(iterate), source)
        return iterate

    result = descend(0, jnp.stack([rhs_psi, rhs_n]))
    return result[0], result[1]
```

```python
import functools
import jax
import jax.numpy as jnp
from jax import lax
from jax.experimental import pallas as pl
from jax.experimental.pallas import tpu as pltpu
from jax.sharding import PartitionSpec as P

OMEGA = 0.8
COARSE_ITERS = 20
RIM = 4
LANES = 128
VMEM = pl.BlockSpec(memory_space=pltpu.VMEM)
SMEM = pl.BlockSpec(memory_space=pltpu.SMEM)


def params(mib):
    return pltpu.CompilerParams(vmem_limit_bytes=mib * 1024 * 1024)


def bernoulli(x):
    t = x * x
    series = 1.0 - 0.5 * x + t * (1 / 12 + t * (-1 / 720 + t * (1 / 30240)))
    near = t < 0.25
    guarded = jnp.where(near, 1.0, x)
    return jnp.where(near, series, guarded / (jnp.exp(guarded) - 1.0))


def iota(shape, dim):
    return lax.broadcasted_iota(jnp.int32, shape, dim)


def up(v, step, dim):
    return pltpu.roll(v, v.shape[dim] - step, dim)


def down(v, step, dim):
    return pltpu.roll(v, step, dim)


def rim_y_kernel(cls, pot, fp, fn, out_a, out_b):
    even = lax.axis_index("gy") % 2 == 0
    length = cls.shape[1]
    for pair, (first, second) in enumerate(((cls, pot), (fp, fn))):
        lo, hi = (
            jnp.concatenate(
                [r[:, at : at + RIM, :].astype(jnp.float32) for r in (first, second)], axis=1
            )
            for at in (0, length - RIM)
        )
        out_a[pair] = jnp.where(even, hi, lo)
        out_b[pair] = jnp.where(even, lo, hi)


def rim_x_kernel(cls, pot, fp, fn, in_a, in_b, out, out_a, out_b):
    y, ny = lax.axis_index("gy"), lax.axis_size("gy")
    even_x, even_y = lax.axis_index("gx") % 2 == 0, y % 2 == 0
    planes, length = cls.shape[0], cls.shape[1]
    row = iota((planes, 2 * RIM, LANES), 1)
    for pair, refs in enumerate(((cls, pot), (fp, fn))):
        a, b = in_a[pair], in_b[pair]
        hi, lo = jnp.where(even_y, a, b), jnp.where(even_y, b, a)
        for slot, ref in enumerate(refs):
            field = 2 * pair + slot
            outside = -1.0 if field == 0 else 0.0
            h, l = jnp.where(y == ny - 1, outside, hi), jnp.where(y == 0, outside, lo)
            if slot == 0:
                l = down(l, RIM, 1)
            else:
                h = down(h, RIM, 1)
            out[field, :, 0:length, :] = ref[...].astype(jnp.float32)
            out[field, :, length : length + 2 * RIM, :] = jnp.where(row < RIM, h, l)
        for slot in range(2):
            field = 2 * pair + slot
            lo_x, hi_x = out[field, 0:RIM], out[field, planes - RIM : planes]
            out_a[field] = jnp.where(even_x, hi_x, lo_x)
            out_b[field] = jnp.where(even_x, lo_x, hi_x)


W_P, GX, GY, GZ, W_N, XP, XM, YP, YM, ZP, ZM, WF_P, WF_N, U_P, U_N = range(15)
KEPT = 15


def coupled_fine(kept, u, i, poisson):
    v = u(i)
    if poisson:
        xp, xm, yp, ym, zp, zm = GX, GX, GY, GY, GZ, GZ
    else:
        xp, xm, yp, ym, zp, zm = XP, XM, YP, YM, ZP, ZM
    s = kept[xp, i] * u(i + 1) + kept[xm, i - 1] * u(i - 1)
    s = s + (kept[yp, i] * up(v, 1, 0) + down(kept[ym, i] * v, 1, 0))
    return s + (kept[zp, i] * up(v, 1, 1) + down(kept[zm, i] * v, 1, 1))


def halve_lanes(a, b):
    lane = iota(a.shape, 1)
    at = (2 * lane) % LANES
    a = jnp.take_along_axis(a + up(a, 1, 1), at, axis=1)
    b = jnp.take_along_axis(b + up(b, 1, 1), at, axis=1)
    return jnp.where(lane < LANES // 2, a, b)


def first_kernel(eps_t, mob_t, cap_t, mid, in_a, in_b, kept, block, fld, work, tmp):
    x, nx = lax.axis_index("gx"), lax.axis_size("gx")
    even = x % 2 == 0
    planes = mid.shape[1]
    rows = mid.shape[2]
    own = rows - 2 * RIM
    total = planes + 2 * RIM
    EPS, MOB, POT, CAP, F_P, F_N, D_P, D_N = range(8)
    classes = eps_t.shape[0]

    def materials(i, c, pot, fp, fn):
        eps, mob, cap = jnp.zeros_like(c), jnp.zeros_like(c), jnp.zeros_like(c)
        for k in range(classes):
            same = c == float(k)
            eps = jnp.where(same, eps_t[k], eps)
            mob = jnp.where(same, mob_t[k], mob)
            cap = jnp.where(same, cap_t[k], cap)
        fld[EPS, i], fld[MOB, i], fld[POT, i], fld[CAP, i] = eps, mob, pot, cap
        fld[F_P, i], fld[F_N, i] = fp, fn

    def low(i, _):
        v = [jnp.where(even, in_b[f, i], in_a[f, i]) for f in range(4)]
        materials(i, *[jnp.where(x == 0, -1.0 if f == 0 else 0.0, v[f]) for f in range(4)])
        return 0

    def middle(i, _):
        materials(i + RIM, *[mid[f, i] for f in range(4)])
        return 0

    def high(i, _):
        v = [jnp.where(even, in_a[f, i], in_b[f, i]) for f in range(4)]
        materials(
            i + RIM + planes,
            *[jnp.where(x == nx - 1, -1.0 if f == 0 else 0.0, v[f]) for f in range(4)],
        )
        return 0

    lax.fori_loop(0, RIM, low, 0)
    lax.fori_loop(0, planes, middle, 0)
    lax.fori_loop(0, RIM, high, 0)

    shape = (rows, LANES)
    lane = iota(shape, 1)
    ends = (lane == 0) | (lane == LANES - 1)
    top = lane == LANES - 1

    def x_faces(i):
        eps, mob, pot = fld[EPS, i], fld[MOB, i], fld[POT, i]
        kept[GX, i] = 0.5 * (eps + fld[EPS, i + 1])
        k = 0.5 * (mob + fld[MOB, i + 1])
        delta = fld[POT, i + 1] - pot
        kb = k * bernoulli(delta)
        kept[XP, i] = kb
        kept[XM, i] = kb + k * delta

    x_faces(0)

    def operators(i, _):
        x_faces(i)
        eps, mob, pot = fld[EPS, i], fld[MOB, i], fld[POT, i]
        gy = 0.5 * (eps + up(eps, 1, 0))
        k = 0.5 * (mob + up(mob, 1, 0))
        delta = up(pot, 1, 0) - pot
        yp = k * bernoulli(delta)
        ym = yp + k * delta
        gz = jnp.where(top, 0.0, 0.5 * (eps + up(eps, 1, 1)))
        k = jnp.where(top, 0.0, 0.5 * (mob + up(mob, 1, 1)))
        delta = up(pot, 1, 1) - pot
        zp = k * bernoulli(delta)
        zm = zp + k * delta
        kept[GY, i], kept[YP, i], kept[YM, i] = gy, yp, ym
        kept[GZ, i], kept[ZP, i], kept[ZM, i] = gz, zp, zm
        d_p = (kept[GX, i] + kept[GX, i - 1]) + (gy + down(gy, 1, 0)) + (gz + down(gz, 1, 1))
        d_p = d_p + jnp.where(ends, 0.5 * eps, 0.0)
        d_n = (kept[XM, i] + kept[XP, i - 1]) + (ym + down(yp, 1, 0)) + (zm + down(zp, 1, 1))
        d_n = d_n + jnp.where(ends, 0.5 * mob * bernoulli(pot), 0.0) + fld[CAP, i]
        inside = eps > 0.0
        w_p = jnp.where(inside, OMEGA / jnp.where(inside, d_p, 1.0), 0.0)
        w_n = jnp.where(inside, OMEGA / jnp.where(inside, d_n, 1.0), 0.0)
        kept[W_P, i], kept[W_N, i] = w_p, w_n
        kept[WF_P, i], kept[WF_N, i] = w_p * fld[F_P, i], w_n * fld[F_N, i]
        fld[D_P, i], fld[D_N, i] = d_p, d_n
        return 0

    lax.fori_loop(1, total - 1, operators, 0)

    def sweep(i, _):
        for poisson, w, wf, u in ((True, W_P, WF_P, U_P), (False, W_N, WF_N, U_N)):
            s = coupled_fine(kept, lambda j: kept[wf, j], i, poisson)
            kept[u, i] = (2.0 - OMEGA) * kept[wf, i] + kept[w, i] * s
        return 0

    lax.fori_loop(2, total - 2, sweep, 0)

    def residual(i, poisson, f, d, u):
        s = coupled_fine(kept, lambda j: kept[u, j], i, poisson)
        return fld[f, i] - fld[d, i] * kept[u, i] + s

    def halved(v):
        tmp[...] = v
        return tmp[0 : own : 2, :] + tmp[1 : own : 2, :]

    def coarse(i, _):
        at = RIM + 2 * i
        r_p = residual(at, True, F_P, D_P, U_P) + residual(at + 1, True, F_P, D_P, U_P)
        r_n = residual(at, False, F_N, D_N, U_N) + residual(at + 1, False, F_N, D_N, U_N)
        values = [r_p, r_n] + [fld[f, at] + fld[f, at + 1] for f in (EPS, MOB, CAP, POT)]
        for k, v in enumerate(values):
            work[k] = v[0:own]
        even_odd = [
            work[k, pl.ds(0, own // 2, stride=2), :] + work[k, pl.ds(1, own // 2, stride=2), :]
            for k in range(6)
        ]
        for k in range(3):
            block[(2, 0, 1)[k], i] = 0.125 * halve_lanes(even_odd[2 * k], even_odd[2 * k + 1])
        return 0

    lax.fori_loop(0, planes // 2, coarse, 0)


def low_lane(shape, bit):
    return (iota(shape, 1) & bit) == 0


class Level:
    def __init__(self, level, refs):
        self.level, self.step, self.factor = level, 1 << (level - 1), 0.25**level
        (self.eps, self.pot, self.cap, self.f, self.xp, self.xm, self.yp, self.ym, self.zp, self.zm,
         self.w, self.d, self.wf, self.u, self.v) = refs
        self.nx, self.ny = self.eps.shape[0], self.eps.shape[1]

    @staticmethod
    def scratch(nx, ny):
        plain, face, padded = (pltpu.VMEM((n, ny, LANES), jnp.float32) for n in (nx, nx + 1, nx + 2))
        return [plain] * 4 + [face] * 2 + [plain] * 7 + [padded] * 2

    def assemble(self):
        nx, ny, step = self.nx, self.ny, self.step
        shape = (ny, LANES)
        row, spot = iota(shape, 0), iota(shape, 1) % (LANES // 2)
        last_row, top = row == ny - 1, spot >= LANES // 2 - step
        walls = (
            jnp.where(row == 0, 1.0, 0.0)
            + jnp.where(last_row, 1.0, 0.0)
            + jnp.where(spot < step, 1.0, 0.0)
            + jnp.where(top, 1.0, 0.0)
        )
        zero = jnp.zeros(shape, jnp.float32)
        half = 0.5 * self.factor
        for ref in (self.xp, self.xm):
            ref[0], ref[nx] = zero, zero
        for ref in (self.u, self.v):
            ref[0], ref[nx + 1] = zero, zero

        def x_face(i, _):
            k = half * (self.eps[i - 1] + self.eps[i])
            delta = self.pot[i] - self.pot[i - 1]
            kb = k * bernoulli(delta)
            self.xp[i], self.xm[i] = kb, kb + k * delta
            return 0

        lax.fori_loop(1, nx, x_face, 0)

        def plane(i, _):
            eps, pot = self.eps[i], self.pot[i]
            k = jnp.where(last_row, 0.0, half * (eps + up(eps, 1, 0)))
            delta = up(pot, 1, 0) - pot
            yp = k * bernoulli(delta)
            ym = yp + k * delta
            k = jnp.where(top, 0.0, half * (eps + up(eps, step, 1)))
            delta = up(pot, step, 1) - pot
            zp = k * bernoulli(delta)
            zm = zp + k * delta
            outer = walls + jnp.where(i == 0, 1.0, 0.0) + jnp.where(i == nx - 1, 1.0, 0.0)
            d = (self.xm[i + 1] + self.xp[i]) + (ym + down(yp, 1, 0)) + (zm + down(zp, step, 1))
            d = d + outer * (half * eps * bernoulli(pot)) + self.cap[i]
            w = OMEGA / d
            self.yp[i], self.ym[i], self.zp[i], self.zm[i] = yp, ym, zp, zm
            self.d[i], self.w[i] = d, w
            return 0

        lax.fori_loop(0, nx, plane, 0)

    def coupled(self, u, i):
        v = u[i + 1]
        s = self.xp[i + 1] * u[i + 2] + self.xm[i] * u[i]
        s = s + (self.yp[i] * up(v, 1, 0) + down(self.ym[i] * v, 1, 0))
        return s + (self.zp[i] * up(v, self.step, 1) + down(self.zm[i] * v, self.step, 1))

    def start(self):
        def body(i, _):
            wf = self.w[i] * self.f[i]
            self.wf[i] = wf
            self.u[i + 1] = wf
            return 0

        lax.fori_loop(0, self.nx, body, 0)

    def sweep(self, u, v):
        def body(i, _):
            v[i + 1] = (1.0 - OMEGA) * u[i + 1] + self.wf[i] + self.w[i] * self.coupled(u, i)
            return 0

        lax.fori_loop(0, self.nx, body, 0)

    def halve(self, tmp, v):
        step, ny = self.step, self.ny
        tmp[0:ny] = v
        v = tmp[pl.ds(0, ny // 2, stride=2), :] + tmp[pl.ds(1, ny // 2, stride=2), :]
        other = jnp.where(low_lane(v.shape, step), up(v, step, 1), down(v, step, 1))
        return 0.125 * (v + other)

    def descend_fields(self, coarser, tmp):
        def body(i, _):
            for here, there in ((self.eps, coarser.eps), (self.pot, coarser.pot), (self.cap, coarser.cap)):
                there[i] = self.halve(tmp, here[2 * i] + here[2 * i + 1])
            return 0

        lax.fori_loop(0, coarser.nx, body, 0)

    def descend_residual(self, u, coarser, tmp):
        def residual(i):
            return self.f[i] - self.d[i] * u[i + 1] + self.coupled(u, i)

        def body(i, _):
            coarser.f[i] = self.halve(tmp, residual(2 * i) + residual(2 * i + 1))
            return 0

        lax.fori_loop(0, coarser.nx, body, 0)

    def correct(self, u, coarser_u, tmp):
        half_ny = self.ny // 2

        def body(i, _):
            e = coarser_u(i)
            tmp[pl.ds(0, half_ny, stride=2), :] = e
            tmp[pl.ds(1, half_ny, stride=2), :] = e
            wide = tmp[0 : self.ny]
            u[2 * i + 1] = u[2 * i + 1] + wide
            u[2 * i + 2] = u[2 * i + 2] + wide
            return 0

        lax.fori_loop(0, self.nx // 2, body, 0)


def coarsest(lv):
    nx, step = lv.nx, lv.step
    cxp = [lv.w[i] * lv.xp[i + 1] for i in range(nx)]
    cxm = [lv.w[i] * lv.xm[i] for i in range(nx)]
    cyp = [lv.w[i] * lv.yp[i] for i in range(nx)]
    cym = [lv.w[i] * down(lv.ym[i], 1, 0) for i in range(nx)]
    czp = [lv.w[i] * lv.zp[i] for i in range(nx)]
    czm = [lv.w[i] * down(lv.zm[i], step, 1) for i in range(nx)]
    wf = [lv.w[i] * lv.f[i] for i in range(nx)]

    def body(_, u):
        new = []
        for i in range(nx):
            s = czp[i] * up(u[i], step, 1) + czm[i] * down(u[i], step, 1)
            t = cyp[i] * up(u[i], 1, 0) + cym[i] * down(u[i], 1, 0)
            r = (1.0 - OMEGA) * u[i] + wf[i]
            if i + 1 < nx:
                r = r + cxp[i] * u[i + 1]
            if i > 0:
                r = r + cxm[i] * u[i - 1]
            new.append(r + t + s)
        return tuple(new)

    u = lax.fori_loop(0, COARSE_ITERS - 1, body, tuple(wf))
    for i in range(nx):
        lv.u[i + 1] = u[i]


def second_kernel(bits, near, far, kept, out_p, out_n, *scratch):
    x, y = lax.axis_index("gx"), lax.axis_index("gy")
    ny = lax.axis_size("gy")
    l1, l2, l3 = (Level(k + 1, scratch[15 * k : 15 * k + 15]) for k in range(3))
    sol, tmp, fine_a, fine_b = scratch[45:]
    bx, by = near.shape[2], near.shape[3]
    half = near.shape[0]
    lane = iota((by, LANES), 1)
    right = lane >= LANES // 2

    def place(ref, flip):
        def body(m, _):
            b = m // ny
            to_x = x ^ flip
            for k, bit in enumerate(bits[:-1]):
                to_x = to_x ^ (((b >> k) & 1) * bit)
            to_y = y ^ (m % ny)
            row = pl.ds(pl.multiple_of(to_y * by, by), by)
            for i in range(bx):
                at = to_x * bx + i
                q = ref[m, 1, i]
                l1.eps[at, row, :] = ref[m, 0, i]
                l1.pot[at, row, :] = jnp.where(right, q, 0.0)
                l1.cap[at, row, :] = jnp.where(right, down(q, LANES // 2, 1), 0.0)
                l1.f[at, row, :] = ref[m, 2, i]
            return 0

        lax.fori_loop(0, half, body, 0)

    place(near, 0)
    place(far, bits[-1])
    l1.assemble()
    l1.descend_fields(l2, tmp)
    l2.assemble()
    l2.descend_fields(l3, tmp)
    l3.assemble()
    for here, there in ((l1, l2), (l2, l3)):
        here.start()
        here.sweep(here.u, here.v)
        here.descend_residual(here.v, there, tmp)
    coarsest(l3)
    l2.correct(l2.v, lambda i: l3.u[i + 1], tmp)
    l2.sweep(l2.v, l2.u)
    l2.sweep(l2.u, l2.v)
    l1.correct(l1.v, lambda i: l2.v[i + 1], tmp)
    l1.sweep(l1.v, l1.u)
    edge = jnp.zeros((by, LANES), jnp.float32)
    n1x, n1y = l1.nx, l1.ny
    blank = jnp.zeros((n1y + 2 * by, LANES), jnp.float32)
    sol[0], sol[n1x + 1] = blank, blank

    def last(i, _):
        sol[i + 1, 0:by] = edge
        sol[i + 1, by + n1y :] = edge
        sol[i + 1, by : by + n1y] = (
            (1.0 - OMEGA) * l1.u[i + 1] + l1.wf[i] + l1.w[i] * l1.coupled(l1.u, i)
        )
        return 0

    lax.fori_loop(0, n1x, last, 0)

    rows = kept.shape[2]
    own = rows - 2 * RIM
    tile_row = iota((by, LANES), 0)
    spread = iota((by, LANES), 1) // 2

    def widen(v, channel):
        return jnp.take_along_axis(v, spread + channel * (LANES // 2), axis=1)

    def correct(i, _):
        at = x * bx + i
        middle, above, below = (
            sol[at, pl.ds(pl.multiple_of((y + k) * by, by), by), :] for k in (1, 2, 0)
        )
        rim = jnp.where(
            tile_row < 2,
            jnp.broadcast_to(above[0:1], (by, LANES)),
            jnp.where(tile_row >= by - 2, jnp.broadcast_to(below[by - 1 : by], (by, LANES)), 0.0),
        )
        for channel, u in ((0, U_P), (1, U_N)):
            e = widen(middle, channel)
            tmp[pl.ds(0, by, stride=2), :] = e
            tmp[pl.ds(1, by, stride=2), :] = e
            tmp[own:rows] = widen(rim, channel)
            e = tmp[0:rows]
            for k in (0, 1):
                p = RIM - 2 + 2 * i + k
                fine_a[channel, p] = kept[u, p] + e
        return 0

    lax.fori_loop(0, bx + 2, correct, 0)

    def fine(u, channel, i):
        w, wf = ((W_P, WF_P), (W_N, WF_N))[channel]
        s = coupled_fine(kept, lambda j: u[channel, j], i, channel == 0)
        return (1.0 - OMEGA) * u[channel, i] + kept[wf, i] + kept[w, i] * s

    def post_one(i, _):
        for channel in (0, 1):
            fine_b[channel, i] = fine(fine_a, channel, i)
        return 0

    def post_two(i, _):
        out_p[i] = fine(fine_b, 0, i + RIM)[0:own]
        out_n[i] = fine(fine_b, 1, i + RIM)[0:own]
        return 0

    lax.fori_loop(RIM - 1, RIM + 2 * bx + 1, post_one, 0)
    lax.fori_loop(0, 2 * bx, post_two, 0)


def moves(nx, ny):
    def of(partner):
        return [(a * ny + b, (lambda t: t[0] * ny + t[1])(partner(a, b))) for a in range(nx) for b in range(ny)]

    def other(k, n):
        return k + 1 if k % 2 else k - 1

    return {
        "xa": of(lambda a, b: (a ^ 1, b)),
        "xb": of(lambda a, b: (other(a, nx), b) if 0 < a < nx - 1 else (a, b ^ 1)),
        "ya": of(lambda a, b: (a, b ^ 1)),
        "yb": of(lambda a, b: (a, other(b, ny)) if 0 < b < ny - 1 else (a ^ 1, b)),
        **{("x", k): of(lambda a, b, k=k: (a ^ k, b)) for k in range(1, nx)},
        **{("y", k): of(lambda a, b, k=k: (a, b ^ k)) for k in range(1, ny)},
    }


def per_device(nx, ny, layer_class, permittivity, mobility, capture, potential, rhs_psi, rhs_n):
    send = moves(nx, ny)
    f32 = jnp.float32

    def permute(v, name):
        return lax.ppermute(v, ("gx", "gy"), send[name])

    planes, own = layer_class.shape[0], layer_class.shape[1]
    rows, total = own + 2 * RIM, planes + 2 * RIM
    bx, by = planes // 2, own // 2
    raw = (layer_class, potential, rhs_psi, rhs_n)

    def shape(*dims):
        return jax.ShapeDtypeStruct(dims, f32)

    a, b = pl.pallas_call(
        rim_y_kernel,
        out_shape=[shape(2, planes, 2 * RIM, LANES)] * 2,
        in_specs=[VMEM] * 4,
        out_specs=[VMEM] * 2,
        compiler_params=params(16),
    )(*raw)
    b = permute(b, "yb")
    a = permute(a, "ya")
    mid, a, b = pl.pallas_call(
        rim_x_kernel,
        out_shape=[shape(4, planes, rows, LANES)] + [shape(4, RIM, rows, LANES)] * 2,
        in_specs=[VMEM] * 6,
        out_specs=[VMEM] * 3,
        compiler_params=params(16),
    )(*raw, a, b)
    b = permute(b, "xb")
    a = permute(a, "xa")
    kept, block = pl.pallas_call(
        first_kernel,
        out_shape=[shape(KEPT, total, rows, LANES), shape(3, bx, by, LANES)],
        in_specs=[SMEM] * 3 + [VMEM] * 3,
        out_specs=[VMEM] * 2,
        scratch_shapes=[
            pltpu.VMEM((8, total, rows, LANES), f32),
            pltpu.VMEM((6, own, LANES), f32),
            pltpu.VMEM((rows, LANES), f32),
        ],
        compiler_params=params(24),
    )(permittivity, mobility, capture, mid, a, b)

    near = jnp.stack([block] + [permute(block, ("y", k)) for k in range(1, ny)])
    bits = []
    bit = nx // 2
    while bit:
        bits.append(bit)
        far = permute(near, ("x", bit))
        if bit > 1:
            near = jnp.concatenate([near, far], axis=0)
        bit //= 2
    gx1, gy1 = bx * nx, by * ny
    scratch = []
    for level in range(3):
        scratch += Level.scratch(gx1 >> level, gy1 >> level)
    scratch += [
        pltpu.VMEM((gx1 + 2, gy1 + 2 * by, LANES), f32),
        pltpu.VMEM((max(gy1, rows), LANES), f32),
        pltpu.VMEM((2, total, rows, LANES), f32),
        pltpu.VMEM((2, total, rows, LANES), f32),
    ]
    return pl.pallas_call(
        functools.partial(second_kernel, tuple(bits)),
        out_shape=[shape(planes, own, LANES)] * 2,
        in_specs=[VMEM] * 3,
        out_specs=[VMEM] * 2,
        scratch_shapes=scratch,
        compiler_params=params(60 if gx1 * gy1 > 1024 else 32),
    )(near, far, kept)


def solution(mesh):
    grid = P(("groups", "gx"), "gy", None)
    fn = functools.partial(per_device, mesh.shape["gx"], mesh.shape["gy"])
    return jax.shard_map(
        fn,
        mesh=mesh,
        in_specs=(grid, P(), P(), P(), grid, grid, grid),
        out_specs=(grid, grid),
        check_vma=False,
    )
```

```python
import functools
import jax
import jax.numpy as jnp
from jax import lax
from jax.experimental import pallas as pl
from jax.experimental.pallas import tpu as pltpu
from jax.sharding import PartitionSpec as P

OMEGA = 0.8
COARSE_ITERS = 20
RIM = 4
LANES = 128
VMEM = pl.BlockSpec(memory_space=pltpu.VMEM)
SMEM = pl.BlockSpec(memory_space=pltpu.SMEM)


UNROLL = 16


def loop(first, end, body, init):
    if end - first > UNROLL:
        return lax.fori_loop(first, end, body, init)
    for i in range(first, end):
        body(i, 0)
    return init


def params(mib):
    return pltpu.CompilerParams(vmem_limit_bytes=mib * 1024 * 1024)


def bernoulli(x):
    t = x * x
    series = 1.0 - 0.5 * x + t * (1 / 12 + t * (-1 / 720 + t * (1 / 30240)))
    near = t < 0.25
    guarded = jnp.where(near, 1.0, x)
    return jnp.where(near, series, guarded / (jnp.exp(guarded) - 1.0))


def iota(shape, dim):
    return lax.broadcasted_iota(jnp.int32, shape, dim)


def up(v, step, dim):
    return pltpu.roll(v, v.shape[dim] - step, dim)


def down(v, step, dim):
    return pltpu.roll(v, step, dim)


def rim_y_kernel(cls, pot, fp, fn, out_a, out_b):
    even = lax.axis_index("gy") % 2 == 0
    length = cls.shape[1]
    for pair, (first, second) in enumerate(((cls, pot), (fp, fn))):
        lo, hi = (
            jnp.concatenate(
                [r[:, at : at + RIM, :].astype(jnp.float32) for r in (first, second)], axis=1
            )
            for at in (0, length - RIM)
        )
        out_a[pair] = jnp.where(even, hi, lo)
        out_b[pair] = jnp.where(even, lo, hi)


def rim_x_kernel(cls, pot, fp, fn, in_a, in_b, out, out_a, out_b):
    y, ny = lax.axis_index("gy"), lax.axis_size("gy")
    even_x, even_y = lax.axis_index("gx") % 2 == 0, y % 2 == 0
    planes, length = cls.shape[0], cls.shape[1]
    row = iota((planes, 2 * RIM, LANES), 1)
    for pair, refs in enumerate(((cls, pot), (fp, fn))):
        a, b = in_a[pair], in_b[pair]
        hi, lo = jnp.where(even_y, a, b), jnp.where(even_y, b, a)
        for slot, ref in enumerate(refs):
            field = 2 * pair + slot
            outside = -1.0 if field == 0 else 0.0
            h, l = jnp.where(y == ny - 1, outside, hi), jnp.where(y == 0, outside, lo)
            if slot == 0:
                l = down(l, RIM, 1)
            else:
                h = down(h, RIM, 1)
            out[field, :, 0:length, :] = ref[...].astype(jnp.float32)
            out[field, :, length : length + 2 * RIM, :] = jnp.where(row < RIM, h, l)
        for slot in range(2):
            field = 2 * pair + slot
            lo_x, hi_x = out[field, 0:RIM], out[field, planes - RIM : planes]
            out_a[field] = jnp.where(even_x, hi_x, lo_x)
            out_b[field] = jnp.where(even_x, lo_x, hi_x)


W_P, GX, GY, GZ, W_N, XP, XM, YP, YM, ZP, ZM, WF_P, WF_N, U_P, U_N = range(15)
KEPT = 15


def coupled_fine(kept, u, i, poisson):
    v = u(i)
    if poisson:
        xp, xm, yp, ym, zp, zm = GX, GX, GY, GY, GZ, GZ
    else:
        xp, xm, yp, ym, zp, zm = XP, XM, YP, YM, ZP, ZM
    s = kept[xp, i] * u(i + 1) + kept[xm, i - 1] * u(i - 1)
    s = s + (kept[yp, i] * up(v, 1, 0) + down(kept[ym, i] * v, 1, 0))
    return s + (kept[zp, i] * up(v, 1, 1) + down(kept[zm, i] * v, 1, 1))


def halve_lanes(a, b):
    lane = iota(a.shape, 1)
    at = (2 * lane) % LANES
    a = jnp.take_along_axis(a + up(a, 1, 1), at, axis=1)
    b = jnp.take_along_axis(b + up(b, 1, 1), at, axis=1)
    return jnp.where(lane < LANES // 2, a, b)


def first_kernel(eps_t, mob_t, cap_t, mid, in_a, in_b, kept, block, fld, work):
    x, nx = lax.axis_index("gx"), lax.axis_size("gx")
    even = x % 2 == 0
    planes = mid.shape[1]
    rows = mid.shape[2]
    own = rows - 2 * RIM
    total = planes + 2 * RIM
    EPS, MOB, POT, CAP, F_P, F_N, D_P, D_N = range(8)
    classes = eps_t.shape[0]

    def materials(i, c, pot, fp, fn):
        eps, mob, cap = jnp.zeros_like(c), jnp.zeros_like(c), jnp.zeros_like(c)
        for k in range(classes):
            same = c == float(k)
            eps = jnp.where(same, eps_t[k], eps)
            mob = jnp.where(same, mob_t[k], mob)
            cap = jnp.where(same, cap_t[k], cap)
        fld[EPS, i], fld[MOB, i], fld[POT, i], fld[CAP, i] = eps, mob, pot, cap
        fld[F_P, i], fld[F_N, i] = fp, fn

    def low(i, _):
        v = [jnp.where(even, in_b[f, i], in_a[f, i]) for f in range(4)]
        materials(i, *[jnp.where(x == 0, -1.0 if f == 0 else 0.0, v[f]) for f in range(4)])
        return 0

    def middle(i, _):
        materials(i + RIM, *[mid[f, i] for f in range(4)])
        return 0

    def high(i, _):
        v = [jnp.where(even, in_a[f, i], in_b[f, i]) for f in range(4)]
        materials(
            i + RIM + planes,
            *[jnp.where(x == nx - 1, -1.0 if f == 0 else 0.0, v[f]) for f in range(4)],
        )
        return 0

    loop(0, RIM, low, 0)
    loop(0, planes, middle, 0)
    loop(0, RIM, high, 0)

    shape = (rows, LANES)
    lane = iota(shape, 1)
    ends = (lane == 0) | (lane == LANES - 1)
    top = lane == LANES - 1

    def x_faces(i):
        eps, mob, pot = fld[EPS, i], fld[MOB, i], fld[POT, i]
        kept[GX, i] = 0.5 * (eps + fld[EPS, i + 1])
        k = 0.5 * (mob + fld[MOB, i + 1])
        delta = fld[POT, i + 1] - pot
        kb = k * bernoulli(delta)
        kept[XP, i] = kb
        kept[XM, i] = kb + k * delta

    x_faces(0)

    def operators(i, _):
        x_faces(i)
        eps, mob, pot = fld[EPS, i], fld[MOB, i], fld[POT, i]
        gy = 0.5 * (eps + up(eps, 1, 0))
        k = 0.5 * (mob + up(mob, 1, 0))
        delta = up(pot, 1, 0) - pot
        yp = k * bernoulli(delta)
        ym = yp + k * delta
        gz = jnp.where(top, 0.0, 0.5 * (eps + up(eps, 1, 1)))
        k = jnp.where(top, 0.0, 0.5 * (mob + up(mob, 1, 1)))
        delta = up(pot, 1, 1) - pot
        zp = k * bernoulli(delta)
        zm = zp + k * delta
        kept[GY, i], kept[YP, i], kept[YM, i] = gy, yp, ym
        kept[GZ, i], kept[ZP, i], kept[ZM, i] = gz, zp, zm
        d_p = (kept[GX, i] + kept[GX, i - 1]) + (gy + down(gy, 1, 0)) + (gz + down(gz, 1, 1))
        d_p = d_p + jnp.where(ends, 0.5 * eps, 0.0)
        d_n = (kept[XM, i] + kept[XP, i - 1]) + (ym + down(yp, 1, 0)) + (zm + down(zp, 1, 1))
        d_n = d_n + jnp.where(ends, 0.5 * mob * bernoulli(pot), 0.0) + fld[CAP, i]
        inside = eps > 0.0
        w_p = jnp.where(inside, OMEGA / jnp.where(inside, d_p, 1.0), 0.0)
        w_n = jnp.where(inside, OMEGA / jnp.where(inside, d_n, 1.0), 0.0)
        kept[W_P, i], kept[W_N, i] = w_p, w_n
        kept[WF_P, i], kept[WF_N, i] = w_p * fld[F_P, i], w_n * fld[F_N, i]
        fld[D_P, i], fld[D_N, i] = d_p, d_n
        return 0

    loop(1, total - 1, operators, 0)

    def sweep(i, _):
        for poisson, w, wf, u in ((True, W_P, WF_P, U_P), (False, W_N, WF_N, U_N)):
            s = coupled_fine(kept, lambda j: kept[wf, j], i, poisson)
            kept[u, i] = (2.0 - OMEGA) * kept[wf, i] + kept[w, i] * s
        return 0

    loop(2, total - 2, sweep, 0)

    def residual(i, poisson, f, d, u):
        s = coupled_fine(kept, lambda j: kept[u, j], i, poisson)
        return fld[f, i] - fld[d, i] * kept[u, i] + s

    def coarse(i, _):
        at = RIM + 2 * i
        r_p = residual(at, True, F_P, D_P, U_P) + residual(at + 1, True, F_P, D_P, U_P)
        r_n = residual(at, False, F_N, D_N, U_N) + residual(at + 1, False, F_N, D_N, U_N)
        values = [r_p, r_n] + [fld[f, at] + fld[f, at + 1] for f in (EPS, MOB, CAP, POT)]
        for k, v in enumerate(values):
            work[k] = v[0:own]
        even_odd = [
            work[k, pl.ds(0, own // 2, stride=2), :] + work[k, pl.ds(1, own // 2, stride=2), :]
            for k in range(6)
        ]
        for k in range(3):
            block[(2, 0, 1)[k], i] = 0.125 * halve_lanes(even_odd[2 * k], even_odd[2 * k + 1])
        return 0

    loop(0, planes // 2, coarse, 0)


def low_lane(shape, bit):
    return (iota(shape, 1) & bit) == 0


class Level:
    def __init__(self, level, refs):
        self.level, self.step, self.factor = level, 1 << (level - 1), 0.25**level
        (self.eps, self.pot, self.cap, self.f, self.xp, self.xm, self.yp, self.ym, self.zp, self.zm,
         self.w, self.d, self.wf, self.u, self.v) = refs
        self.nx, self.ny = self.eps.shape[0], self.eps.shape[1]

    @staticmethod
    def scratch(nx, ny):
        plain, face, padded = (pltpu.VMEM((n, ny, LANES), jnp.float32) for n in (nx, nx + 1, nx + 2))
        return [plain] * 4 + [face] * 2 + [plain] * 7 + [padded] * 2

    def assemble(self):
        nx, ny, step = self.nx, self.ny, self.step
        shape = (ny, LANES)
        row, spot = iota(shape, 0), iota(shape, 1) % (LANES // 2)
        last_row, top = row == ny - 1, spot >= LANES // 2 - step
        walls = (
            jnp.where(row == 0, 1.0, 0.0)
            + jnp.where(last_row, 1.0, 0.0)
            + jnp.where(spot < step, 1.0, 0.0)
            + jnp.where(top, 1.0, 0.0)
        )
        zero = jnp.zeros(shape, jnp.float32)
        half = 0.5 * self.factor
        for ref in (self.xp, self.xm):
            ref[0], ref[nx] = zero, zero
        for ref in (self.u, self.v):
            ref[0], ref[nx + 1] = zero, zero

        def x_face(i, _):
            k = half * (self.eps[i - 1] + self.eps[i])
            delta = self.pot[i] - self.pot[i - 1]
            kb = k * bernoulli(delta)
            self.xp[i], self.xm[i] = kb, kb + k * delta
            return 0

        loop(1, nx, x_face, 0)

        def plane(i, _):
            eps, pot = self.eps[i], self.pot[i]
            k = jnp.where(last_row, 0.0, half * (eps + up(eps, 1, 0)))
            delta = up(pot, 1, 0) - pot
            yp = k * bernoulli(delta)
            ym = yp + k * delta
            k = jnp.where(top, 0.0, half * (eps + up(eps, step, 1)))
            delta = up(pot, step, 1) - pot
            zp = k * bernoulli(delta)
            zm = zp + k * delta
            outer = walls + jnp.where(i == 0, 1.0, 0.0) + jnp.where(i == nx - 1, 1.0, 0.0)
            d = (self.xm[i + 1] + self.xp[i]) + (ym + down(yp, 1, 0)) + (zm + down(zp, step, 1))
            d = d + outer * (half * eps * bernoulli(pot)) + self.cap[i]
            w = OMEGA / d
            self.yp[i], self.ym[i], self.zp[i], self.zm[i] = yp, ym, zp, zm
            self.d[i], self.w[i] = d, w
            return 0

        loop(0, nx, plane, 0)

    def coupled(self, u, i):
        v = u[i + 1]
        s = self.xp[i + 1] * u[i + 2] + self.xm[i] * u[i]
        s = s + (self.yp[i] * up(v, 1, 0) + down(self.ym[i] * v, 1, 0))
        return s + (self.zp[i] * up(v, self.step, 1) + down(self.zm[i] * v, self.step, 1))

    def start(self):
        def body(i, _):
            wf = self.w[i] * self.f[i]
            self.wf[i] = wf
            self.u[i + 1] = wf
            return 0

        loop(0, self.nx, body, 0)

    def sweep(self, u, v):
        def body(i, _):
            v[i + 1] = (1.0 - OMEGA) * u[i + 1] + self.wf[i] + self.w[i] * self.coupled(u, i)
            return 0

        loop(0, self.nx, body, 0)

    def halve(self, tmp, v):
        step, ny = self.step, self.ny
        tmp[0:ny] = v
        v = tmp[pl.ds(0, ny // 2, stride=2), :] + tmp[pl.ds(1, ny // 2, stride=2), :]
        other = jnp.where(low_lane(v.shape, step), up(v, step, 1), down(v, step, 1))
        return 0.125 * (v + other)

    def descend_fields(self, coarser, tmp):
        def body(i, _):
            for here, there in ((self.eps, coarser.eps), (self.pot, coarser.pot), (self.cap, coarser.cap)):
                there[i] = self.halve(tmp, here[2 * i] + here[2 * i + 1])
            return 0

        loop(0, coarser.nx, body, 0)

    def descend_residual(self, u, coarser, tmp):
        def residual(i):
            return self.f[i] - self.d[i] * u[i + 1] + self.coupled(u, i)

        def body(i, _):
            coarser.f[i] = self.halve(tmp, residual(2 * i) + residual(2 * i + 1))
            return 0

        loop(0, coarser.nx, body, 0)

    def correct(self, u, coarser_u, tmp):
        half_ny = self.ny // 2

        def body(i, _):
            e = coarser_u(i)
            tmp[pl.ds(0, half_ny, stride=2), :] = e
            tmp[pl.ds(1, half_ny, stride=2), :] = e
            wide = tmp[0 : self.ny]
            u[2 * i + 1] = u[2 * i + 1] + wide
            u[2 * i + 2] = u[2 * i + 2] + wide
            return 0

        loop(0, self.nx // 2, body, 0)


def coarsest(lv):
    nx, step = lv.nx, lv.step
    cxp = [lv.w[i] * lv.xp[i + 1] for i in range(nx)]
    cxm = [lv.w[i] * lv.xm[i] for i in range(nx)]
    cyp = [lv.w[i] * lv.yp[i] for i in range(nx)]
    cym = [lv.w[i] * down(lv.ym[i], 1, 0) for i in range(nx)]
    czp = [lv.w[i] * lv.zp[i] for i in range(nx)]
    czm = [lv.w[i] * down(lv.zm[i], step, 1) for i in range(nx)]
    wf = [lv.w[i] * lv.f[i] for i in range(nx)]

    def body(_, u):
        new = []
        for i in range(nx):
            s = czp[i] * up(u[i], step, 1) + czm[i] * down(u[i], step, 1)
            t = cyp[i] * up(u[i], 1, 0) + cym[i] * down(u[i], 1, 0)
            r = (1.0 - OMEGA) * u[i] + wf[i]
            if i + 1 < nx:
                r = r + cxp[i] * u[i + 1]
            if i > 0:
                r = r + cxm[i] * u[i - 1]
            new.append(r + t + s)
        return tuple(new)

    u = lax.fori_loop(0, COARSE_ITERS - 1, body, tuple(wf))
    for i in range(nx):
        lv.u[i + 1] = u[i]


def second_kernel(bits, near, far, kept, out_p, out_n, *scratch):
    x, y = lax.axis_index("gx"), lax.axis_index("gy")
    ny = lax.axis_size("gy")
    l1, l2, l3 = (Level(k + 1, scratch[15 * k : 15 * k + 15]) for k in range(3))
    sol, tmp, fine_a, fine_b = scratch[45:]
    bx, by = near.shape[2], near.shape[3]
    half = near.shape[0]
    lane = iota((by, LANES), 1)
    right = lane >= LANES // 2

    def place(ref, flip):
        def body(m, _):
            b = m // ny
            to_x = x ^ flip
            for k, bit in enumerate(bits[:-1]):
                to_x = to_x ^ (((b >> k) & 1) * bit)
            to_y = y ^ (m % ny)
            row = pl.ds(pl.multiple_of(to_y * by, by), by)
            for i in range(bx):
                at = to_x * bx + i
                q = ref[m, 1, i]
                l1.eps[at, row, :] = ref[m, 0, i]
                l1.pot[at, row, :] = jnp.where(right, q, 0.0)
                l1.cap[at, row, :] = jnp.where(right, down(q, LANES // 2, 1), 0.0)
                l1.f[at, row, :] = ref[m, 2, i]
            return 0

        loop(0, half, body, 0)

    place(near, 0)
    place(far, bits[-1])
    l1.assemble()
    l1.descend_fields(l2, tmp)
    l2.assemble()
    l2.descend_fields(l3, tmp)
    l3.assemble()
    for here, there in ((l1, l2), (l2, l3)):
        here.start()
        here.sweep(here.u, here.v)
        here.descend_residual(here.v, there, tmp)
    coarsest(l3)
    l2.correct(l2.v, lambda i: l3.u[i + 1], tmp)
    l2.sweep(l2.v, l2.u)
    l2.sweep(l2.u, l2.v)
    l1.correct(l1.v, lambda i: l2.v[i + 1], tmp)
    l1.sweep(l1.v, l1.u)
    edge = jnp.zeros((by, LANES), jnp.float32)
    n1x, n1y = l1.nx, l1.ny
    blank = jnp.zeros((n1y + 2 * by, LANES), jnp.float32)
    sol[0], sol[n1x + 1] = blank, blank

    def last(i, _):
        sol[i + 1, 0:by] = edge
        sol[i + 1, by + n1y :] = edge
        sol[i + 1, by : by + n1y] = (
            (1.0 - OMEGA) * l1.u[i + 1] + l1.wf[i] + l1.w[i] * l1.coupled(l1.u, i)
        )
        return 0

    loop(0, n1x, last, 0)

    rows = kept.shape[2]
    own = rows - 2 * RIM
    tile_row = iota((by, LANES), 0)
    spread = iota((by, LANES), 1) // 2

    def widen(v, channel):
        return jnp.take_along_axis(v, spread + channel * (LANES // 2), axis=1)

    def correct(i, _):
        at = x * bx + i
        middle, above, below = (
            sol[at, pl.ds(pl.multiple_of((y + k) * by, by), by), :] for k in (1, 2, 0)
        )
        rim = jnp.where(
            tile_row < 2,
            jnp.broadcast_to(above[0:1], (by, LANES)),
            jnp.where(tile_row >= by - 2, jnp.broadcast_to(below[by - 1 : by], (by, LANES)), 0.0),
        )
        for channel, u in ((0, U_P), (1, U_N)):
            e = widen(middle, channel)
            tmp[pl.ds(0, by, stride=2), :] = e
            tmp[pl.ds(1, by, stride=2), :] = e
            tmp[own:rows] = widen(rim, channel)
            e = tmp[0:rows]
            for k in (0, 1):
                p = RIM - 2 + 2 * i + k
                fine_a[channel, p] = kept[u, p] + e
        return 0

    loop(0, bx + 2, correct, 0)

    def fine(u, channel, i):
        w, wf = ((W_P, WF_P), (W_N, WF_N))[channel]
        s = coupled_fine(kept, lambda j: u[channel, j], i, channel == 0)
        return (1.0 - OMEGA) * u[channel, i] + kept[wf, i] + kept[w, i] * s

    def post_one(i, _):
        for channel in (0, 1):
            fine_b[channel, i] = fine(fine_a, channel, i)
        return 0

    def post_two(i, _):
        out_p[i] = fine(fine_b, 0, i + RIM)[0:own]
        out_n[i] = fine(fine_b, 1, i + RIM)[0:own]
        return 0

    loop(RIM - 1, RIM + 2 * bx + 1, post_one, 0)
    loop(0, 2 * bx, post_two, 0)


def moves(nx, ny):
    def of(partner):
        return [(a * ny + b, (lambda t: t[0] * ny + t[1])(partner(a, b))) for a in range(nx) for b in range(ny)]

    def other(k, n):
        return k + 1 if k % 2 else k - 1

    return {
        "xa": of(lambda a, b: (a ^ 1, b)),
        "xb": of(lambda a, b: (other(a, nx), b) if 0 < a < nx - 1 else (a, b ^ 1)),
        "ya": of(lambda a, b: (a, b ^ 1)),
        "yb": of(lambda a, b: (a, other(b, ny)) if 0 < b < ny - 1 else (a ^ 1, b)),
        **{("x", k): of(lambda a, b, k=k: (a ^ k, b)) for k in range(1, nx)},
        **{("y", k): of(lambda a, b, k=k: (a, b ^ k)) for k in range(1, ny)},
    }


def per_device(nx, ny, layer_class, permittivity, mobility, capture, potential, rhs_psi, rhs_n):
    send = moves(nx, ny)
    f32 = jnp.float32

    def permute(v, name):
        return lax.ppermute(v, ("gx", "gy"), send[name])

    planes, own = layer_class.shape[0], layer_class.shape[1]
    rows, total = own + 2 * RIM, planes + 2 * RIM
    bx, by = planes // 2, own // 2
    raw = (layer_class, potential, rhs_psi, rhs_n)

    def shape(*dims):
        return jax.ShapeDtypeStruct(dims, f32)

    a, b = pl.pallas_call(
        rim_y_kernel,
        out_shape=[shape(2, planes, 2 * RIM, LANES)] * 2,
        in_specs=[VMEM] * 4,
        out_specs=[VMEM] * 2,
        compiler_params=params(16),
    )(*raw)
    b = permute(b, "yb")
    a = permute(a, "ya")
    mid, a, b = pl.pallas_call(
        rim_x_kernel,
        out_shape=[shape(4, planes, rows, LANES)] + [shape(4, RIM, rows, LANES)] * 2,
        in_specs=[VMEM] * 6,
        out_specs=[VMEM] * 3,
        compiler_params=params(16),
    )(*raw, a, b)
    b = permute(b, "xb")
    a = permute(a, "xa")
    kept, block = pl.pallas_call(
        first_kernel,
        out_shape=[shape(KEPT, total, rows, LANES), shape(3, bx, by, LANES)],
        in_specs=[SMEM] * 3 + [VMEM] * 3,
        out_specs=[VMEM] * 2,
        scratch_shapes=[
            pltpu.VMEM((8, total, rows, LANES), f32),
            pltpu.VMEM((6, own, LANES), f32),
        ],
        compiler_params=params(24),
    )(permittivity, mobility, capture, mid, a, b)

    near = jnp.stack([block] + [permute(block, ("y", k)) for k in range(1, ny)])
    bits = []
    bit = nx // 2
    while bit:
        bits.append(bit)
        far = permute(near, ("x", bit))
        if bit > 1:
            near = jnp.concatenate([near, far], axis=0)
        bit //= 2
    gx1, gy1 = bx * nx, by * ny
    scratch = []
    for level in range(3):
        scratch += Level.scratch(gx1 >> level, gy1 >> level)
    scratch += [
        pltpu.VMEM((gx1 + 2, gy1 + 2 * by, LANES), f32),
        pltpu.VMEM((max(gy1, rows), LANES), f32),
        pltpu.VMEM((2, total, rows, LANES), f32),
        pltpu.VMEM((2, total, rows, LANES), f32),
    ]
    return pl.pallas_call(
        functools.partial(second_kernel, tuple(bits)),
        out_shape=[shape(planes, own, LANES)] * 2,
        in_specs=[VMEM] * 3,
        out_specs=[VMEM] * 2,
        scratch_shapes=scratch,
        compiler_params=params(60 if gx1 * gy1 > 1024 else 32),
    )(near, far, kept)


def solution(mesh):
    grid = P(("groups", "gx"), "gy", None)
    fn = functools.partial(per_device, mesh.shape["gx"], mesh.shape["gy"])
    return jax.shard_map(
        fn,
        mesh=mesh,
        in_specs=(grid, P(), P(), P(), grid, grid, grid),
        out_specs=(grid, grid),
        check_vma=False,
    )
```

```python
import functools
import itertools
import jax
import jax.numpy as jnp
from jax import lax
from jax.experimental import pallas as pl
from jax.experimental.pallas import tpu as pltpu
from jax.sharding import PartitionSpec as P

OMEGA = 0.8
COARSE_ITERS = 20
RIM = 4
LANES = 128
VMEM = pl.BlockSpec(memory_space=pltpu.VMEM)


UNROLL = 16


def loop(first, end, body, init):
    if end - first > UNROLL:
        return lax.fori_loop(first, end, body, init)
    for i in range(first, end):
        body(i, 0)
    return init


def params(mib):
    return pltpu.CompilerParams(vmem_limit_bytes=mib * 1024 * 1024)


def bernoulli(x):
    t = x * x
    series = 1.0 - 0.5 * x + t * (1 / 12 + t * (-1 / 720 + t * (1 / 30240)))
    near = t < 0.25
    guarded = jnp.where(near, 1.0, x)
    return jnp.where(near, series, guarded / (jnp.exp(guarded) - 1.0))


def iota(shape, dim):
    return lax.broadcasted_iota(jnp.int32, shape, dim)


def up(v, step, dim):
    return pltpu.roll(v, v.shape[dim] - step, dim)


def down(v, step, dim):
    return pltpu.roll(v, step, dim)


def halve_lanes(a, b):
    lane = iota(a.shape, 1)
    at = (2 * lane) % LANES
    a = jnp.take_along_axis(a + up(a, 1, 1), at, axis=1)
    b = jnp.take_along_axis(b + up(b, 1, 1), at, axis=1)
    return jnp.where(lane < LANES // 2, a, b)


def look_up(table, c, shape):
    found = [jnp.zeros(shape, jnp.float32)] * 3
    for k in range(table.shape[1]):
        same = c == float(k)
        found = [
            jnp.where(same, jnp.broadcast_to(table[f, k : k + 1], shape), found[f]) for f in range(3)
        ]
    return found


def rim_y_kernel(cls, raw, out_a, out_b):
    even = lax.axis_index("gy") % 2 == 0
    planes, length = cls.shape[0], cls.shape[1]
    for pair in range(2):
        first = cls if pair == 0 else raw.at[1]
        lo, hi = (
            jnp.concatenate(
                [r[:, at : at + RIM, :].astype(jnp.float32) for r in (first, raw.at[2 * pair])], axis=1
            )
            for at in (0, length - RIM)
        )
        out_a[pair * planes : (pair + 1) * planes] = jnp.where(even, hi, lo)
        out_b[pair * planes : (pair + 1) * planes] = jnp.where(even, lo, hi)


def fields_kernel(table, cls, raw, block, work):
    planes, length = cls.shape[0], cls.shape[1]
    bx = planes // 2
    for i in range(bx):
        one, two = (
            look_up(table, cls[2 * i + k].astype(jnp.float32), (length, LANES)) for k in (0, 1)
        )
        values = [p + q for p, q in zip(one, two)] + [raw[0, 2 * i] + raw[0, 2 * i + 1]]
        for k, v in enumerate(values):
            work[k, i] = v
    for i in range(bx):
        eps, mob, cap, pot = (
            work[k, i, pl.ds(0, length // 2, stride=2), :] + work[k, i, pl.ds(1, length // 2, stride=2), :]
            for k in range(4)
        )
        for f, v in enumerate((halve_lanes(eps, mob), halve_lanes(cap, pot))):
            block[0, f, i] = 0.125 * v


def rim_x_kernel(cls, raw, in_a, in_b, out, out_a, out_b):
    y, ny = lax.axis_index("gy"), lax.axis_size("gy")
    even_x, even_y = lax.axis_index("gx") % 2 == 0, y % 2 == 0
    planes, length = cls.shape[0], cls.shape[1]
    row = iota((planes, 2 * RIM, LANES), 1)
    for pair in range(2):
        a, b = (r[pair * planes : (pair + 1) * planes] for r in (in_a, in_b))
        hi, lo = jnp.where(even_y, a, b), jnp.where(even_y, b, a)
        for slot in range(2):
            field = 2 * pair + slot
            outside = -1.0 if field == 0 else 0.0
            h, l = jnp.where(y == ny - 1, outside, hi), jnp.where(y == 0, outside, lo)
            if slot == 0:
                l = down(l, RIM, 1)
            else:
                h = down(h, RIM, 1)
            own = cls[...].astype(jnp.float32) if field == 0 else raw[field - 1]
            out[field, :, 0:length, :] = own
            out[field, :, length : length + 2 * RIM, :] = jnp.where(row < RIM, h, l)
        for slot in range(2):
            field = 2 * pair + slot
            lo_x, hi_x = out[field, 0:RIM], out[field, planes - RIM : planes]
            out_a[field] = jnp.where(even_x, hi_x, lo_x)
            out_b[field] = jnp.where(even_x, lo_x, hi_x)


W_P, GX, GY, GZ, W_N, XP, XM, YP, YM, ZP, ZM, WF_P, WF_N, U_P, U_N = range(15)
KEPT = 15


def coupled_fine(kept, u, i, poisson):
    v = u(i)
    if poisson:
        xp, xm, yp, ym, zp, zm = GX, GX, GY, GY, GZ, GZ
    else:
        xp, xm, yp, ym, zp, zm = XP, XM, YP, YM, ZP, ZM
    s = kept[xp, i] * u(i + 1) + kept[xm, i - 1] * u(i - 1)
    s = s + (kept[yp, i] * up(v, 1, 0) + down(kept[ym, i] * v, 1, 0))
    return s + (kept[zp, i] * up(v, 1, 1) + down(kept[zm, i] * v, 1, 1))


def first_kernel(table, mid, in_a, in_b, kept, block, fld, work):
    x, nx = lax.axis_index("gx"), lax.axis_size("gx")
    even = x % 2 == 0
    planes = mid.shape[1]
    rows = mid.shape[2]
    own = rows - 2 * RIM
    total = planes + 2 * RIM
    EPS, MOB, POT, CAP, F_P, F_N, D_P, D_N = range(8)

    def materials(i, c, pot, fp, fn):
        eps, mob, cap = look_up(table, c, (rows, LANES))
        fld[EPS, i], fld[MOB, i], fld[POT, i], fld[CAP, i] = eps, mob, pot, cap
        fld[F_P, i], fld[F_N, i] = fp, fn

    def low(i, _):
        v = [jnp.where(even, in_b[f, i], in_a[f, i]) for f in range(4)]
        materials(i, *[jnp.where(x == 0, -1.0 if f == 0 else 0.0, v[f]) for f in range(4)])
        return 0

    def middle(i, _):
        materials(i + RIM, *[mid[f, i] for f in range(4)])
        return 0

    def high(i, _):
        v = [jnp.where(even, in_a[f, i], in_b[f, i]) for f in range(4)]
        materials(
            i + RIM + planes,
            *[jnp.where(x == nx - 1, -1.0 if f == 0 else 0.0, v[f]) for f in range(4)],
        )
        return 0

    loop(0, RIM, low, 0)
    loop(0, planes, middle, 0)
    loop(0, RIM, high, 0)

    shape = (rows, LANES)
    lane = iota(shape, 1)
    ends = (lane == 0) | (lane == LANES - 1)
    top = lane == LANES - 1

    def x_faces(i):
        eps, mob, pot = fld[EPS, i], fld[MOB, i], fld[POT, i]
        kept[GX, i] = 0.5 * (eps + fld[EPS, i + 1])
        k = 0.5 * (mob + fld[MOB, i + 1])
        delta = fld[POT, i + 1] - pot
        kb = k * bernoulli(delta)
        kept[XP, i] = kb
        kept[XM, i] = kb + k * delta

    x_faces(0)

    def operators(i, _):
        x_faces(i)
        eps, mob, pot = fld[EPS, i], fld[MOB, i], fld[POT, i]
        gy = 0.5 * (eps + up(eps, 1, 0))
        k = 0.5 * (mob + up(mob, 1, 0))
        delta = up(pot, 1, 0) - pot
        yp = k * bernoulli(delta)
        ym = yp + k * delta
        gz = jnp.where(top, 0.0, 0.5 * (eps + up(eps, 1, 1)))
        k = jnp.where(top, 0.0, 0.5 * (mob + up(mob, 1, 1)))
        delta = up(pot, 1, 1) - pot
        zp = k * bernoulli(delta)
        zm = zp + k * delta
        kept[GY, i], kept[YP, i], kept[YM, i] = gy, yp, ym
        kept[GZ, i], kept[ZP, i], kept[ZM, i] = gz, zp, zm
        d_p = (kept[GX, i] + kept[GX, i - 1]) + (gy + down(gy, 1, 0)) + (gz + down(gz, 1, 1))
        d_p = d_p + jnp.where(ends, 0.5 * eps, 0.0)
        d_n = (kept[XM, i] + kept[XP, i - 1]) + (ym + down(yp, 1, 0)) + (zm + down(zp, 1, 1))
        d_n = d_n + jnp.where(ends, 0.5 * mob * bernoulli(pot), 0.0) + fld[CAP, i]
        inside = eps > 0.0
        w_p = jnp.where(inside, OMEGA / jnp.where(inside, d_p, 1.0), 0.0)
        w_n = jnp.where(inside, OMEGA / jnp.where(inside, d_n, 1.0), 0.0)
        kept[W_P, i], kept[W_N, i] = w_p, w_n
        kept[WF_P, i], kept[WF_N, i] = w_p * fld[F_P, i], w_n * fld[F_N, i]
        fld[D_P, i], fld[D_N, i] = d_p, d_n
        return 0

    loop(1, total - 1, operators, 0)

    def sweep(i, _):
        for poisson, w, wf, u in ((True, W_P, WF_P, U_P), (False, W_N, WF_N, U_N)):
            s = coupled_fine(kept, lambda j: kept[wf, j], i, poisson)
            kept[u, i] = (2.0 - OMEGA) * kept[wf, i] + kept[w, i] * s
        return 0

    loop(2, total - 2, sweep, 0)

    def residual(i, poisson, f, d, u):
        s = coupled_fine(kept, lambda j: kept[u, j], i, poisson)
        return fld[f, i] - fld[d, i] * kept[u, i] + s

    def coarse(i, _):
        at = RIM + 2 * i
        r_p = residual(at, True, F_P, D_P, U_P) + residual(at + 1, True, F_P, D_P, U_P)
        r_n = residual(at, False, F_N, D_N, U_N) + residual(at + 1, False, F_N, D_N, U_N)
        work[0, i], work[1, i] = r_p[0:own], r_n[0:own]
        r_p, r_n = (
            work[k, i, pl.ds(0, own // 2, stride=2), :] + work[k, i, pl.ds(1, own // 2, stride=2), :]
            for k in range(2)
        )
        block[0, i] = 0.125 * halve_lanes(r_p, r_n)
        return 0

    loop(0, planes // 2, coarse, 0)


def low_lane(shape, bit):
    return (iota(shape, 1) & bit) == 0


OPERATOR = 8


class Level:
    def __init__(self, level, refs):
        self.level, self.step, self.factor = level, 1 << (level - 1), 0.25**level
        (self.xp, self.xm, self.yp, self.ym, self.zp, self.zm, self.w, self.d) = refs[:OPERATOR]
        if len(refs) == OPERATOR + 3:
            self.eps, self.pot, self.cap = refs[OPERATOR:]
        else:
            self.f, self.wf, self.u, self.v = refs[OPERATOR:]
        self.nx, self.ny = self.w.shape[0], self.w.shape[1]

    @staticmethod
    def operator(nx, ny):
        return [(nx + 1, ny, LANES)] * 2 + [(nx, ny, LANES)] * 6

    @staticmethod
    def fields(nx, ny):
        return [(nx, ny, LANES)] * 3

    @staticmethod
    def iterates(nx, ny):
        return [(nx, ny, LANES)] * 2 + [(nx + 2, ny, LANES)] * 2

    def assemble(self):
        nx, ny, step = self.nx, self.ny, self.step
        shape = (ny, LANES)
        row, spot = iota(shape, 0), iota(shape, 1) % (LANES // 2)
        last_row, top = row == ny - 1, spot >= LANES // 2 - step
        walls = (
            jnp.where(row == 0, 1.0, 0.0)
            + jnp.where(last_row, 1.0, 0.0)
            + jnp.where(spot < step, 1.0, 0.0)
            + jnp.where(top, 1.0, 0.0)
        )
        zero = jnp.zeros(shape, jnp.float32)
        half = 0.5 * self.factor
        for ref in (self.xp, self.xm):
            ref[0], ref[nx] = zero, zero

        def x_face(i, _):
            k = half * (self.eps[i - 1] + self.eps[i])
            delta = self.pot[i] - self.pot[i - 1]
            kb = k * bernoulli(delta)
            self.xp[i], self.xm[i] = kb, kb + k * delta
            return 0

        loop(1, nx, x_face, 0)

        def plane(i, _):
            eps, pot = self.eps[i], self.pot[i]
            k = jnp.where(last_row, 0.0, half * (eps + up(eps, 1, 0)))
            delta = up(pot, 1, 0) - pot
            yp = k * bernoulli(delta)
            ym = yp + k * delta
            k = jnp.where(top, 0.0, half * (eps + up(eps, step, 1)))
            delta = up(pot, step, 1) - pot
            zp = k * bernoulli(delta)
            zm = zp + k * delta
            outer = walls + jnp.where(i == 0, 1.0, 0.0) + jnp.where(i == nx - 1, 1.0, 0.0)
            d = (self.xm[i + 1] + self.xp[i]) + (ym + down(yp, 1, 0)) + (zm + down(zp, step, 1))
            d = d + outer * (half * eps * bernoulli(pot)) + self.cap[i]
            w = OMEGA / d
            self.yp[i], self.ym[i], self.zp[i], self.zm[i] = yp, ym, zp, zm
            self.d[i], self.w[i] = d, w
            return 0

        loop(0, nx, plane, 0)

    def coupled(self, u, i):
        v = u[i + 1]
        s = self.xp[i + 1] * u[i + 2] + self.xm[i] * u[i]
        s = s + (self.yp[i] * up(v, 1, 0) + down(self.ym[i] * v, 1, 0))
        return s + (self.zp[i] * up(v, self.step, 1) + down(self.zm[i] * v, self.step, 1))

    def start(self):
        zero = jnp.zeros((self.ny, LANES), jnp.float32)
        for ref in (self.u, self.v):
            ref[0], ref[self.nx + 1] = zero, zero

        def body(i, _):
            wf = self.w[i] * self.f[i]
            self.wf[i] = wf
            self.u[i + 1] = wf
            return 0

        loop(0, self.nx, body, 0)

    def sweep(self, u, v):
        def body(i, _):
            v[i + 1] = (1.0 - OMEGA) * u[i + 1] + self.wf[i] + self.w[i] * self.coupled(u, i)
            return 0

        loop(0, self.nx, body, 0)

    def halve(self, tmp, v):
        step, ny = self.step, self.ny
        tmp[0:ny] = v
        v = tmp[pl.ds(0, ny // 2, stride=2), :] + tmp[pl.ds(1, ny // 2, stride=2), :]
        other = jnp.where(low_lane(v.shape, step), up(v, step, 1), down(v, step, 1))
        return 0.125 * (v + other)

    def descend_fields(self, coarser, tmp):
        def body(i, _):
            for here, there in ((self.eps, coarser.eps), (self.pot, coarser.pot), (self.cap, coarser.cap)):
                there[i] = self.halve(tmp, here[2 * i] + here[2 * i + 1])
            return 0

        loop(0, coarser.nx, body, 0)

    def descend_residual(self, u, coarser, tmp):
        def residual(i):
            return self.f[i] - self.d[i] * u[i + 1] + self.coupled(u, i)

        def body(i, _):
            coarser.f[i] = self.halve(tmp, residual(2 * i) + residual(2 * i + 1))
            return 0

        loop(0, coarser.nx, body, 0)

    def correct(self, u, coarser_u, tmp):
        half_ny = self.ny // 2

        def body(i, _):
            e = coarser_u(i)
            tmp[pl.ds(0, half_ny, stride=2), :] = e
            tmp[pl.ds(1, half_ny, stride=2), :] = e
            wide = tmp[0 : self.ny]
            u[2 * i + 1] = u[2 * i + 1] + wide
            u[2 * i + 2] = u[2 * i + 2] + wide
            return 0

        loop(0, self.nx // 2, body, 0)


def coarsest(lv):
    nx, step = lv.nx, lv.step
    cxp = [lv.w[i] * lv.xp[i + 1] for i in range(nx)]
    cxm = [lv.w[i] * lv.xm[i] for i in range(nx)]
    cyp = [lv.w[i] * lv.yp[i] for i in range(nx)]
    cym = [lv.w[i] * down(lv.ym[i], 1, 0) for i in range(nx)]
    czp = [lv.w[i] * lv.zp[i] for i in range(nx)]
    czm = [lv.w[i] * down(lv.zm[i], step, 1) for i in range(nx)]
    wf = [lv.w[i] * lv.f[i] for i in range(nx)]

    def body(_, u):
        new = []
        for i in range(nx):
            s = czp[i] * up(u[i], step, 1) + czm[i] * down(u[i], step, 1)
            t = cyp[i] * up(u[i], 1, 0) + cym[i] * down(u[i], 1, 0)
            r = (1.0 - OMEGA) * u[i] + wf[i]
            if i + 1 < nx:
                r = r + cxp[i] * u[i + 1]
            if i > 0:
                r = r + cxm[i] * u[i - 1]
            new.append(r + t + s)
        return tuple(new)

    u = lax.fori_loop(0, COARSE_ITERS - 1, body, tuple(wf))
    for i in range(nx):
        lv.u[i + 1] = u[i]


def place(bits, ref, flip, x, y, ny, put):
    bx, by = ref.shape[-3], ref.shape[-2]

    def body(m, _):
        b = m // ny
        to_x = x ^ flip
        for k, bit in enumerate(bits[:-1]):
            to_x = to_x ^ (((b >> k) & 1) * bit)
        row = pl.ds(pl.multiple_of((y ^ (m % ny)) * by, by), by)
        for i in range(bx):
            put(m, i, to_x * bx + i, row)
        return 0

    loop(0, ref.shape[0], body, 0)


def operators_kernel(bits, near, far, *refs):
    x, y, ny = lax.axis_index("gx"), lax.axis_index("gy"), lax.axis_size("gy")
    outs, scratch = refs[: 3 * OPERATOR], refs[3 * OPERATOR :]
    l1, l2, l3 = (
        Level(k + 1, outs[OPERATOR * k : OPERATOR * (k + 1)] + scratch[3 * k : 3 * k + 3]) for k in range(3)
    )
    tmp = scratch[9]
    right = iota((near.shape[-2], LANES), 1) >= LANES // 2
    for ref, flip in ((near, 0), (far, bits[-1])):

        def put(m, i, at, row, ref=ref):
            q = ref[m, 1, i]
            l1.eps[at, row, :] = ref[m, 0, i]
            l1.pot[at, row, :] = jnp.where(right, q, 0.0)
            l1.cap[at, row, :] = jnp.where(right, down(q, LANES // 2, 1), 0.0)

        place(bits, ref, flip, x, y, ny, put)
    l1.assemble()
    l1.descend_fields(l2, tmp)
    l2.assemble()
    l2.descend_fields(l3, tmp)
    l3.assemble()


def second_kernel(bits, near, far, kept, *refs):
    x, y, ny = lax.axis_index("gx"), lax.axis_index("gy"), lax.axis_size("gy")
    given, (out_p, out_n), scratch = refs[: 3 * OPERATOR], refs[3 * OPERATOR : 3 * OPERATOR + 2], refs[3 * OPERATOR + 2 :]
    l1, l2, l3 = (
        Level(k + 1, given[OPERATOR * k : OPERATOR * (k + 1)] + scratch[4 * k : 4 * k + 4]) for k in range(3)
    )
    sol, tmp, fine_a, fine_b = scratch[12:]
    bx, by = near.shape[-3], near.shape[-2]
    for ref, flip in ((near, 0), (far, bits[-1])):

        def put(m, i, at, row, ref=ref):
            l1.f[at, row, :] = ref[m, i]

        place(bits, ref, flip, x, y, ny, put)
    for here, there in ((l1, l2), (l2, l3)):
        here.start()
        here.sweep(here.u, here.v)
        here.descend_residual(here.v, there, tmp)
    coarsest(l3)
    l2.correct(l2.v, lambda i: l3.u[i + 1], tmp)
    l2.sweep(l2.v, l2.u)
    l2.sweep(l2.u, l2.v)
    l1.correct(l1.v, lambda i: l2.v[i + 1], tmp)
    l1.sweep(l1.v, l1.u)
    edge = jnp.zeros((by, LANES), jnp.float32)
    n1x, n1y = l1.nx, l1.ny
    blank = jnp.zeros((n1y + 2 * by, LANES), jnp.float32)
    sol[0], sol[n1x + 1] = blank, blank

    def last(i, _):
        sol[i + 1, 0:by] = edge
        sol[i + 1, by + n1y :] = edge
        sol[i + 1, by : by + n1y] = (
            (1.0 - OMEGA) * l1.u[i + 1] + l1.wf[i] + l1.w[i] * l1.coupled(l1.u, i)
        )
        return 0

    loop(0, n1x, last, 0)

    rows = kept.shape[2]
    own = rows - 2 * RIM
    tile_row = iota((by, LANES), 0)
    spread = iota((by, LANES), 1) // 2

    def widen(v, channel):
        return jnp.take_along_axis(v, spread + channel * (LANES // 2), axis=1)

    def correct(i, _):
        at = x * bx + i
        middle, above, below = (
            sol[at, pl.ds(pl.multiple_of((y + k) * by, by), by), :] for k in (1, 2, 0)
        )
        rim = jnp.where(
            tile_row < 2,
            jnp.broadcast_to(above[0:1], (by, LANES)),
            jnp.where(tile_row >= by - 2, jnp.broadcast_to(below[by - 1 : by], (by, LANES)), 0.0),
        )
        for channel, u in ((0, U_P), (1, U_N)):
            e = widen(middle, channel)
            tmp[pl.ds(0, by, stride=2), :] = e
            tmp[pl.ds(1, by, stride=2), :] = e
            tmp[own:rows] = widen(rim, channel)
            e = tmp[0:rows]
            for k in (0, 1):
                p = RIM - 2 + 2 * i + k
                fine_a[channel, p] = kept[u, p] + e
        return 0

    loop(0, bx + 2, correct, 0)

    def fine(u, channel, i):
        w, wf = ((W_P, WF_P), (W_N, WF_N))[channel]
        s = coupled_fine(kept, lambda j: u[channel, j], i, channel == 0)
        return (1.0 - OMEGA) * u[channel, i] + kept[wf, i] + kept[w, i] * s

    def post_one(i, _):
        for channel in (0, 1):
            fine_b[channel, i] = fine(fine_a, channel, i)
        return 0

    def post_two(i, _):
        out_p[i] = fine(fine_b, 0, i + RIM)[0:own]
        out_n[i] = fine(fine_b, 1, i + RIM)[0:own]
        return 0

    loop(RIM - 1, RIM + 2 * bx + 1, post_one, 0)
    loop(0, 2 * bx, post_two, 0)


def moves(ng, nx, ny):
    def of(partner):
        place = {p: k for k, p in enumerate(itertools.product(range(ng), range(nx), range(ny)))}
        return [(k, place[partner(*p)]) for p, k in place.items()]

    def other(k):
        return k + 1 if k % 2 else k - 1

    return {
        "xa": of(lambda g, a, b: (g, a ^ 1, b)),
        "xb": of(lambda g, a, b: (g, other(a), b) if 0 < a < nx - 1 else (g ^ 1, a, b)),
        "ya": of(lambda g, a, b: (g, a, b ^ 1)),
        "yb": of(lambda g, a, b: (g, a, other(b)) if 0 < b < ny - 1 else (g, a ^ 1, b)),
        **{("x", 1 << k): of(lambda g, a, b, k=k: (g, a ^ (1 << k), b)) for k in range((nx - 1).bit_length())},
        **{("y", 1 << k): of(lambda g, a, b, k=k: (g, a, b ^ (1 << k))) for k in range((ny - 1).bit_length())},
    }


def per_device(ng, nx, ny, layer_class, permittivity, mobility, capture, potential, rhs_psi, rhs_n):
    send = moves(ng, nx, ny)
    f32 = jnp.float32

    def permute(v, name):
        return lax.ppermute(v, ("groups", "gx", "gy"), send[name])

    planes, own = layer_class.shape[0], layer_class.shape[1]
    rows, total = own + 2 * RIM, planes + 2 * RIM
    bx, by = planes // 2, own // 2
    def shape(*dims):
        return jax.ShapeDtypeStruct(dims, f32)

    raw = jnp.stack([potential, rhs_psi, rhs_n])
    a, b = pl.pallas_call(
        rim_y_kernel,
        out_shape=[shape(2 * planes, by, LANES)] * 2,
        in_specs=[VMEM] * 2,
        out_specs=[VMEM] * 2,
        compiler_params=params(16),
    )(layer_class, raw)
    cut = a
    b = permute(b, "yb")
    a = permute(a, "ya")
    later, _ = lax.optimization_barrier(((raw, permittivity, mobility, capture), cut))
    table = jnp.stack(later[1:])
    table = jnp.broadcast_to(table[:, :, None], (*table.shape, LANES))
    fields = pl.pallas_call(
        fields_kernel,
        out_shape=shape(1, 2, bx, by, LANES),
        in_specs=[VMEM] * 3,
        out_specs=VMEM,
        scratch_shapes=[pltpu.VMEM((4, bx, own, LANES), f32)],
        compiler_params=params(16),
    )(table, layer_class, later[0])
    fields_y = [fields, permute(fields, ("y", 1))]
    mid, a, b = pl.pallas_call(
        rim_x_kernel,
        out_shape=[shape(4, planes, rows, LANES)] + [shape(4, RIM, rows, LANES)] * 2,
        in_specs=[VMEM] * 4,
        out_specs=[VMEM] * 3,
        compiler_params=params(16),
    )(layer_class, raw, a, b)
    fields_y, _ = lax.optimization_barrier((jnp.concatenate(fields_y), mid))
    b = permute(b, "xb")
    a = permute(a, "xa")
    kept, block = pl.pallas_call(
        first_kernel,
        out_shape=[shape(KEPT, total, rows, LANES), shape(1, bx, by, LANES)],
        in_specs=[VMEM] * 4,
        out_specs=[VMEM] * 2,
        scratch_shapes=[
            pltpu.VMEM((8, total, rows, LANES), f32),
            pltpu.VMEM((2, bx, own, LANES), f32),
        ],
        compiler_params=params(24),
    )(table, mid, a, b)

    bits = [1 << k for k in reversed(range((nx - 1).bit_length()))]

    def over_y(near, first):
        bit = first
        while bit < ny:
            near = jnp.concatenate([near, permute(near, ("y", bit))])
            bit *= 2
        return near

    def over_x(near):
        for bit in bits[:-1]:
            near = jnp.concatenate([near, permute(near, ("x", bit))], axis=0)
        return near, permute(near, ("x", bits[-1]))

    fields_y = over_y(fields_y, 2)
    pair = jnp.concatenate([block, permute(block, ("y", 1))])
    fields_y, _ = lax.optimization_barrier((fields_y, pair))
    grids = [(bx * nx >> level, by * ny >> level) for level in range(3)]
    large = grids[0][0] * grids[0][1] > 1024
    operators = pl.pallas_call(
        functools.partial(operators_kernel, tuple(bits)),
        out_shape=[shape(*s) for g in grids for s in Level.operator(*g)],
        in_specs=[VMEM] * 2,
        out_specs=[VMEM] * (3 * OPERATOR),
        scratch_shapes=[pltpu.VMEM(s, f32) for g in grids for s in Level.fields(*g)]
        + [pltpu.VMEM((grids[0][1], LANES), f32)],
        compiler_params=params(60 if large else 16),
    )(*over_x(fields_y))
    near, far = over_x(over_y(pair, 2))
    return pl.pallas_call(
        functools.partial(second_kernel, tuple(bits)),
        out_shape=[shape(planes, own, LANES)] * 2,
        in_specs=[VMEM] * (3 + 3 * OPERATOR),
        out_specs=[VMEM] * 2,
        scratch_shapes=[pltpu.VMEM(s, f32) for g in grids for s in Level.iterates(*g)]
        + [
            pltpu.VMEM((grids[0][0] + 2, grids[0][1] + 2 * by, LANES), f32),
            pltpu.VMEM((max(grids[0][1], rows), LANES), f32),
            pltpu.VMEM((2, total, rows, LANES), f32),
            pltpu.VMEM((2, total, rows, LANES), f32),
        ],
        compiler_params=params(60 if large else 16),
    )(near, far, kept, *operators)


def solution(mesh):
    grid = P(("groups", "gx"), "gy", None)
    fn = functools.partial(per_device, *(mesh.shape[a] for a in ("groups", "gx", "gy")))
    return jax.shard_map(
        fn,
        mesh=mesh,
        in_specs=(grid, P(), P(), P(), grid, grid, grid),
        out_specs=(grid, grid),
        check_vma=False,
    )
```

```python
import functools
import itertools
import jax
import jax.numpy as jnp
from jax import lax
from jax.experimental import pallas as pl
from jax.experimental.pallas import tpu as pltpu
from jax.sharding import PartitionSpec as P

OMEGA = 0.8
COARSE_ITERS = 20
RIM = 4
LANES = 128
VMEM = pl.BlockSpec(memory_space=pltpu.VMEM)
HBM = pl.BlockSpec(memory_space=pltpu.HBM)


UNROLL = 16


def loop(first, end, body, init):
    if end - first > UNROLL:
        return lax.fori_loop(first, end, body, init)
    for i in range(first, end):
        body(i, 0)
    return init


def params(mib):
    return pltpu.CompilerParams(vmem_limit_bytes=int(mib * 1024 * 1024))


def bernoulli(x):
    t = x * x
    series = 1.0 - 0.5 * x + t * (1 / 12 + t * (-1 / 720 + t * (1 / 30240)))
    near = t < 0.25
    guarded = jnp.where(near, 1.0, x)
    return jnp.where(near, series, guarded / (jnp.exp(guarded) - 1.0))


def iota(shape, dim):
    return lax.broadcasted_iota(jnp.int32, shape, dim)


def up(v, step, dim):
    return pltpu.roll(v, v.shape[dim] - step, dim)


def down(v, step, dim):
    return pltpu.roll(v, step, dim)


def halve_lanes(a, b):
    lane = iota(a.shape, 1)
    at = (2 * lane) % LANES
    a = jnp.take_along_axis(a + up(a, 1, 1), at, axis=1)
    b = jnp.take_along_axis(b + up(b, 1, 1), at, axis=1)
    return jnp.where(lane < LANES // 2, a, b)


def look_up(table, c, shape):
    found = [jnp.zeros(shape, jnp.float32)] * 3
    for k in range(table.shape[1]):
        same = c == float(k)
        found = [
            jnp.where(same, jnp.broadcast_to(table[f, k : k + 1], shape), found[f]) for f in range(3)
        ]
    return found


def rim_y_kernel(c_in, p_in, fp_in, fn_in, out_a, out_b, c_out, p_out, fp_out, fn_out, cls, sems):
    outs = (c_out, p_out, fp_out, fn_out)
    copies = [
        pltpu.make_async_copy(s, d, sems.at[k])
        for k, (s, d) in enumerate(zip((c_in, p_in, fp_in, fn_in), (cls, *outs[1:])))
    ]
    for c in copies:
        c.start()
    for c in copies:
        c.wait()
    c_out[...] = cls[...].astype(jnp.float32)
    even = lax.axis_index("gy") % 2 == 0
    planes, length = cls.shape[0], cls.shape[1]
    for pair in range(2):
        lo, hi = (
            jnp.concatenate([r[:, at : at + RIM, :] for r in outs[2 * pair : 2 * pair + 2]], axis=1)
            for at in (0, length - RIM)
        )
        out_a[pair * planes : (pair + 1) * planes] = jnp.where(even, hi, lo)
        out_b[pair * planes : (pair + 1) * planes] = jnp.where(even, lo, hi)


def fields_kernel(table, cls, pot, block, work):
    planes, length = cls.shape[0], cls.shape[1]
    bx = planes // 2
    for i in range(bx):
        one, two = (
            look_up(table, cls[2 * i + k], (length, LANES)) for k in (0, 1)
        )
        values = [p + q for p, q in zip(one, two)] + [pot[2 * i] + pot[2 * i + 1]]
        for k, v in enumerate(values):
            work[k, i] = v
    for i in range(bx):
        eps, mob, cap, pot = (
            work[k, i, pl.ds(0, length // 2, stride=2), :] + work[k, i, pl.ds(1, length // 2, stride=2), :]
            for k in range(4)
        )
        for f, v in enumerate((halve_lanes(eps, mob), halve_lanes(cap, pot))):
            block[0, f, i] = 0.125 * v


def rim_x_kernel(cls, pot, fp, fn, in_a, in_b, out, out_a, out_b):
    y, ny = lax.axis_index("gy"), lax.axis_size("gy")
    even_x, even_y = lax.axis_index("gx") % 2 == 0, y % 2 == 0
    planes, length = cls.shape[0], cls.shape[1]
    row = iota((planes, 2 * RIM, LANES), 1)
    for pair in range(2):
        a, b = (r[pair * planes : (pair + 1) * planes] for r in (in_a, in_b))
        hi, lo = jnp.where(even_y, a, b), jnp.where(even_y, b, a)
        for slot in range(2):
            field = 2 * pair + slot
            outside = -1.0 if field == 0 else 0.0
            h, l = jnp.where(y == ny - 1, outside, hi), jnp.where(y == 0, outside, lo)
            if slot == 0:
                l = down(l, RIM, 1)
            else:
                h = down(h, RIM, 1)
            out[field, :, 0:length, :] = (cls, pot, fp, fn)[field][...]
            out[field, :, length : length + 2 * RIM, :] = jnp.where(row < RIM, h, l)
        for slot in range(2):
            field = 2 * pair + slot
            lo_x, hi_x = out[field, 0:RIM], out[field, planes - RIM : planes]
            out_a[field] = jnp.where(even_x, hi_x, lo_x)
            out_b[field] = jnp.where(even_x, lo_x, hi_x)


W_P, GX, GY, GZ, W_N, XP, XM, YP, YM, ZP, ZM, WF_P, WF_N, U_P, U_N = range(15)
KEPT = 15


def coupled_fine(kept, u, i, poisson):
    v = u(i)
    if poisson:
        xp, xm, yp, ym, zp, zm = GX, GX, GY, GY, GZ, GZ
    else:
        xp, xm, yp, ym, zp, zm = XP, XM, YP, YM, ZP, ZM
    s = kept[xp, i] * u(i + 1) + kept[xm, i - 1] * u(i - 1)
    s = s + (kept[yp, i] * up(v, 1, 0) + down(kept[ym, i] * v, 1, 0))
    return s + (kept[zp, i] * up(v, 1, 1) + down(kept[zm, i] * v, 1, 1))


def first_kernel(table, mid, in_a, in_b, kept, block, fld, work):
    x, nx = lax.axis_index("gx"), lax.axis_size("gx")
    even = x % 2 == 0
    planes = mid.shape[1]
    rows = mid.shape[2]
    own = rows - 2 * RIM
    total = planes + 2 * RIM
    EPS, MOB, POT, CAP, F_P, F_N, D_P, D_N = range(8)

    def materials(i, c, pot, fp, fn):
        eps, mob, cap = look_up(table, c, (rows, LANES))
        fld[EPS, i], fld[MOB, i], fld[POT, i], fld[CAP, i] = eps, mob, pot, cap
        fld[F_P, i], fld[F_N, i] = fp, fn

    def low(i, _):
        v = [jnp.where(even, in_b[f, i], in_a[f, i]) for f in range(4)]
        materials(i, *[jnp.where(x == 0, -1.0 if f == 0 else 0.0, v[f]) for f in range(4)])
        return 0

    def middle(i, _):
        materials(i + RIM, *[mid[f, i] for f in range(4)])
        return 0

    def high(i, _):
        v = [jnp.where(even, in_a[f, i], in_b[f, i]) for f in range(4)]
        materials(
            i + RIM + planes,
            *[jnp.where(x == nx - 1, -1.0 if f == 0 else 0.0, v[f]) for f in range(4)],
        )
        return 0

    loop(0, RIM, low, 0)
    loop(0, planes, middle, 0)
    loop(0, RIM, high, 0)

    shape = (rows, LANES)
    lane = iota(shape, 1)
    ends = (lane == 0) | (lane == LANES - 1)
    top = lane == LANES - 1

    def x_faces(i):
        eps, mob, pot = fld[EPS, i], fld[MOB, i], fld[POT, i]
        kept[GX, i] = 0.5 * (eps + fld[EPS, i + 1])
        k = 0.5 * (mob + fld[MOB, i + 1])
        delta = fld[POT, i + 1] - pot
        kb = k * bernoulli(delta)
        kept[XP, i] = kb
        kept[XM, i] = kb + k * delta

    x_faces(0)

    def operators(i, _):
        x_faces(i)
        eps, mob, pot = fld[EPS, i], fld[MOB, i], fld[POT, i]
        gy = 0.5 * (eps + up(eps, 1, 0))
        k = 0.5 * (mob + up(mob, 1, 0))
        delta = up(pot, 1, 0) - pot
        yp = k * bernoulli(delta)
        ym = yp + k * delta
        gz = jnp.where(top, 0.0, 0.5 * (eps + up(eps, 1, 1)))
        k = jnp.where(top, 0.0, 0.5 * (mob + up(mob, 1, 1)))
        delta = up(pot, 1, 1) - pot
        zp = k * bernoulli(delta)
        zm = zp + k * delta
        kept[GY, i], kept[YP, i], kept[YM, i] = gy, yp, ym
        kept[GZ, i], kept[ZP, i], kept[ZM, i] = gz, zp, zm
        d_p = (kept[GX, i] + kept[GX, i - 1]) + (gy + down(gy, 1, 0)) + (gz + down(gz, 1, 1))
        d_p = d_p + jnp.where(ends, 0.5 * eps, 0.0)
        d_n = (kept[XM, i] + kept[XP, i - 1]) + (ym + down(yp, 1, 0)) + (zm + down(zp, 1, 1))
        d_n = d_n + jnp.where(ends, 0.5 * mob * bernoulli(pot), 0.0) + fld[CAP, i]
        inside = eps > 0.0
        w_p = jnp.where(inside, OMEGA / jnp.where(inside, d_p, 1.0), 0.0)
        w_n = jnp.where(inside, OMEGA / jnp.where(inside, d_n, 1.0), 0.0)
        kept[W_P, i], kept[W_N, i] = w_p, w_n
        kept[WF_P, i], kept[WF_N, i] = w_p * fld[F_P, i], w_n * fld[F_N, i]
        fld[D_P, i], fld[D_N, i] = d_p, d_n
        return 0

    loop(1, total - 1, operators, 0)

    def sweep(i, _):
        for poisson, w, wf, u in ((True, W_P, WF_P, U_P), (False, W_N, WF_N, U_N)):
            s = coupled_fine(kept, lambda j: kept[wf, j], i, poisson)
            kept[u, i] = (2.0 - OMEGA) * kept[wf, i] + kept[w, i] * s
        return 0

    loop(2, total - 2, sweep, 0)

    def residual(i, poisson, f, d, u):
        s = coupled_fine(kept, lambda j: kept[u, j], i, poisson)
        return fld[f, i] - fld[d, i] * kept[u, i] + s

    def coarse(i, _):
        at = RIM + 2 * i
        r_p = residual(at, True, F_P, D_P, U_P) + residual(at + 1, True, F_P, D_P, U_P)
        r_n = residual(at, False, F_N, D_N, U_N) + residual(at + 1, False, F_N, D_N, U_N)
        work[0, i], work[1, i] = r_p[0:own], r_n[0:own]
        r_p, r_n = (
            work[k, i, pl.ds(0, own // 2, stride=2), :] + work[k, i, pl.ds(1, own // 2, stride=2), :]
            for k in range(2)
        )
        block[0, i] = 0.125 * halve_lanes(r_p, r_n)
        return 0

    loop(0, planes // 2, coarse, 0)


def low_lane(shape, bit):
    return (iota(shape, 1) & bit) == 0


OPERATOR = 8


class Level:
    def __init__(self, level, refs):
        self.level, self.step, self.factor = level, 1 << (level - 1), 0.25**level
        (self.xp, self.xm, self.yp, self.ym, self.zp, self.zm, self.w, self.d) = refs[:OPERATOR]
        if len(refs) == OPERATOR + 3:
            self.eps, self.pot, self.cap = refs[OPERATOR:]
        else:
            self.f, self.wf, self.u, self.v = refs[OPERATOR:]
        self.nx, self.ny = self.w.shape[0], self.w.shape[1]

    @staticmethod
    def operator(nx, ny):
        return [(nx + 1, ny, LANES)] * 2 + [(nx, ny, LANES)] * 6

    @staticmethod
    def fields(nx, ny):
        return [(nx, ny, LANES)] * 3

    @staticmethod
    def iterates(nx, ny):
        return [(nx, ny, LANES)] * 2 + [(nx + 2, ny, LANES)] * 2

    def assemble(self):
        nx, ny, step = self.nx, self.ny, self.step
        shape = (ny, LANES)
        row, spot = iota(shape, 0), iota(shape, 1) % (LANES // 2)
        last_row, top = row == ny - 1, spot >= LANES // 2 - step
        walls = (
            jnp.where(row == 0, 1.0, 0.0)
            + jnp.where(last_row, 1.0, 0.0)
            + jnp.where(spot < step, 1.0, 0.0)
            + jnp.where(top, 1.0, 0.0)
        )
        zero = jnp.zeros(shape, jnp.float32)
        half = 0.5 * self.factor
        for ref in (self.xp, self.xm):
            ref[0], ref[nx] = zero, zero

        def x_face(i, _):
            k = half * (self.eps[i - 1] + self.eps[i])
            delta = self.pot[i] - self.pot[i - 1]
            kb = k * bernoulli(delta)
            self.xp[i], self.xm[i] = kb, kb + k * delta
            return 0

        loop(1, nx, x_face, 0)

        def plane(i, _):
            eps, pot = self.eps[i], self.pot[i]
            k = jnp.where(last_row, 0.0, half * (eps + up(eps, 1, 0)))
            delta = up(pot, 1, 0) - pot
            yp = k * bernoulli(delta)
            ym = yp + k * delta
            k = jnp.where(top, 0.0, half * (eps + up(eps, step, 1)))
            delta = up(pot, step, 1) - pot
            zp = k * bernoulli(delta)
            zm = zp + k * delta
            outer = walls + jnp.where(i == 0, 1.0, 0.0) + jnp.where(i == nx - 1, 1.0, 0.0)
            d = (self.xm[i + 1] + self.xp[i]) + (ym + down(yp, 1, 0)) + (zm + down(zp, step, 1))
            d = d + outer * (half * eps * bernoulli(pot)) + self.cap[i]
            w = OMEGA / d
            self.yp[i], self.ym[i], self.zp[i], self.zm[i] = yp, ym, zp, zm
            self.d[i], self.w[i] = d, w
            return 0

        loop(0, nx, plane, 0)

    def coupled(self, u, i):
        v = u[i + 1]
        s = self.xp[i + 1] * u[i + 2] + self.xm[i] * u[i]
        s = s + (self.yp[i] * up(v, 1, 0) + down(self.ym[i] * v, 1, 0))
        return s + (self.zp[i] * up(v, self.step, 1) + down(self.zm[i] * v, self.step, 1))

    def start(self):
        zero = jnp.zeros((self.ny, LANES), jnp.float32)
        for ref in (self.u, self.v):
            ref[0], ref[self.nx + 1] = zero, zero

        def body(i, _):
            wf = self.w[i] * self.f[i]
            self.wf[i] = wf
            self.u[i + 1] = wf
            return 0

        loop(0, self.nx, body, 0)

    def sweep(self, u, v):
        def body(i, _):
            v[i + 1] = (1.0 - OMEGA) * u[i + 1] + self.wf[i] + self.w[i] * self.coupled(u, i)
            return 0

        loop(0, self.nx, body, 0)

    def halve(self, tmp, v):
        step, ny = self.step, self.ny
        tmp[0:ny] = v
        v = tmp[pl.ds(0, ny // 2, stride=2), :] + tmp[pl.ds(1, ny // 2, stride=2), :]
        other = jnp.where(low_lane(v.shape, step), up(v, step, 1), down(v, step, 1))
        return 0.125 * (v + other)

    def descend_fields(self, coarser, tmp):
        def body(i, _):
            for here, there in ((self.eps, coarser.eps), (self.pot, coarser.pot), (self.cap, coarser.cap)):
                there[i] = self.halve(tmp, here[2 * i] + here[2 * i + 1])
            return 0

        loop(0, coarser.nx, body, 0)

    def descend_residual(self, u, coarser, tmp):
        def residual(i):
            return self.f[i] - self.d[i] * u[i + 1] + self.coupled(u, i)

        def body(i, _):
            coarser.f[i] = self.halve(tmp, residual(2 * i) + residual(2 * i + 1))
            return 0

        loop(0, coarser.nx, body, 0)

    def correct(self, u, coarser_u, tmp):
        half_ny = self.ny // 2

        def body(i, _):
            e = coarser_u(i)
            tmp[pl.ds(0, half_ny, stride=2), :] = e
            tmp[pl.ds(1, half_ny, stride=2), :] = e
            wide = tmp[0 : self.ny]
            u[2 * i + 1] = u[2 * i + 1] + wide
            u[2 * i + 2] = u[2 * i + 2] + wide
            return 0

        loop(0, self.nx // 2, body, 0)


def coarsest(lv):
    nx, step = lv.nx, lv.step
    cxp = [lv.w[i] * lv.xp[i + 1] for i in range(nx)]
    cxm = [lv.w[i] * lv.xm[i] for i in range(nx)]
    cyp = [lv.w[i] * lv.yp[i] for i in range(nx)]
    cym = [lv.w[i] * down(lv.ym[i], 1, 0) for i in range(nx)]
    czp = [lv.w[i] * lv.zp[i] for i in range(nx)]
    czm = [lv.w[i] * down(lv.zm[i], step, 1) for i in range(nx)]
    wf = [lv.w[i] * lv.f[i] for i in range(nx)]

    def body(_, u):
        new = []
        for i in range(nx):
            s = czp[i] * up(u[i], step, 1) + czm[i] * down(u[i], step, 1)
            t = cyp[i] * up(u[i], 1, 0) + cym[i] * down(u[i], 1, 0)
            r = (1.0 - OMEGA) * u[i] + wf[i]
            if i + 1 < nx:
                r = r + cxp[i] * u[i + 1]
            if i > 0:
                r = r + cxm[i] * u[i - 1]
            new.append(r + t + s)
        return tuple(new)

    u = lax.fori_loop(0, COARSE_ITERS - 1, body, tuple(wf))
    for i in range(nx):
        lv.u[i + 1] = u[i]


def place(bits, ref, flip, x, y, ny, put):
    bx, by = ref.shape[-3], ref.shape[-2]

    def body(m, _):
        b = m // ny
        to_x = x ^ flip
        for k, bit in enumerate(bits[:-1]):
            to_x = to_x ^ (((b >> k) & 1) * bit)
        row = pl.ds(pl.multiple_of((y ^ (m % ny)) * by, by), by)
        for i in range(bx):
            put(m, i, to_x * bx + i, row)
        return 0

    loop(0, ref.shape[0], body, 0)


def operators_kernel(bits, near, far, *refs):
    x, y, ny = lax.axis_index("gx"), lax.axis_index("gy"), lax.axis_size("gy")
    outs, scratch = refs[: 3 * OPERATOR], refs[3 * OPERATOR :]
    l1, l2, l3 = (
        Level(k + 1, outs[OPERATOR * k : OPERATOR * (k + 1)] + scratch[3 * k : 3 * k + 3]) for k in range(3)
    )
    tmp = scratch[9]
    right = iota((near.shape[-2], LANES), 1) >= LANES // 2
    for ref, flip in ((near, 0), (far, bits[-1])):

        def put(m, i, at, row, ref=ref):
            q = ref[m, 1, i]
            l1.eps[at, row, :] = ref[m, 0, i]
            l1.pot[at, row, :] = jnp.where(right, q, 0.0)
            l1.cap[at, row, :] = jnp.where(right, down(q, LANES // 2, 1), 0.0)

        place(bits, ref, flip, x, y, ny, put)
    l1.assemble()
    l1.descend_fields(l2, tmp)
    l2.assemble()
    l2.descend_fields(l3, tmp)
    l3.assemble()


def second_kernel(bits, near, far, kept, *refs):
    x, y, ny = lax.axis_index("gx"), lax.axis_index("gy"), lax.axis_size("gy")
    given, (out_p, out_n), scratch = refs[: 3 * OPERATOR], refs[3 * OPERATOR : 3 * OPERATOR + 2], refs[3 * OPERATOR + 2 :]
    l1, l2, l3 = (
        Level(k + 1, given[OPERATOR * k : OPERATOR * (k + 1)] + scratch[4 * k : 4 * k + 4]) for k in range(3)
    )
    sol, tmp, fine_a, fine_b = scratch[12:]
    bx, by = near.shape[-3], near.shape[-2]
    for ref, flip in ((near, 0), (far, bits[-1])):

        def put(m, i, at, row, ref=ref):
            l1.f[at, row, :] = ref[m, i]

        place(bits, ref, flip, x, y, ny, put)
    for here, there in ((l1, l2), (l2, l3)):
        here.start()
        here.sweep(here.u, here.v)
        here.descend_residual(here.v, there, tmp)
    coarsest(l3)
    l2.correct(l2.v, lambda i: l3.u[i + 1], tmp)
    l2.sweep(l2.v, l2.u)
    l2.sweep(l2.u, l2.v)
    l1.correct(l1.v, lambda i: l2.v[i + 1], tmp)
    l1.sweep(l1.v, l1.u)
    edge = jnp.zeros((by, LANES), jnp.float32)
    n1x, n1y = l1.nx, l1.ny
    blank = jnp.zeros((n1y + 2 * by, LANES), jnp.float32)
    sol[0], sol[n1x + 1] = blank, blank

    def last(i, _):
        sol[i + 1, 0:by] = edge
        sol[i + 1, by + n1y :] = edge
        sol[i + 1, by : by + n1y] = (
            (1.0 - OMEGA) * l1.u[i + 1] + l1.wf[i] + l1.w[i] * l1.coupled(l1.u, i)
        )
        return 0

    loop(0, n1x, last, 0)

    rows = kept.shape[2]
    own = rows - 2 * RIM
    tile_row = iota((by, LANES), 0)
    spread = iota((by, LANES), 1) // 2

    def widen(v, channel):
        return jnp.take_along_axis(v, spread + channel * (LANES // 2), axis=1)

    def correct(i, _):
        at = x * bx + i
        middle, above, below = (
            sol[at, pl.ds(pl.multiple_of((y + k) * by, by), by), :] for k in (1, 2, 0)
        )
        rim = jnp.where(
            tile_row < 2,
            jnp.broadcast_to(above[0:1], (by, LANES)),
            jnp.where(tile_row >= by - 2, jnp.broadcast_to(below[by - 1 : by], (by, LANES)), 0.0),
        )
        for channel, u in ((0, U_P), (1, U_N)):
            e = widen(middle, channel)
            tmp[pl.ds(0, by, stride=2), :] = e
            tmp[pl.ds(1, by, stride=2), :] = e
            tmp[own:rows] = widen(rim, channel)
            e = tmp[0:rows]
            for k in (0, 1):
                p = RIM - 2 + 2 * i + k
                fine_a[channel, p] = kept[u, p] + e
        return 0

    loop(0, bx + 2, correct, 0)

    def fine(u, channel, i):
        w, wf = ((W_P, WF_P), (W_N, WF_N))[channel]
        s = coupled_fine(kept, lambda j: u[channel, j], i, channel == 0)
        return (1.0 - OMEGA) * u[channel, i] + kept[wf, i] + kept[w, i] * s

    def post_one(i, _):
        for channel in (0, 1):
            fine_b[channel, i] = fine(fine_a, channel, i)
        return 0

    def post_two(i, _):
        out_p[i] = fine(fine_b, 0, i + RIM)[0:own]
        out_n[i] = fine(fine_b, 1, i + RIM)[0:own]
        return 0

    loop(RIM - 1, RIM + 2 * bx + 1, post_one, 0)
    loop(0, 2 * bx, post_two, 0)


def moves(ng, nx, ny):
    def of(partner):
        place = {p: k for k, p in enumerate(itertools.product(range(ng), range(nx), range(ny)))}
        return [(k, place[partner(*p)]) for p, k in place.items()]

    def other(k):
        return k + 1 if k % 2 else k - 1

    return {
        "xa": of(lambda g, a, b: (g, a ^ 1, b)),
        "xb": of(lambda g, a, b: (g, other(a), b) if 0 < a < nx - 1 else (g ^ 1, a, b)),
        "ya": of(lambda g, a, b: (g, a, b ^ 1)),
        "yb": of(lambda g, a, b: (g, a, other(b)) if 0 < b < ny - 1 else (g, a ^ 1, b)),
        **{("x", 1 << k): of(lambda g, a, b, k=k: (g, a ^ (1 << k), b)) for k in range((nx - 1).bit_length())},
        **{("y", 1 << k): of(lambda g, a, b, k=k: (g, a, b ^ (1 << k))) for k in range((ny - 1).bit_length())},
    }


def per_device(ng, nx, ny, layer_class, permittivity, mobility, capture, potential, rhs_psi, rhs_n):
    send = moves(ng, nx, ny)
    f32 = jnp.float32

    def permute(v, name):
        return lax.ppermute(v, ("groups", "gx", "gy"), send[name])

    planes, own = layer_class.shape[0], layer_class.shape[1]
    rows, total = own + 2 * RIM, planes + 2 * RIM
    bx, by = planes // 2, own // 2
    def shape(*dims):
        return jax.ShapeDtypeStruct(dims, f32)

    cell = (planes, own, LANES)
    a, b, *raw = pl.pallas_call(
        rim_y_kernel,
        out_shape=[shape(2 * planes, by, LANES)] * 2 + [shape(*cell)] * 4,
        in_specs=[HBM] * 4,
        out_specs=[VMEM] * 6,
        scratch_shapes=[pltpu.VMEM(cell, jnp.int32), pltpu.SemaphoreType.DMA((4,))],
        compiler_params=params(53.55),
    )(layer_class, potential, rhs_psi, rhs_n)
    cut = a
    b = permute(b, "yb")
    a = permute(a, "ya")
    later, _ = lax.optimization_barrier(((permittivity, mobility, capture, raw[1]), cut))
    table = jnp.stack(later[:3])
    table = jnp.broadcast_to(table[:, :, None], (*table.shape, LANES))
    fields = pl.pallas_call(
        fields_kernel,
        out_shape=shape(1, 2, bx, by, LANES),
        in_specs=[VMEM] * 3,
        out_specs=VMEM,
        scratch_shapes=[pltpu.VMEM((4, bx, own, LANES), f32)],
        compiler_params=params(16),
    )(table, raw[0], later[3])
    fields_y = [fields, permute(fields, ("y", 1))]
    mid, a, b = pl.pallas_call(
        rim_x_kernel,
        out_shape=[shape(4, planes, rows, LANES)] + [shape(4, RIM, rows, LANES)] * 2,
        in_specs=[VMEM] * 6,
        out_specs=[VMEM] * 3,
        compiler_params=params(16),
    )(*raw, a, b)
    fields_y, _ = lax.optimization_barrier((jnp.concatenate(fields_y), mid))
    b = permute(b, "xb")
    a = permute(a, "xa")
    kept, block = pl.pallas_call(
        first_kernel,
        out_shape=[shape(KEPT, total, rows, LANES), shape(1, bx, by, LANES)],
        in_specs=[VMEM] * 4,
        out_specs=[VMEM] * 2,
        scratch_shapes=[
            pltpu.VMEM((8, total, rows, LANES), f32),
            pltpu.VMEM((2, bx, own, LANES), f32),
        ],
        compiler_params=params(24),
    )(table, mid, a, b)

    bits = [1 << k for k in reversed(range((nx - 1).bit_length()))]

    def over_y(near, first):
        bit = first
        while bit < ny:
            near = jnp.concatenate([near, permute(near, ("y", bit))])
            bit *= 2
        return near

    def over_x(near):
        for bit in bits[:-1]:
            near = jnp.concatenate([near, permute(near, ("x", bit))], axis=0)
        return near, permute(near, ("x", bits[-1]))

    fields_y = over_y(fields_y, 2)
    pair = jnp.concatenate([block, permute(block, ("y", 1))])
    fields_y, _ = lax.optimization_barrier((fields_y, pair))
    grids = [(bx * nx >> level, by * ny >> level) for level in range(3)]
    large = grids[0][0] * grids[0][1] > 1024
    operators = pl.pallas_call(
        functools.partial(operators_kernel, tuple(bits)),
        out_shape=[shape(*s) for g in grids for s in Level.operator(*g)],
        in_specs=[VMEM] * 2,
        out_specs=[VMEM] * (3 * OPERATOR),
        scratch_shapes=[pltpu.VMEM(s, f32) for g in grids for s in Level.fields(*g)]
        + [pltpu.VMEM((grids[0][1], LANES), f32)],
        compiler_params=params(60 if large else 16),
    )(*over_x(fields_y))
    near, far = over_x(over_y(pair, 2))
    return pl.pallas_call(
        functools.partial(second_kernel, tuple(bits)),
        out_shape=[shape(planes, own, LANES)] * 2,
        in_specs=[VMEM] * (3 + 3 * OPERATOR),
        out_specs=[VMEM] * 2,
        scratch_shapes=[pltpu.VMEM(s, f32) for g in grids for s in Level.iterates(*g)]
        + [
            pltpu.VMEM((grids[0][0] + 2, grids[0][1] + 2 * by, LANES), f32),
            pltpu.VMEM((max(grids[0][1], rows), LANES), f32),
            pltpu.VMEM((2, total, rows, LANES), f32),
            pltpu.VMEM((2, total, rows, LANES), f32),
        ],
        compiler_params=params(60 if large else 16),
    )(near, far, kept, *operators)


def solution(mesh):
    grid = P(("groups", "gx"), "gy", None)
    fn = functools.partial(per_device, *(mesh.shape[a] for a in ("groups", "gx", "gy")))
    return jax.shard_map(
        fn,
        mesh=mesh,
        in_specs=(grid, P(), P(), P(), grid, grid, grid),
        out_specs=(grid, grid),
        check_vma=False,
    )
```

```python
import functools
import itertools
import jax
import jax.numpy as jnp
from jax import lax
from jax.experimental import pallas as pl
from jax.experimental.pallas import tpu as pltpu
from jax.sharding import PartitionSpec as P

OMEGA = 0.8
COARSE_ITERS = 20
RIM = 4
LANES = 128
VMEM = pl.BlockSpec(memory_space=pltpu.VMEM)
HBM = pl.BlockSpec(memory_space=pltpu.HBM)


UNROLL = 16


def loop(first, end, body, init):
    if end - first > UNROLL:
        return lax.fori_loop(first, end, body, init)
    for i in range(first, end):
        body(i, 0)
    return init


def params(mib):
    return pltpu.CompilerParams(vmem_limit_bytes=int(mib * 1024 * 1024))


def bernoulli(x):
    t = x * x
    series = (1.0 - 0.5 * x) + t * (1 / 12 - t * (1 / 720))
    near = t < 0.0625
    guarded = jnp.where(near, 1.0, x)
    return jnp.where(near, series, guarded / (jnp.exp(guarded) - 1.0))


def iota(shape, dim):
    return lax.broadcasted_iota(jnp.int32, shape, dim)


def up(v, step, dim):
    return pltpu.roll(v, v.shape[dim] - step, dim)


def down(v, step, dim):
    return pltpu.roll(v, step, dim)


def halve_lanes(a, b):
    lane = iota(a.shape, 1)
    at = (2 * lane) % LANES
    a = jnp.take_along_axis(a + up(a, 1, 1), at, axis=1)
    b = jnp.take_along_axis(b + up(b, 1, 1), at, axis=1)
    return jnp.where(lane < LANES // 2, a, b)


def look_up(table, c, shape):
    found = [jnp.zeros(shape, jnp.float32)] * 3
    for k in range(table.shape[1]):
        same = c == float(k)
        found = [
            jnp.where(same, jnp.broadcast_to(table[f, k : k + 1], shape), found[f]) for f in range(3)
        ]
    return found


def rim_y_kernel(table, c_in, p_in, fp_in, fn_in, out_a, out_b, block, c_out, p_out, fp_out, fn_out, cls, work, sems):
    outs = (c_out, p_out, fp_out, fn_out)
    copies = [
        pltpu.make_async_copy(s, d, sems.at[k])
        for k, (s, d) in enumerate(zip((c_in, p_in, fp_in, fn_in), (cls, *outs[1:])))
    ]
    for c in copies:
        c.start()
    for c in copies:
        c.wait()
    c_out[...] = cls[...].astype(jnp.float32)
    even = lax.axis_index("gy") % 2 == 0
    planes, length = cls.shape[0], cls.shape[1]
    for pair in range(2):
        lo, hi = (
            jnp.concatenate([r[:, at : at + RIM, :] for r in outs[2 * pair : 2 * pair + 2]], axis=1)
            for at in (0, length - RIM)
        )
        out_a[pair * planes : (pair + 1) * planes] = jnp.where(even, hi, lo)
        out_b[pair * planes : (pair + 1) * planes] = jnp.where(even, lo, hi)
    bx = planes // 2
    for i in range(bx):
        one, two = (look_up(table, c_out[2 * i + k], (length, LANES)) for k in (0, 1))
        values = [p + q for p, q in zip(one, two)] + [p_out[2 * i] + p_out[2 * i + 1]]
        for k, v in enumerate(values):
            work[k, i] = v
    for i in range(bx):
        eps, mob, cap, pot = (
            work[k, i, pl.ds(0, length // 2, stride=2), :] + work[k, i, pl.ds(1, length // 2, stride=2), :]
            for k in range(4)
        )
        for f, v in enumerate((halve_lanes(eps, mob), halve_lanes(cap, pot))):
            block[0, f, i] = 0.125 * v


def rim_x_kernel(cls, pot, fp, fn, in_a, in_b, out, out_a, out_b):
    y, ny = lax.axis_index("gy"), lax.axis_size("gy")
    even_x, even_y = lax.axis_index("gx") % 2 == 0, y % 2 == 0
    planes, length = cls.shape[0], cls.shape[1]
    row = iota((planes, 2 * RIM, LANES), 1)
    for pair in range(2):
        a, b = (r[pair * planes : (pair + 1) * planes] for r in (in_a, in_b))
        hi, lo = jnp.where(even_y, a, b), jnp.where(even_y, b, a)
        for slot in range(2):
            field = 2 * pair + slot
            outside = -1.0 if field == 0 else 0.0
            h, l = jnp.where(y == ny - 1, outside, hi), jnp.where(y == 0, outside, lo)
            if slot == 0:
                l = down(l, RIM, 1)
            else:
                h = down(h, RIM, 1)
            out[field, :, 0:length, :] = (cls, pot, fp, fn)[field][...]
            out[field, :, length : length + 2 * RIM, :] = jnp.where(row < RIM, h, l)
        for slot in range(2):
            field = 2 * pair + slot
            lo_x, hi_x = out[field, 0:RIM], out[field, planes - RIM : planes]
            out_a[field] = jnp.where(even_x, hi_x, lo_x)
            out_b[field] = jnp.where(even_x, lo_x, hi_x)


W_P, GX, GY, GZ, W_N, XP, XM, YP, YM, ZP, ZM, WF_P, WF_N, U_P, U_N = range(15)
KEPT = 15


def coupled_fine(kept, u, i, poisson):
    v = u(i)
    if poisson:
        xp, xm, yp, ym, zp, zm = GX, GX, GY, GY, GZ, GZ
    else:
        xp, xm, yp, ym, zp, zm = XP, XM, YP, YM, ZP, ZM
    s = kept[xp, i] * u(i + 1) + kept[xm, i - 1] * u(i - 1)
    s = s + (kept[yp, i] * up(v, 1, 0) + down(kept[ym, i] * v, 1, 0))
    return s + (kept[zp, i] * up(v, 1, 1) + down(kept[zm, i] * v, 1, 1))


def first_kernel(table, mid, in_a, in_b, kept, block, fld, work):
    x, nx = lax.axis_index("gx"), lax.axis_size("gx")
    even = x % 2 == 0
    planes = mid.shape[1]
    rows = mid.shape[2]
    own = rows - 2 * RIM
    total = planes + 2 * RIM
    EPS, MOB, POT, CAP, F_P, F_N, D_P, D_N = range(8)

    def materials(i, c, pot, fp, fn):
        eps, mob, cap = look_up(table, c, (rows, LANES))
        fld[EPS, i], fld[MOB, i], fld[POT, i], fld[CAP, i] = eps, mob, pot, cap
        fld[F_P, i], fld[F_N, i] = fp, fn

    def low(i, _):
        v = [jnp.where(even, in_b[f, i], in_a[f, i]) for f in range(4)]
        materials(i, *[jnp.where(x == 0, -1.0 if f == 0 else 0.0, v[f]) for f in range(4)])
        return 0

    def middle(i, _):
        materials(i + RIM, *[mid[f, i] for f in range(4)])
        return 0

    def high(i, _):
        v = [jnp.where(even, in_a[f, i], in_b[f, i]) for f in range(4)]
        materials(
            i + RIM + planes,
            *[jnp.where(x == nx - 1, -1.0 if f == 0 else 0.0, v[f]) for f in range(4)],
        )
        return 0

    loop(0, RIM, low, 0)
    loop(0, planes, middle, 0)
    loop(0, RIM, high, 0)

    shape = (rows, LANES)
    lane = iota(shape, 1)
    ends = (lane == 0) | (lane == LANES - 1)
    top = lane == LANES - 1

    def x_faces(i):
        eps, mob, pot = fld[EPS, i], fld[MOB, i], fld[POT, i]
        kept[GX, i] = 0.5 * (eps + fld[EPS, i + 1])
        k = 0.5 * (mob + fld[MOB, i + 1])
        delta = fld[POT, i + 1] - pot
        kb = k * bernoulli(delta)
        kept[XP, i] = kb
        kept[XM, i] = kb + k * delta

    x_faces(0)

    def operators(i, _):
        x_faces(i)
        eps, mob, pot = fld[EPS, i], fld[MOB, i], fld[POT, i]
        gy = 0.5 * (eps + up(eps, 1, 0))
        k = 0.5 * (mob + up(mob, 1, 0))
        delta = up(pot, 1, 0) - pot
        yp = k * bernoulli(delta)
        ym = yp + k * delta
        gz = jnp.where(top, 0.0, 0.5 * (eps + up(eps, 1, 1)))
        k = jnp.where(top, 0.0, 0.5 * (mob + up(mob, 1, 1)))
        delta = up(pot, 1, 1) - pot
        zp = k * bernoulli(delta)
        zm = zp + k * delta
        kept[GY, i], kept[YP, i], kept[YM, i] = gy, yp, ym
        kept[GZ, i], kept[ZP, i], kept[ZM, i] = gz, zp, zm
        d_p = (kept[GX, i] + kept[GX, i - 1]) + (gy + down(gy, 1, 0)) + (gz + down(gz, 1, 1))
        d_p = d_p + jnp.where(ends, 0.5 * eps, 0.0)
        d_n = (kept[XM, i] + kept[XP, i - 1]) + (ym + down(yp, 1, 0)) + (zm + down(zp, 1, 1))
        d_n = d_n + jnp.where(ends, 0.5 * mob * bernoulli(pot), 0.0) + fld[CAP, i]
        inside = eps > 0.0
        w_p = jnp.where(inside, OMEGA / jnp.where(inside, d_p, 1.0), 0.0)
        w_n = jnp.where(inside, OMEGA / jnp.where(inside, d_n, 1.0), 0.0)
        kept[W_P, i], kept[W_N, i] = w_p, w_n
        kept[WF_P, i], kept[WF_N, i] = w_p * fld[F_P, i], w_n * fld[F_N, i]
        fld[D_P, i], fld[D_N, i] = d_p, d_n
        return 0

    loop(1, total - 1, operators, 0)

    def sweep(i, _):
        for poisson, w, wf, u in ((True, W_P, WF_P, U_P), (False, W_N, WF_N, U_N)):
            s = coupled_fine(kept, lambda j: kept[wf, j], i, poisson)
            kept[u, i] = (2.0 - OMEGA) * kept[wf, i] + kept[w, i] * s
        return 0

    loop(2, total - 2, sweep, 0)

    def residual(i, poisson, f, d, u):
        s = coupled_fine(kept, lambda j: kept[u, j], i, poisson)
        return fld[f, i] - fld[d, i] * kept[u, i] + s

    def coarse(i, _):
        at = RIM + 2 * i
        r_p = residual(at, True, F_P, D_P, U_P) + residual(at + 1, True, F_P, D_P, U_P)
        r_n = residual(at, False, F_N, D_N, U_N) + residual(at + 1, False, F_N, D_N, U_N)
        work[0, i], work[1, i] = r_p[0:own], r_n[0:own]
        r_p, r_n = (
            work[k, i, pl.ds(0, own // 2, stride=2), :] + work[k, i, pl.ds(1, own // 2, stride=2), :]
            for k in range(2)
        )
        block[0, i] = 0.125 * halve_lanes(r_p, r_n)
        return 0

    loop(0, planes // 2, coarse, 0)


def low_lane(shape, bit):
    return (iota(shape, 1) & bit) == 0


OPERATOR = 8


class Level:
    def __init__(self, level, refs):
        self.level, self.step, self.factor = level, 1 << (level - 1), 0.25**level
        (self.xp, self.xm, self.yp, self.ym, self.zp, self.zm, self.w, self.d) = refs[:OPERATOR]
        if len(refs) == OPERATOR + 3:
            self.eps, self.pot, self.cap = refs[OPERATOR:]
        else:
            self.f, self.wf, self.u, self.v = refs[OPERATOR:]
        self.nx, self.ny = self.w.shape[0], self.w.shape[1]

    @staticmethod
    def operator(nx, ny):
        return [(nx + 1, ny, LANES)] * 2 + [(nx, ny, LANES)] * 6

    @staticmethod
    def fields(nx, ny):
        return [(nx, ny, LANES)] * 3

    @staticmethod
    def iterates(nx, ny):
        return [(nx, ny, LANES)] * 2 + [(nx + 2, ny, LANES)] * 2

    def assemble(self):
        nx, ny, step = self.nx, self.ny, self.step
        shape = (ny, LANES)
        row, spot = iota(shape, 0), iota(shape, 1) % (LANES // 2)
        last_row, top = row == ny - 1, spot >= LANES // 2 - step
        walls = (
            jnp.where(row == 0, 1.0, 0.0)
            + jnp.where(last_row, 1.0, 0.0)
            + jnp.where(spot < step, 1.0, 0.0)
            + jnp.where(top, 1.0, 0.0)
        )
        zero = jnp.zeros(shape, jnp.float32)
        half = 0.5 * self.factor
        for ref in (self.xp, self.xm):
            ref[0], ref[nx] = zero, zero

        def x_face(i, _):
            k = half * (self.eps[i - 1] + self.eps[i])
            delta = self.pot[i] - self.pot[i - 1]
            kb = k * bernoulli(delta)
            self.xp[i], self.xm[i] = kb, kb + k * delta
            return 0

        loop(1, nx, x_face, 0)

        def plane(i, _):
            eps, pot = self.eps[i], self.pot[i]
            k = jnp.where(last_row, 0.0, half * (eps + up(eps, 1, 0)))
            delta = up(pot, 1, 0) - pot
            yp = k * bernoulli(delta)
            ym = yp + k * delta
            k = jnp.where(top, 0.0, half * (eps + up(eps, step, 1)))
            delta = up(pot, step, 1) - pot
            zp = k * bernoulli(delta)
            zm = zp + k * delta
            outer = walls + jnp.where(i == 0, 1.0, 0.0) + jnp.where(i == nx - 1, 1.0, 0.0)
            d = (self.xm[i + 1] + self.xp[i]) + (ym + down(yp, 1, 0)) + (zm + down(zp, step, 1))
            d = d + outer * (half * eps * bernoulli(pot)) + self.cap[i]
            w = OMEGA / d
            self.yp[i], self.ym[i], self.zp[i], self.zm[i] = yp, ym, zp, zm
            self.d[i], self.w[i] = d, w
            return 0

        loop(0, nx, plane, 0)

    def coupled(self, u, i):
        v = u[i + 1]
        s = self.xp[i + 1] * u[i + 2] + self.xm[i] * u[i]
        s = s + (self.yp[i] * up(v, 1, 0) + down(self.ym[i] * v, 1, 0))
        return s + (self.zp[i] * up(v, self.step, 1) + down(self.zm[i] * v, self.step, 1))

    def start(self):
        zero = jnp.zeros((self.ny, LANES), jnp.float32)
        for ref in (self.u, self.v):
            ref[0], ref[self.nx + 1] = zero, zero

        def body(i, _):
            wf = self.w[i] * self.f[i]
            self.wf[i] = wf
            self.u[i + 1] = wf
            return 0

        loop(0, self.nx, body, 0)

    def sweep(self, u, v):
        def body(i, _):
            v[i + 1] = (1.0 - OMEGA) * u[i + 1] + self.wf[i] + self.w[i] * self.coupled(u, i)
            return 0

        loop(0, self.nx, body, 0)

    def halve(self, tmp, v):
        step, ny = self.step, self.ny
        tmp[0:ny] = v
        v = tmp[pl.ds(0, ny // 2, stride=2), :] + tmp[pl.ds(1, ny // 2, stride=2), :]
        other = jnp.where(low_lane(v.shape, step), up(v, step, 1), down(v, step, 1))
        return 0.125 * (v + other)

    def descend_fields(self, coarser, tmp):
        def body(i, _):
            for here, there in ((self.eps, coarser.eps), (self.pot, coarser.pot), (self.cap, coarser.cap)):
                there[i] = self.halve(tmp, here[2 * i] + here[2 * i + 1])
            return 0

        loop(0, coarser.nx, body, 0)

    def descend_residual(self, u, coarser, tmp):
        def residual(i):
            return self.f[i] - self.d[i] * u[i + 1] + self.coupled(u, i)

        def body(i, _):
            coarser.f[i] = self.halve(tmp, residual(2 * i) + residual(2 * i + 1))
            return 0

        loop(0, coarser.nx, body, 0)

    def correct(self, u, coarser_u, tmp):
        half_ny = self.ny // 2

        def body(i, _):
            e = coarser_u(i)
            tmp[pl.ds(0, half_ny, stride=2), :] = e
            tmp[pl.ds(1, half_ny, stride=2), :] = e
            wide = tmp[0 : self.ny]
            u[2 * i + 1] = u[2 * i + 1] + wide
            u[2 * i + 2] = u[2 * i + 2] + wide
            return 0

        loop(0, self.nx // 2, body, 0)


def coarsest(lv):
    nx, step = lv.nx, lv.step
    cxp = [lv.w[i] * lv.xp[i + 1] for i in range(nx)]
    cxm = [lv.w[i] * lv.xm[i] for i in range(nx)]
    cyp = [lv.w[i] * lv.yp[i] for i in range(nx)]
    cym = [lv.w[i] * down(lv.ym[i], 1, 0) for i in range(nx)]
    czp = [lv.w[i] * lv.zp[i] for i in range(nx)]
    czm = [lv.w[i] * down(lv.zm[i], step, 1) for i in range(nx)]
    wf = [lv.w[i] * lv.f[i] for i in range(nx)]

    def body(_, u):
        new = []
        for i in range(nx):
            s = czp[i] * up(u[i], step, 1) + czm[i] * down(u[i], step, 1)
            t = cyp[i] * up(u[i], 1, 0) + cym[i] * down(u[i], 1, 0)
            r = (1.0 - OMEGA) * u[i] + wf[i]
            if i + 1 < nx:
                r = r + cxp[i] * u[i + 1]
            if i > 0:
                r = r + cxm[i] * u[i - 1]
            new.append(r + t + s)
        return tuple(new)

    u = tuple(wf)
    for _ in range(COARSE_ITERS - 1):
        u = body(0, u)
    for i in range(nx):
        lv.u[i + 1] = u[i]


def place(bits, ref, flip, x, y, ny, put):
    bx, by = ref.shape[-3], ref.shape[-2]

    def body(m, _):
        b = m // ny
        to_x = x ^ flip
        for k, bit in enumerate(bits[:-1]):
            to_x = to_x ^ (((b >> k) & 1) * bit)
        row = pl.ds(pl.multiple_of((y ^ (m % ny)) * by, by), by)
        for i in range(bx):
            put(m, i, to_x * bx + i, row)
        return 0

    loop(0, ref.shape[0], body, 0)


def operators_kernel(bits, near, far, *refs):
    x, y, ny = lax.axis_index("gx"), lax.axis_index("gy"), lax.axis_size("gy")
    outs, scratch = refs[: 3 * OPERATOR], refs[3 * OPERATOR :]
    l1, l2, l3 = (
        Level(k + 1, outs[OPERATOR * k : OPERATOR * (k + 1)] + scratch[3 * k : 3 * k + 3]) for k in range(3)
    )
    tmp = scratch[9]
    right = iota((near.shape[-2], LANES), 1) >= LANES // 2
    for ref, flip in ((near, 0), (far, bits[-1])):

        def put(m, i, at, row, ref=ref):
            q = ref[m, 1, i]
            l1.eps[at, row, :] = ref[m, 0, i]
            l1.pot[at, row, :] = jnp.where(right, q, 0.0)
            l1.cap[at, row, :] = jnp.where(right, down(q, LANES // 2, 1), 0.0)

        place(bits, ref, flip, x, y, ny, put)
    l1.assemble()
    l1.descend_fields(l2, tmp)
    l2.assemble()
    l2.descend_fields(l3, tmp)
    l3.assemble()


def second_kernel(bits, near, far, kept, *refs):
    x, y, ny = lax.axis_index("gx"), lax.axis_index("gy"), lax.axis_size("gy")
    given, (out_p, out_n), scratch = refs[: 3 * OPERATOR], refs[3 * OPERATOR : 3 * OPERATOR + 2], refs[3 * OPERATOR + 2 :]
    l1, l2, l3 = (
        Level(k + 1, given[OPERATOR * k : OPERATOR * (k + 1)] + scratch[4 * k : 4 * k + 4]) for k in range(3)
    )
    sol, tmp, fine_a, fine_b = scratch[12:]
    bx, by = near.shape[-3], near.shape[-2]
    for ref, flip in ((near, 0), (far, bits[-1])):

        def put(m, i, at, row, ref=ref):
            l1.f[at, row, :] = ref[m, i]

        place(bits, ref, flip, x, y, ny, put)
    for here, there in ((l1, l2), (l2, l3)):
        here.start()
        here.sweep(here.u, here.v)
        here.descend_residual(here.v, there, tmp)
    coarsest(l3)
    l2.correct(l2.v, lambda i: l3.u[i + 1], tmp)
    l2.sweep(l2.v, l2.u)
    l2.sweep(l2.u, l2.v)
    l1.correct(l1.v, lambda i: l2.v[i + 1], tmp)
    l1.sweep(l1.v, l1.u)
    edge = jnp.zeros((by, LANES), jnp.float32)
    n1x, n1y = l1.nx, l1.ny
    blank = jnp.zeros((n1y + 2 * by, LANES), jnp.float32)
    sol[0], sol[n1x + 1] = blank, blank

    def last(i, _):
        sol[i + 1, 0:by] = edge
        sol[i + 1, by + n1y :] = edge
        sol[i + 1, by : by + n1y] = (
            (1.0 - OMEGA) * l1.u[i + 1] + l1.wf[i] + l1.w[i] * l1.coupled(l1.u, i)
        )
        return 0

    loop(0, n1x, last, 0)

    rows = kept.shape[2]
    own = rows - 2 * RIM
    tile_row = iota((by, LANES), 0)
    spread = iota((by, LANES), 1) // 2

    def widen(v, channel):
        return jnp.take_along_axis(v, spread + channel * (LANES // 2), axis=1)

    def correct(i, _):
        at = x * bx + i
        middle, above, below = (
            sol[at, pl.ds(pl.multiple_of((y + k) * by, by), by), :] for k in (1, 2, 0)
        )
        rim = jnp.where(
            tile_row < 2,
            jnp.broadcast_to(above[0:1], (by, LANES)),
            jnp.where(tile_row >= by - 2, jnp.broadcast_to(below[by - 1 : by], (by, LANES)), 0.0),
        )
        for channel, u in ((0, U_P), (1, U_N)):
            e = widen(middle, channel)
            tmp[pl.ds(0, by, stride=2), :] = e
            tmp[pl.ds(1, by, stride=2), :] = e
            tmp[own:rows] = widen(rim, channel)
            e = tmp[0:rows]
            for k in (0, 1):
                p = RIM - 2 + 2 * i + k
                fine_a[channel, p] = kept[u, p] + e
        return 0

    loop(0, bx + 2, correct, 0)

    def fine(u, channel, i):
        w, wf = ((W_P, WF_P), (W_N, WF_N))[channel]
        s = coupled_fine(kept, lambda j: u[channel, j], i, channel == 0)
        return (1.0 - OMEGA) * u[channel, i] + kept[wf, i] + kept[w, i] * s

    def post_one(i, _):
        for channel in (0, 1):
            fine_b[channel, i] = fine(fine_a, channel, i)
        return 0

    def post_two(i, _):
        out_p[i] = fine(fine_b, 0, i + RIM)[0:own]
        out_n[i] = fine(fine_b, 1, i + RIM)[0:own]
        return 0

    loop(RIM - 1, RIM + 2 * bx + 1, post_one, 0)
    loop(0, 2 * bx, post_two, 0)


def moves(ng, nx, ny):
    def of(partner):
        place = {p: k for k, p in enumerate(itertools.product(range(ng), range(nx), range(ny)))}
        return [(k, place[partner(*p)]) for p, k in place.items()]

    def other(k):
        return k + 1 if k % 2 else k - 1

    return {
        "xa": of(lambda g, a, b: (g, a ^ 1, b)),
        "xb": of(lambda g, a, b: (g, other(a), b) if 0 < a < nx - 1 else (g ^ 1, a, b)),
        "ya": of(lambda g, a, b: (g, a, b ^ 1)),
        "yb": of(lambda g, a, b: (g, a, other(b)) if 0 < b < ny - 1 else (g, a ^ 1, b)),
        **{("x", 1 << k): of(lambda g, a, b, k=k: (g, a ^ (1 << k), b)) for k in range((nx - 1).bit_length())},
        **{("y", 1 << k): of(lambda g, a, b, k=k: (g, a, b ^ (1 << k))) for k in range((ny - 1).bit_length())},
    }


def per_device(ng, nx, ny, layer_class, permittivity, mobility, capture, potential, rhs_psi, rhs_n):
    send = moves(ng, nx, ny)
    f32 = jnp.float32

    def permute(v, name):
        return lax.ppermute(v, ("groups", "gx", "gy"), send[name])

    planes, own = layer_class.shape[0], layer_class.shape[1]
    rows, total = own + 2 * RIM, planes + 2 * RIM
    bx, by = planes // 2, own // 2
    def shape(*dims):
        return jax.ShapeDtypeStruct(dims, f32)

    table = jnp.stack([permittivity, mobility, capture])
    table = jnp.broadcast_to(table[:, :, None], (*table.shape, LANES))
    cell = (planes, own, LANES)
    a, b, fields, *raw = pl.pallas_call(
        rim_y_kernel,
        out_shape=[
            shape(2 * planes, by, LANES),
            shape(2 * planes, by, LANES),
            shape(1, 2, bx, by, LANES),
        ]
        + [shape(*cell)] * 4,
        in_specs=[VMEM] + [HBM] * 4,
        out_specs=[VMEM] * 7,
        scratch_shapes=[
            pltpu.VMEM(cell, jnp.int32),
            pltpu.VMEM((4, bx, own, LANES), f32),
            pltpu.SemaphoreType.DMA((4,)),
        ],
        compiler_params=params(53.5),
    )(table, layer_class, potential, rhs_psi, rhs_n)
    b = permute(b, "yb")
    a = permute(jnp.concatenate([a, fields.reshape(-1, by, LANES)]), "ya")
    fields_y = [fields, a[2 * planes :].reshape(fields.shape)]
    mid, a, b = pl.pallas_call(
        rim_x_kernel,
        out_shape=[shape(4, planes, rows, LANES)] + [shape(4, RIM, rows, LANES)] * 2,
        in_specs=[VMEM] * 6,
        out_specs=[VMEM] * 3,
        compiler_params=params(16),
    )(*raw, a, b)
    fields_y, _ = lax.optimization_barrier((jnp.concatenate(fields_y), mid))
    b = permute(b, "xb")
    a = permute(a, "xa")
    kept, block = pl.pallas_call(
        first_kernel,
        out_shape=[shape(KEPT, total, rows, LANES), shape(1, bx, by, LANES)],
        in_specs=[VMEM] * 4,
        out_specs=[VMEM] * 2,
        scratch_shapes=[
            pltpu.VMEM((8, total, rows, LANES), f32),
            pltpu.VMEM((2, bx, own, LANES), f32),
        ],
        compiler_params=params(24),
    )(table, mid, a, b)

    bits = [1 << k for k in reversed(range((nx - 1).bit_length()))]

    def over_y(near, first):
        bit = first
        while bit < ny:
            near = jnp.concatenate([near, permute(near, ("y", bit))])
            bit *= 2
        return near

    def over_x(near):
        for bit in bits[:-1]:
            near = jnp.concatenate([near, permute(near, ("x", bit))], axis=0)
        return near, permute(near, ("x", bits[-1]))

    halves = [fields_y, permute(fields_y, ("y", 2))]
    pair = jnp.concatenate([block, permute(block, ("y", 1))])
    halves, _ = lax.optimization_barrier((halves, pair))
    fields_y = over_y(jnp.concatenate(halves), 4)
    grids = [(bx * nx >> level, by * ny >> level) for level in range(3)]
    large = grids[0][0] * grids[0][1] > 1024
    operators = pl.pallas_call(
        functools.partial(operators_kernel, tuple(bits)),
        out_shape=[shape(*s) for g in grids for s in Level.operator(*g)],
        in_specs=[VMEM] * 2,
        out_specs=[VMEM] * (3 * OPERATOR),
        scratch_shapes=[pltpu.VMEM(s, f32) for g in grids for s in Level.fields(*g)]
        + [pltpu.VMEM((grids[0][1], LANES), f32)],
        compiler_params=params(60 if large else 16),
    )(*over_x(fields_y))
    near, far = over_x(over_y(pair, 2))
    return pl.pallas_call(
        functools.partial(second_kernel, tuple(bits)),
        out_shape=[shape(planes, own, LANES)] * 2,
        in_specs=[VMEM] * (3 + 3 * OPERATOR),
        out_specs=[VMEM] * 2,
        scratch_shapes=[pltpu.VMEM(s, f32) for g in grids for s in Level.iterates(*g)]
        + [
            pltpu.VMEM((grids[0][0] + 2, grids[0][1] + 2 * by, LANES), f32),
            pltpu.VMEM((max(grids[0][1], rows), LANES), f32),
            pltpu.VMEM((2, total, rows, LANES), f32),
            pltpu.VMEM((2, total, rows, LANES), f32),
        ],
        compiler_params=params(60 if large else 16),
    )(near, far, kept, *operators)


def solution(mesh):
    grid = P(("groups", "gx"), "gy", None)
    fn = functools.partial(per_device, *(mesh.shape[a] for a in ("groups", "gx", "gy")))
    return jax.shard_map(
        fn,
        mesh=mesh,
        in_specs=(grid, P(), P(), P(), grid, grid, grid),
        out_specs=(grid, grid),
        check_vma=False,
    )
```

```python
import functools
import itertools
import jax
import jax.numpy as jnp
from jax import lax
from jax.experimental import pallas as pl
from jax.experimental.pallas import tpu as pltpu
from jax.sharding import PartitionSpec as P

OMEGA = 0.8
COARSE_ITERS = 20
RIM = 4
LANES = 128
RIM_PLANES = ((0, RIM), (RIM, RIM), (2 * RIM, RIM - 1), (3 * RIM - 1, RIM - 1))
VMEM = pl.BlockSpec(memory_space=pltpu.VMEM)
HBM = pl.BlockSpec(memory_space=pltpu.HBM)


UNROLL = 16


def loop(first, end, body, init):
    if end - first > UNROLL:
        return lax.fori_loop(first, end, body, init)
    for i in range(first, end):
        body(i, 0)
    return init


def params(mib):
    return pltpu.CompilerParams(vmem_limit_bytes=int(mib * 1024 * 1024))


def bernoulli(x):
    t = x * x
    series = (1.0 - 0.5 * x) + t * (1 / 12 - t * (1 / 720))
    near = t < 0.0625
    guarded = jnp.where(near, 1.0, x)
    return jnp.where(near, series, guarded / (jnp.exp(guarded) - 1.0))


def iota(shape, dim):
    return lax.broadcasted_iota(jnp.int32, shape, dim)


def up(v, step, dim):
    return pltpu.roll(v, v.shape[dim] - step, dim)


def down(v, step, dim):
    return pltpu.roll(v, step, dim)


def halve_lanes(a, b):
    lane = iota(a.shape, 1)
    at = (2 * lane) % LANES
    a = jnp.take_along_axis(a + up(a, 1, 1), at, axis=1)
    b = jnp.take_along_axis(b + up(b, 1, 1), at, axis=1)
    return jnp.where(lane < LANES // 2, a, b)


def look_up(table, c, shape):
    found = [jnp.zeros(shape, jnp.float32)] * 3
    for k in range(table.shape[1]):
        same = c == float(k)
        found = [
            jnp.where(same, jnp.broadcast_to(table[f, k : k + 1], shape), found[f]) for f in range(3)
        ]
    return found


def rim_y_kernel(table, c_in, p_in, fp_in, fn_in, out_a, out_b, block, c_out, p_out, fp_out, fn_out, cls, work, sems):
    outs = (c_out, p_out, fp_out, fn_out)
    copies = [
        pltpu.make_async_copy(s, d, sems.at[k])
        for k, (s, d) in enumerate(zip((c_in, p_in, fp_in, fn_in), (cls, *outs[1:])))
    ]
    for c in copies:
        c.start()
    for c in copies:
        c.wait()
    c_out[...] = cls[...].astype(jnp.float32)
    even = lax.axis_index("gy") % 2 == 0
    planes, length = cls.shape[0], cls.shape[1]
    for pair in range(2):
        lo, hi = (
            jnp.concatenate([r[:, at : at + RIM, :] for r in outs[2 * pair : 2 * pair + 2]], axis=1)
            for at in (0, length - RIM)
        )
        out_a[pair * planes : (pair + 1) * planes] = jnp.where(even, hi, lo)
        out_b[pair * planes : (pair + 1) * planes] = jnp.where(even, lo, hi)
    bx = planes // 2
    for i in range(bx):
        one, two = (look_up(table, c_out[2 * i + k], (length, LANES)) for k in (0, 1))
        values = [p + q for p, q in zip(one, two)] + [p_out[2 * i] + p_out[2 * i + 1]]
        for k, v in enumerate(values):
            work[k, i] = v
    for i in range(bx):
        eps, mob, cap, pot = (
            work[k, i, pl.ds(0, length // 2, stride=2), :] + work[k, i, pl.ds(1, length // 2, stride=2), :]
            for k in range(4)
        )
        for f, v in enumerate((halve_lanes(eps, mob), halve_lanes(cap, pot))):
            block[0, f, i] = 0.125 * v


def rim_x_kernel(cls, pot, fp, fn, in_a, in_b, out, out_a, out_b):
    y, ny = lax.axis_index("gy"), lax.axis_size("gy")
    even_x, even_y = lax.axis_index("gx") % 2 == 0, y % 2 == 0
    planes, length = cls.shape[0], cls.shape[1]
    row = iota((planes, 2 * RIM, LANES), 1)
    for pair in range(2):
        a, b = (r[pair * planes : (pair + 1) * planes] for r in (in_a, in_b))
        hi, lo = jnp.where(even_y, a, b), jnp.where(even_y, b, a)
        for slot in range(2):
            field = 2 * pair + slot
            outside = -1.0 if field == 0 else 0.0
            h, l = jnp.where(y == ny - 1, outside, hi), jnp.where(y == 0, outside, lo)
            if slot == 0:
                l = down(l, RIM, 1)
            else:
                h = down(h, RIM, 1)
            out[field, :, 0:length, :] = (cls, pot, fp, fn)[field][...]
            out[field, :, length : length + 2 * RIM, :] = jnp.where(row < RIM, h, l)
        for slot in range(2):
            field = 2 * pair + slot
            at, n = RIM_PLANES[field]
            lo_x, hi_x = out[field, 0:n], out[field, planes - n : planes]
            out_a[at : at + n] = jnp.where(even_x, hi_x, lo_x)
            out_b[at : at + n] = jnp.where(even_x, lo_x, hi_x)


W_P, GX, GY, GZ, W_N, XP, XM, YP, YM, ZP, ZM, WF_P, WF_N, U_P, U_N = range(15)
KEPT = 15


def coupled_fine(kept, u, i, poisson):
    v = u(i)
    if poisson:
        xp, xm, yp, ym, zp, zm = GX, GX, GY, GY, GZ, GZ
    else:
        xp, xm, yp, ym, zp, zm = XP, XM, YP, YM, ZP, ZM
    s = kept[xp, i] * u(i + 1) + kept[xm, i - 1] * u(i - 1)
    s = s + (kept[yp, i] * up(v, 1, 0) + down(kept[ym, i] * v, 1, 0))
    return s + (kept[zp, i] * up(v, 1, 1) + down(kept[zm, i] * v, 1, 1))


def first_kernel(table, mid, in_a, in_b, kept, block, fld, work):
    x, nx = lax.axis_index("gx"), lax.axis_size("gx")
    even = x % 2 == 0
    planes = mid.shape[1]
    rows = mid.shape[2]
    own = rows - 2 * RIM
    total = planes + 2 * RIM
    EPS, MOB, POT, CAP, F_P, F_N, D_P, D_N = range(8)

    def materials(i, c, pot, fp, fn):
        eps, mob, cap = look_up(table, c, (rows, LANES))
        fld[EPS, i], fld[MOB, i], fld[POT, i], fld[CAP, i] = eps, mob, pot, cap
        fld[F_P, i], fld[F_N, i] = fp, fn

    def rim(i, ref_even, ref_odd, skip, outside):
        values = []
        for f, (at, n) in enumerate(RIM_PLANES):
            if n < RIM and i == skip:
                values.append(jnp.zeros((rows, LANES), jnp.float32))
                continue
            k = at + i - (1 if n < RIM and skip == 0 else 0)
            v = jnp.where(even, ref_even[k], ref_odd[k])
            values.append(jnp.where(outside, -1.0 if f == 0 else 0.0, v))
        return values

    def low(i, _):
        materials(i, *rim(i, in_b, in_a, 0, x == 0))
        return 0

    def middle(i, _):
        materials(i + RIM, *[mid[f, i] for f in range(4)])
        return 0

    def high(i, _):
        materials(i + RIM + planes, *rim(i, in_a, in_b, RIM - 1, x == nx - 1))
        return 0

    loop(0, RIM, low, 0)
    loop(0, planes, middle, 0)
    loop(0, RIM, high, 0)

    shape = (rows, LANES)
    lane = iota(shape, 1)
    ends = (lane == 0) | (lane == LANES - 1)
    top = lane == LANES - 1

    def x_faces(i):
        eps, mob, pot = fld[EPS, i], fld[MOB, i], fld[POT, i]
        kept[GX, i] = 0.5 * (eps + fld[EPS, i + 1])
        k = 0.5 * (mob + fld[MOB, i + 1])
        delta = fld[POT, i + 1] - pot
        kb = k * bernoulli(delta)
        kept[XP, i] = kb
        kept[XM, i] = kb + k * delta

    x_faces(0)

    def operators(i, _):
        x_faces(i)
        eps, mob, pot = fld[EPS, i], fld[MOB, i], fld[POT, i]
        gy = 0.5 * (eps + up(eps, 1, 0))
        k = 0.5 * (mob + up(mob, 1, 0))
        delta = up(pot, 1, 0) - pot
        yp = k * bernoulli(delta)
        ym = yp + k * delta
        gz = jnp.where(top, 0.0, 0.5 * (eps + up(eps, 1, 1)))
        k = jnp.where(top, 0.0, 0.5 * (mob + up(mob, 1, 1)))
        delta = up(pot, 1, 1) - pot
        zp = k * bernoulli(delta)
        zm = zp + k * delta
        kept[GY, i], kept[YP, i], kept[YM, i] = gy, yp, ym
        kept[GZ, i], kept[ZP, i], kept[ZM, i] = gz, zp, zm
        d_p = (kept[GX, i] + kept[GX, i - 1]) + (gy + down(gy, 1, 0)) + (gz + down(gz, 1, 1))
        d_p = d_p + jnp.where(ends, 0.5 * eps, 0.0)
        d_n = (kept[XM, i] + kept[XP, i - 1]) + (ym + down(yp, 1, 0)) + (zm + down(zp, 1, 1))
        d_n = d_n + jnp.where(ends, 0.5 * mob * bernoulli(pot), 0.0) + fld[CAP, i]
        inside = eps > 0.0
        w_p = jnp.where(inside, OMEGA / jnp.where(inside, d_p, 1.0), 0.0)
        w_n = jnp.where(inside, OMEGA / jnp.where(inside, d_n, 1.0), 0.0)
        kept[W_P, i], kept[W_N, i] = w_p, w_n
        kept[WF_P, i], kept[WF_N, i] = w_p * fld[F_P, i], w_n * fld[F_N, i]
        fld[D_P, i], fld[D_N, i] = d_p, d_n
        return 0

    loop(1, total - 1, operators, 0)

    def sweep(i, _):
        for poisson, w, wf, u in ((True, W_P, WF_P, U_P), (False, W_N, WF_N, U_N)):
            s = coupled_fine(kept, lambda j: kept[wf, j], i, poisson)
            kept[u, i] = (2.0 - OMEGA) * kept[wf, i] + kept[w, i] * s
        return 0

    loop(2, total - 2, sweep, 0)

    def residual(i, poisson, f, d, u):
        s = coupled_fine(kept, lambda j: kept[u, j], i, poisson)
        return fld[f, i] - fld[d, i] * kept[u, i] + s

    def coarse(i, _):
        at = RIM + 2 * i
        r_p = residual(at, True, F_P, D_P, U_P) + residual(at + 1, True, F_P, D_P, U_P)
        r_n = residual(at, False, F_N, D_N, U_N) + residual(at + 1, False, F_N, D_N, U_N)
        work[0, i], work[1, i] = r_p[0:own], r_n[0:own]
        r_p, r_n = (
            work[k, i, pl.ds(0, own // 2, stride=2), :] + work[k, i, pl.ds(1, own // 2, stride=2), :]
            for k in range(2)
        )
        block[0, i] = 0.125 * halve_lanes(r_p, r_n)
        return 0

    loop(0, planes // 2, coarse, 0)


def low_lane(shape, bit):
    return (iota(shape, 1) & bit) == 0


OPERATOR = 8


class Level:
    def __init__(self, level, refs):
        self.level, self.step, self.factor = level, 1 << (level - 1), 0.25**level
        (self.xp, self.xm, self.yp, self.ym, self.zp, self.zm, self.w, self.d) = refs[:OPERATOR]
        if len(refs) == OPERATOR + 3:
            self.eps, self.pot, self.cap = refs[OPERATOR:]
        else:
            self.f, self.wf, self.u, self.v = refs[OPERATOR:]
        self.nx, self.ny = self.w.shape[0], self.w.shape[1]

    @staticmethod
    def operator(nx, ny):
        return [(nx + 1, ny, LANES)] * 2 + [(nx, ny, LANES)] * 6

    @staticmethod
    def fields(nx, ny):
        return [(nx, ny, LANES)] * 3

    @staticmethod
    def iterates(nx, ny):
        return [(nx, ny, LANES)] * 2 + [(nx + 2, ny, LANES)] * 2

    def assemble(self):
        nx, ny, step = self.nx, self.ny, self.step
        shape = (ny, LANES)
        row, spot = iota(shape, 0), iota(shape, 1) % (LANES // 2)
        last_row, top = row == ny - 1, spot >= LANES // 2 - step
        walls = (
            jnp.where(row == 0, 1.0, 0.0)
            + jnp.where(last_row, 1.0, 0.0)
            + jnp.where(spot < step, 1.0, 0.0)
            + jnp.where(top, 1.0, 0.0)
        )
        zero = jnp.zeros(shape, jnp.float32)
        half = 0.5 * self.factor
        for ref in (self.xp, self.xm):
            ref[0], ref[nx] = zero, zero

        def x_face(i, _):
            k = half * (self.eps[i - 1] + self.eps[i])
            delta = self.pot[i] - self.pot[i - 1]
            kb = k * bernoulli(delta)
            self.xp[i], self.xm[i] = kb, kb + k * delta
            return 0

        loop(1, nx, x_face, 0)

        def plane(i, _):
            eps, pot = self.eps[i], self.pot[i]
            k = jnp.where(last_row, 0.0, half * (eps + up(eps, 1, 0)))
            delta = up(pot, 1, 0) - pot
            yp = k * bernoulli(delta)
            ym = yp + k * delta
            k = jnp.where(top, 0.0, half * (eps + up(eps, step, 1)))
            delta = up(pot, step, 1) - pot
            zp = k * bernoulli(delta)
            zm = zp + k * delta
            outer = walls + jnp.where(i == 0, 1.0, 0.0) + jnp.where(i == nx - 1, 1.0, 0.0)
            d = (self.xm[i + 1] + self.xp[i]) + (ym + down(yp, 1, 0)) + (zm + down(zp, step, 1))
            d = d + outer * (half * eps * bernoulli(pot)) + self.cap[i]
            w = OMEGA / d
            self.yp[i], self.ym[i], self.zp[i], self.zm[i] = yp, ym, zp, zm
            self.d[i], self.w[i] = d, w
            return 0

        loop(0, nx, plane, 0)

    def coupled(self, u, i):
        v = u[i + 1]
        s = self.xp[i + 1] * u[i + 2] + self.xm[i] * u[i]
        s = s + (self.yp[i] * up(v, 1, 0) + down(self.ym[i] * v, 1, 0))
        return s + (self.zp[i] * up(v, self.step, 1) + down(self.zm[i] * v, self.step, 1))

    def start(self):
        zero = jnp.zeros((self.ny, LANES), jnp.float32)
        for ref in (self.u, self.v):
            ref[0], ref[self.nx + 1] = zero, zero

        def body(i, _):
            wf = self.w[i] * self.f[i]
            self.wf[i] = wf
            self.u[i + 1] = wf
            return 0

        loop(0, self.nx, body, 0)

    def sweep(self, u, v):
        def body(i, _):
            v[i + 1] = (1.0 - OMEGA) * u[i + 1] + self.wf[i] + self.w[i] * self.coupled(u, i)
            return 0

        loop(0, self.nx, body, 0)

    def halve(self, tmp, v):
        step, ny = self.step, self.ny
        tmp[0:ny] = v
        v = tmp[pl.ds(0, ny // 2, stride=2), :] + tmp[pl.ds(1, ny // 2, stride=2), :]
        other = jnp.where(low_lane(v.shape, step), up(v, step, 1), down(v, step, 1))
        return 0.125 * (v + other)

    def descend_fields(self, coarser, tmp):
        def body(i, _):
            for here, there in ((self.eps, coarser.eps), (self.pot, coarser.pot), (self.cap, coarser.cap)):
                there[i] = self.halve(tmp, here[2 * i] + here[2 * i + 1])
            return 0

        loop(0, coarser.nx, body, 0)

    def descend_residual(self, u, coarser, tmp):
        def residual(i):
            return self.f[i] - self.d[i] * u[i + 1] + self.coupled(u, i)

        def body(i, _):
            coarser.f[i] = self.halve(tmp, residual(2 * i) + residual(2 * i + 1))
            return 0

        loop(0, coarser.nx, body, 0)

    def correct(self, u, coarser_u, tmp):
        half_ny = self.ny // 2

        def body(i, _):
            e = coarser_u(i)
            tmp[pl.ds(0, half_ny, stride=2), :] = e
            tmp[pl.ds(1, half_ny, stride=2), :] = e
            wide = tmp[0 : self.ny]
            u[2 * i + 1] = u[2 * i + 1] + wide
            u[2 * i + 2] = u[2 * i + 2] + wide
            return 0

        loop(0, self.nx // 2, body, 0)


def coarsest(lv):
    nx, step = lv.nx, lv.step
    cxp = [lv.w[i] * lv.xp[i + 1] for i in range(nx)]
    cxm = [lv.w[i] * lv.xm[i] for i in range(nx)]
    cyp = [lv.w[i] * lv.yp[i] for i in range(nx)]
    cym = [lv.w[i] * down(lv.ym[i], 1, 0) for i in range(nx)]
    czp = [lv.w[i] * lv.zp[i] for i in range(nx)]
    czm = [lv.w[i] * down(lv.zm[i], step, 1) for i in range(nx)]
    wf = [lv.w[i] * lv.f[i] for i in range(nx)]

    def body(_, u):
        new = []
        for i in range(nx):
            s = czp[i] * up(u[i], step, 1) + czm[i] * down(u[i], step, 1)
            t = cyp[i] * up(u[i], 1, 0) + cym[i] * down(u[i], 1, 0)
            r = (1.0 - OMEGA) * u[i] + wf[i]
            if i + 1 < nx:
                r = r + cxp[i] * u[i + 1]
            if i > 0:
                r = r + cxm[i] * u[i - 1]
            new.append(r + t + s)
        return tuple(new)

    u = tuple(wf)
    for _ in range(COARSE_ITERS - 1):
        u = body(0, u)
    for i in range(nx):
        lv.u[i + 1] = u[i]


def place(bits, ref, flip, x, y, ny, put):
    bx, by = ref.shape[-3], ref.shape[-2]

    def body(m, _):
        b = m // ny
        to_x = x ^ flip
        for k, bit in enumerate(bits[:-1]):
            to_x = to_x ^ (((b >> k) & 1) * bit)
        row = pl.ds(pl.multiple_of((y ^ (m % ny)) * by, by), by)
        for i in range(bx):
            put(m, i, to_x * bx + i, row)
        return 0

    loop(0, ref.shape[0], body, 0)


def operators_kernel(bits, near, far, *refs):
    x, y, ny = lax.axis_index("gx"), lax.axis_index("gy"), lax.axis_size("gy")
    outs, scratch = refs[: 3 * OPERATOR], refs[3 * OPERATOR :]
    l1, l2, l3 = (
        Level(k + 1, outs[OPERATOR * k : OPERATOR * (k + 1)] + scratch[3 * k : 3 * k + 3]) for k in range(3)
    )
    tmp = scratch[9]
    right = iota((near.shape[-2], LANES), 1) >= LANES // 2
    for ref, flip in ((near, 0), (far, bits[-1])):

        def put(m, i, at, row, ref=ref):
            q = ref[m, 1, i]
            l1.eps[at, row, :] = ref[m, 0, i]
            l1.pot[at, row, :] = jnp.where(right, q, 0.0)
            l1.cap[at, row, :] = jnp.where(right, down(q, LANES // 2, 1), 0.0)

        place(bits, ref, flip, x, y, ny, put)
    l1.assemble()
    l1.descend_fields(l2, tmp)
    l2.assemble()
    l2.descend_fields(l3, tmp)
    l3.assemble()


def second_kernel(bits, near, far, kept, *refs):
    x, y, ny = lax.axis_index("gx"), lax.axis_index("gy"), lax.axis_size("gy")
    given, (out_p, out_n), scratch = refs[: 3 * OPERATOR], refs[3 * OPERATOR : 3 * OPERATOR + 2], refs[3 * OPERATOR + 2 :]
    l1, l2, l3 = (
        Level(k + 1, given[OPERATOR * k : OPERATOR * (k + 1)] + scratch[4 * k : 4 * k + 4]) for k in range(3)
    )
    sol, tmp, fine_a, fine_b = scratch[12:]
    bx, by = near.shape[-3], near.shape[-2]
    for ref, flip in ((near, 0), (far, bits[-1])):

        def put(m, i, at, row, ref=ref):
            l1.f[at, row, :] = ref[m, i]

        place(bits, ref, flip, x, y, ny, put)
    for here, there in ((l1, l2), (l2, l3)):
        here.start()
        here.sweep(here.u, here.v)
        here.descend_residual(here.v, there, tmp)
    coarsest(l3)
    l2.correct(l2.v, lambda i: l3.u[i + 1], tmp)
    l2.sweep(l2.v, l2.u)
    l2.sweep(l2.u, l2.v)
    l1.correct(l1.v, lambda i: l2.v[i + 1], tmp)
    l1.sweep(l1.v, l1.u)
    edge = jnp.zeros((by, LANES), jnp.float32)
    n1x, n1y = l1.nx, l1.ny
    blank = jnp.zeros((n1y + 2 * by, LANES), jnp.float32)
    sol[0], sol[n1x + 1] = blank, blank

    def last(i, _):
        sol[i + 1, 0:by] = edge
        sol[i + 1, by + n1y :] = edge
        sol[i + 1, by : by + n1y] = (
            (1.0 - OMEGA) * l1.u[i + 1] + l1.wf[i] + l1.w[i] * l1.coupled(l1.u, i)
        )
        return 0

    loop(0, n1x, last, 0)

    rows = kept.shape[2]
    own = rows - 2 * RIM
    tile_row = iota((by, LANES), 0)
    spread = iota((by, LANES), 1) // 2

    def widen(v, channel):
        return jnp.take_along_axis(v, spread + channel * (LANES // 2), axis=1)

    def correct(i, _):
        at = x * bx + i
        middle, above, below = (
            sol[at, pl.ds(pl.multiple_of((y + k) * by, by), by), :] for k in (1, 2, 0)
        )
        rim = jnp.where(
            tile_row < 2,
            jnp.broadcast_to(above[0:1], (by, LANES)),
            jnp.where(tile_row >= by - 2, jnp.broadcast_to(below[by - 1 : by], (by, LANES)), 0.0),
        )
        for channel, u in ((0, U_P), (1, U_N)):
            e = widen(middle, channel)
            tmp[pl.ds(0, by, stride=2), :] = e
            tmp[pl.ds(1, by, stride=2), :] = e
            tmp[own:rows] = widen(rim, channel)
            e = tmp[0:rows]
            for k in (0, 1):
                p = RIM - 2 + 2 * i + k
                fine_a[channel, p] = kept[u, p] + e
        return 0

    loop(0, bx + 2, correct, 0)

    def fine(u, channel, i):
        w, wf = ((W_P, WF_P), (W_N, WF_N))[channel]
        s = coupled_fine(kept, lambda j: u[channel, j], i, channel == 0)
        return (1.0 - OMEGA) * u[channel, i] + kept[wf, i] + kept[w, i] * s

    def post_one(i, _):
        for channel in (0, 1):
            fine_b[channel, i] = fine(fine_a, channel, i)
        return 0

    def post_two(i, _):
        out_p[i] = fine(fine_b, 0, i + RIM)[0:own]
        out_n[i] = fine(fine_b, 1, i + RIM)[0:own]
        return 0

    loop(RIM - 1, RIM + 2 * bx + 1, post_one, 0)
    loop(0, 2 * bx, post_two, 0)


def moves(ng, nx, ny):
    def of(partner):
        place = {p: k for k, p in enumerate(itertools.product(range(ng), range(nx), range(ny)))}
        return [(k, place[partner(*p)]) for p, k in place.items()]

    def other(k):
        return k + 1 if k % 2 else k - 1

    return {
        "xa": of(lambda g, a, b: (g, a ^ 1, b)),
        "xb": of(lambda g, a, b: (g, other(a), b) if 0 < a < nx - 1 else (g ^ 1, a, b)),
        "ya": of(lambda g, a, b: (g, a, b ^ 1)),
        "yb": of(lambda g, a, b: (g, a, other(b)) if 0 < b < ny - 1 else (g, a ^ 1, b)),
        **{("x", 1 << k): of(lambda g, a, b, k=k: (g, a ^ (1 << k), b)) for k in range((nx - 1).bit_length())},
        **{("y", 1 << k): of(lambda g, a, b, k=k: (g, a, b ^ (1 << k))) for k in range((ny - 1).bit_length())},
    }


def per_device(ng, nx, ny, layer_class, permittivity, mobility, capture, potential, rhs_psi, rhs_n):
    send = moves(ng, nx, ny)
    f32 = jnp.float32

    def permute(v, name):
        return lax.ppermute(v, ("groups", "gx", "gy"), send[name])

    planes, own = layer_class.shape[0], layer_class.shape[1]
    rows, total = own + 2 * RIM, planes + 2 * RIM
    bx, by = planes // 2, own // 2
    def shape(*dims):
        return jax.ShapeDtypeStruct(dims, f32)

    table = jnp.stack([permittivity, mobility, capture])
    table = jnp.broadcast_to(table[:, :, None], (*table.shape, LANES))
    cell = (planes, own, LANES)
    a, b, fields, *raw = pl.pallas_call(
        rim_y_kernel,
        out_shape=[
            shape(2 * planes, by, LANES),
            shape(2 * planes, by, LANES),
            shape(1, 2, bx, by, LANES),
        ]
        + [shape(*cell)] * 4,
        in_specs=[VMEM] + [HBM] * 4,
        out_specs=[VMEM] * 7,
        scratch_shapes=[
            pltpu.VMEM(cell, jnp.int32),
            pltpu.VMEM((4, bx, own, LANES), f32),
            pltpu.SemaphoreType.DMA((4,)),
        ],
        compiler_params=params(53.5),
    )(table, layer_class, potential, rhs_psi, rhs_n)
    b = permute(b, "yb")
    a = permute(jnp.concatenate([a, fields.reshape(-1, by, LANES)]), "ya")
    fields_y = [fields, a[2 * planes :].reshape(fields.shape)]
    mid, a, b = pl.pallas_call(
        rim_x_kernel,
        out_shape=[shape(4, planes, rows, LANES)] + [shape(4 * RIM - 2, rows, LANES)] * 2,
        in_specs=[VMEM] * 6,
        out_specs=[VMEM] * 3,
        compiler_params=params(16),
    )(*raw, a, b)
    fields_y, _ = lax.optimization_barrier((jnp.concatenate(fields_y), mid))
    b = permute(b, "xb")
    a = permute(a, "xa")
    kept, block = pl.pallas_call(
        first_kernel,
        out_shape=[shape(KEPT, total, rows, LANES), shape(1, bx, by, LANES)],
        in_specs=[VMEM] * 4,
        out_specs=[VMEM] * 2,
        scratch_shapes=[
            pltpu.VMEM((8, total, rows, LANES), f32),
            pltpu.VMEM((2, bx, own, LANES), f32),
        ],
        compiler_params=params(24),
    )(table, mid, a, b)

    bits = [1 << k for k in reversed(range((nx - 1).bit_length()))]

    def over_y(near, first):
        bit = first
        while bit < ny:
            near = jnp.concatenate([near, permute(near, ("y", bit))])
            bit *= 2
        return near

    def over_x(near):
        for bit in bits[:-1]:
            near = jnp.concatenate([near, permute(near, ("x", bit))], axis=0)
        return near, permute(near, ("x", bits[-1]))

    halves = [fields_y, permute(fields_y, ("y", 2))]
    pair = jnp.concatenate([block, permute(block, ("y", 1))])
    halves, _ = lax.optimization_barrier((halves, pair))
    fields_y = over_y(jnp.concatenate(halves), 4)
    grids = [(bx * nx >> level, by * ny >> level) for level in range(3)]
    large = grids[0][0] * grids[0][1] > 1024
    operators = pl.pallas_call(
        functools.partial(operators_kernel, tuple(bits)),
        out_shape=[shape(*s) for g in grids for s in Level.operator(*g)],
        in_specs=[VMEM] * 2,
        out_specs=[VMEM] * (3 * OPERATOR),
        scratch_shapes=[pltpu.VMEM(s, f32) for g in grids for s in Level.fields(*g)]
        + [pltpu.VMEM((grids[0][1], LANES), f32)],
        compiler_params=params(60 if large else 16),
    )(*over_x(fields_y))
    near, far = over_x(over_y(pair, 2))
    return pl.pallas_call(
        functools.partial(second_kernel, tuple(bits)),
        out_shape=[shape(planes, own, LANES)] * 2,
        in_specs=[VMEM] * (3 + 3 * OPERATOR),
        out_specs=[VMEM] * 2,
        scratch_shapes=[pltpu.VMEM(s, f32) for g in grids for s in Level.iterates(*g)]
        + [
            pltpu.VMEM((grids[0][0] + 2, grids[0][1] + 2 * by, LANES), f32),
            pltpu.VMEM((max(grids[0][1], rows), LANES), f32),
            pltpu.VMEM((2, total, rows, LANES), f32),
            pltpu.VMEM((2, total, rows, LANES), f32),
        ],
        compiler_params=params(60 if large else 16),
    )(near, far, kept, *operators)


def solution(mesh):
    grid = P(("groups", "gx"), "gy", None)
    fn = functools.partial(per_device, *(mesh.shape[a] for a in ("groups", "gx", "gy")))
    return jax.shard_map(
        fn,
        mesh=mesh,
        in_specs=(grid, P(), P(), P(), grid, grid, grid),
        out_specs=(grid, grid),
        check_vma=False,
    )
```

```python
import functools
import itertools
import jax
import jax.numpy as jnp
from jax import lax
from jax.experimental import pallas as pl
from jax.experimental.pallas import tpu as pltpu
from jax.sharding import PartitionSpec as P

OMEGA = 0.8
COARSE_ITERS = 20
RIM = 4
LANES = 128
RIM_PLANES = ((0, RIM), (RIM, RIM), (2 * RIM, RIM - 1), (3 * RIM - 1, RIM - 1))
VMEM = pl.BlockSpec(memory_space=pltpu.VMEM)
HBM = pl.BlockSpec(memory_space=pltpu.HBM)


UNROLL = 16


def loop(first, end, body, init):
    if end - first > UNROLL:
        return lax.fori_loop(first, end, body, init)
    for i in range(first, end):
        body(i, 0)
    return init


def params(mib):
    return pltpu.CompilerParams(vmem_limit_bytes=int(mib * 1024 * 1024))


def bernoulli(x):
    t = x * x
    series = (1.0 - 0.5 * x) + t * (1 / 12 - t * (1 / 720))
    near = t < 0.0625
    guarded = jnp.where(near, 1.0, x)
    return jnp.where(near, series, guarded / (jnp.exp(guarded) - 1.0))


def iota(shape, dim):
    return lax.broadcasted_iota(jnp.int32, shape, dim)


def up(v, step, dim):
    return pltpu.roll(v, v.shape[dim] - step, dim)


def down(v, step, dim):
    return pltpu.roll(v, step, dim)


def halve_lanes(a, b):
    lane = iota(a.shape, 1)
    at = (2 * lane) % LANES
    a = jnp.take_along_axis(a + up(a, 1, 1), at, axis=1)
    b = jnp.take_along_axis(b + up(b, 1, 1), at, axis=1)
    return jnp.where(lane < LANES // 2, a, b)


def look_up(table, c, shape):
    found = [jnp.zeros(shape, jnp.float32)] * 3
    for k in range(table.shape[1]):
        same = c == float(k)
        found = [
            jnp.where(same, jnp.broadcast_to(table[f, k : k + 1], shape), found[f]) for f in range(3)
        ]
    return found


def rim_y_kernel(table, c_in, p_in, fp_in, fn_in, out_a, out_b, block, c_out, p_out, fp_out, fn_out, cls, work, sems):
    outs = (c_out, p_out, fp_out, fn_out)
    copies = [
        pltpu.make_async_copy(s, d, sems.at[k])
        for k, (s, d) in enumerate(zip((c_in, p_in, fp_in, fn_in), (cls, *outs[1:])))
    ]
    for c in copies:
        c.start()
    for c in copies:
        c.wait()
    c_out[...] = cls[...].astype(jnp.float32)
    even = lax.axis_index("gy") % 2 == 0
    planes, length = cls.shape[0], cls.shape[1]
    for pair in range(2):
        lo, hi = (
            jnp.concatenate([r[:, at : at + RIM, :] for r in outs[2 * pair : 2 * pair + 2]], axis=1)
            for at in (0, length - RIM)
        )
        out_a[pair * planes : (pair + 1) * planes] = jnp.where(even, hi, lo)
        out_b[pair * planes : (pair + 1) * planes] = jnp.where(even, lo, hi)
    bx = planes // 2
    for i in range(bx):
        one, two = (look_up(table, c_out[2 * i + k], (length, LANES)) for k in (0, 1))
        values = [p + q for p, q in zip(one, two)] + [p_out[2 * i] + p_out[2 * i + 1]]
        for k, v in enumerate(values):
            work[k, i] = v
    for i in range(bx):
        eps, mob, cap, pot = (
            work[k, i, pl.ds(0, length // 2, stride=2), :] + work[k, i, pl.ds(1, length // 2, stride=2), :]
            for k in range(4)
        )
        for f, v in enumerate((halve_lanes(eps, mob), halve_lanes(cap, pot))):
            block[0, f, i] = 0.125 * v


def rim_x_kernel(cls, pot, fp, fn, in_a, in_b, out, out_a, out_b):
    y, ny = lax.axis_index("gy"), lax.axis_size("gy")
    even_x, even_y = lax.axis_index("gx") % 2 == 0, y % 2 == 0
    planes, length = cls.shape[0], cls.shape[1]
    row = iota((planes, 2 * RIM, LANES), 1)
    for pair in range(2):
        a, b = (r[pair * planes : (pair + 1) * planes] for r in (in_a, in_b))
        hi, lo = jnp.where(even_y, a, b), jnp.where(even_y, b, a)
        for slot in range(2):
            field = 2 * pair + slot
            outside = -1.0 if field == 0 else 0.0
            h, l = jnp.where(y == ny - 1, outside, hi), jnp.where(y == 0, outside, lo)
            if slot == 0:
                l = down(l, RIM, 1)
            else:
                h = down(h, RIM, 1)
            out[field, :, 0:length, :] = (cls, pot, fp, fn)[field][...]
            out[field, :, length : length + 2 * RIM, :] = jnp.where(row < RIM, h, l)
        for slot in range(2):
            field = 2 * pair + slot
            at, n = RIM_PLANES[field]
            lo_x, hi_x = out[field, 0:n], out[field, planes - n : planes]
            out_a[at : at + n] = jnp.where(even_x, hi_x, lo_x)
            out_b[at : at + n] = jnp.where(even_x, lo_x, hi_x)


W_P, GX, GY, GZ, W_N, XP, XM, YP, YM, ZP, ZM, WF_P, WF_N, U_P, U_N = range(15)
KEPT = 15


def coupled_fine(kept, u, i, poisson):
    v = u(i)
    if poisson:
        xp, xm, yp, ym, zp, zm = GX, GX, GY, GY, GZ, GZ
    else:
        xp, xm, yp, ym, zp, zm = XP, XM, YP, YM, ZP, ZM
    s = kept[xp, i] * u(i + 1) + kept[xm, i - 1] * u(i - 1)
    s = s + (kept[yp, i] * up(v, 1, 0) + down(kept[ym, i] * v, 1, 0))
    return s + (kept[zp, i] * up(v, 1, 1) + down(kept[zm, i] * v, 1, 1))


def first_kernel(table, mid, in_a, in_b, kept, block, fld, work):
    x, nx = lax.axis_index("gx"), lax.axis_size("gx")
    even = x % 2 == 0
    planes = mid.shape[1]
    rows = mid.shape[2]
    own = rows - 2 * RIM
    total = planes + 2 * RIM
    EPS, MOB, POT, CAP, F_P, F_N, D_P, D_N = range(8)

    def materials(i, c, pot, fp, fn):
        eps, mob, cap = look_up(table, c, (rows, LANES))
        fld[EPS, i], fld[MOB, i], fld[POT, i], fld[CAP, i] = eps, mob, pot, cap
        fld[F_P, i], fld[F_N, i] = fp, fn

    def rim(i, ref_even, ref_odd, skip, outside):
        values = []
        for f, (at, n) in enumerate(RIM_PLANES):
            if n < RIM and i == skip:
                values.append(jnp.zeros((rows, LANES), jnp.float32))
                continue
            k = at + i - (1 if n < RIM and skip == 0 else 0)
            v = jnp.where(even, ref_even[k], ref_odd[k])
            values.append(jnp.where(outside, -1.0 if f == 0 else 0.0, v))
        return values

    def low(i, _):
        materials(i, *rim(i, in_b, in_a, 0, x == 0))
        return 0

    def middle(i, _):
        materials(i + RIM, *[mid[f, i] for f in range(4)])
        return 0

    def high(i, _):
        materials(i + RIM + planes, *rim(i, in_a, in_b, RIM - 1, x == nx - 1))
        return 0

    loop(0, RIM, low, 0)
    loop(0, planes, middle, 0)
    loop(0, RIM, high, 0)

    shape = (rows, LANES)
    lane = iota(shape, 1)
    ends = (lane == 0) | (lane == LANES - 1)
    top = lane == LANES - 1

    def x_faces(i):
        eps, mob, pot = fld[EPS, i], fld[MOB, i], fld[POT, i]
        kept[GX, i] = 0.5 * (eps + fld[EPS, i + 1])
        k = 0.5 * (mob + fld[MOB, i + 1])
        delta = fld[POT, i + 1] - pot
        kb = k * bernoulli(delta)
        kept[XP, i] = kb
        kept[XM, i] = kb + k * delta

    x_faces(0)

    def operators(i, _):
        x_faces(i)
        eps, mob, pot = fld[EPS, i], fld[MOB, i], fld[POT, i]
        gy = 0.5 * (eps + up(eps, 1, 0))
        k = 0.5 * (mob + up(mob, 1, 0))
        delta = up(pot, 1, 0) - pot
        yp = k * bernoulli(delta)
        ym = yp + k * delta
        gz = jnp.where(top, 0.0, 0.5 * (eps + up(eps, 1, 1)))
        k = jnp.where(top, 0.0, 0.5 * (mob + up(mob, 1, 1)))
        delta = up(pot, 1, 1) - pot
        zp = k * bernoulli(delta)
        zm = zp + k * delta
        kept[GY, i], kept[YP, i], kept[YM, i] = gy, yp, ym
        kept[GZ, i], kept[ZP, i], kept[ZM, i] = gz, zp, zm
        d_p = (kept[GX, i] + kept[GX, i - 1]) + (gy + down(gy, 1, 0)) + (gz + down(gz, 1, 1))
        d_p = d_p + jnp.where(ends, 0.5 * eps, 0.0)
        d_n = (kept[XM, i] + kept[XP, i - 1]) + (ym + down(yp, 1, 0)) + (zm + down(zp, 1, 1))
        d_n = d_n + jnp.where(ends, 0.5 * mob * bernoulli(pot), 0.0) + fld[CAP, i]
        inside = eps > 0.0
        w_p = jnp.where(inside, OMEGA / jnp.where(inside, d_p, 1.0), 0.0)
        w_n = jnp.where(inside, OMEGA / jnp.where(inside, d_n, 1.0), 0.0)
        kept[W_P, i], kept[W_N, i] = w_p, w_n
        kept[WF_P, i], kept[WF_N, i] = w_p * fld[F_P, i], w_n * fld[F_N, i]
        fld[D_P, i], fld[D_N, i] = d_p, d_n
        return 0

    loop(1, total - 1, operators, 0)

    def sweep(i, _):
        for poisson, w, wf, u in ((True, W_P, WF_P, U_P), (False, W_N, WF_N, U_N)):
            s = coupled_fine(kept, lambda j: kept[wf, j], i, poisson)
            kept[u, i] = (2.0 - OMEGA) * kept[wf, i] + kept[w, i] * s
        return 0

    loop(2, total - 2, sweep, 0)

    def residual(i, poisson, f, d, u):
        s = coupled_fine(kept, lambda j: kept[u, j], i, poisson)
        return fld[f, i] - fld[d, i] * kept[u, i] + s

    def coarse(i, _):
        at = RIM + 2 * i
        r_p = residual(at, True, F_P, D_P, U_P) + residual(at + 1, True, F_P, D_P, U_P)
        r_n = residual(at, False, F_N, D_N, U_N) + residual(at + 1, False, F_N, D_N, U_N)
        work[0, i], work[1, i] = r_p[0:own], r_n[0:own]
        r_p, r_n = (
            work[k, i, pl.ds(0, own // 2, stride=2), :] + work[k, i, pl.ds(1, own // 2, stride=2), :]
            for k in range(2)
        )
        block[0, i] = 0.125 * halve_lanes(r_p, r_n)
        return 0

    loop(0, planes // 2, coarse, 0)


def low_lane(shape, bit):
    return (iota(shape, 1) & bit) == 0


OPERATOR = 8


class Level:
    def __init__(self, level, refs):
        self.level, self.step, self.factor = level, 1 << (level - 1), 0.25**level
        (self.xp, self.xm, self.yp, self.ym, self.zp, self.zm, self.w, self.d) = refs[:OPERATOR]
        if len(refs) == OPERATOR + 3:
            self.eps, self.pot, self.cap = refs[OPERATOR:]
        else:
            self.f, self.wf, self.u, self.v = refs[OPERATOR:]
        self.nx, self.ny = self.w.shape[0], self.w.shape[1]

    @staticmethod
    def operator(nx, ny):
        return [(nx + 1, ny, LANES)] * 2 + [(nx, ny, LANES)] * 6

    @staticmethod
    def fields(nx, ny):
        return [(nx, ny, LANES)] * 3

    @staticmethod
    def iterates(nx, ny):
        return [(nx, ny, LANES)] * 2 + [(nx + 2, ny, LANES)] * 2

    def assemble(self):
        nx, ny, step = self.nx, self.ny, self.step
        shape = (ny, LANES)
        row, spot = iota(shape, 0), iota(shape, 1) % (LANES // 2)
        last_row, top = row == ny - 1, spot >= LANES // 2 - step
        walls = (
            jnp.where(row == 0, 1.0, 0.0)
            + jnp.where(last_row, 1.0, 0.0)
            + jnp.where(spot < step, 1.0, 0.0)
            + jnp.where(top, 1.0, 0.0)
        )
        zero = jnp.zeros(shape, jnp.float32)
        half = 0.5 * self.factor
        for ref in (self.xp, self.xm):
            ref[0], ref[nx] = zero, zero

        def x_face(i, _):
            k = half * (self.eps[i - 1] + self.eps[i])
            delta = self.pot[i] - self.pot[i - 1]
            kb = k * bernoulli(delta)
            self.xp[i], self.xm[i] = kb, kb + k * delta
            return 0

        loop(1, nx, x_face, 0)

        def plane(i, _):
            eps, pot = self.eps[i], self.pot[i]
            k = jnp.where(last_row, 0.0, half * (eps + up(eps, 1, 0)))
            delta = up(pot, 1, 0) - pot
            yp = k * bernoulli(delta)
            ym = yp + k * delta
            k = jnp.where(top, 0.0, half * (eps + up(eps, step, 1)))
            delta = up(pot, step, 1) - pot
            zp = k * bernoulli(delta)
            zm = zp + k * delta
            outer = walls + jnp.where(i == 0, 1.0, 0.0) + jnp.where(i == nx - 1, 1.0, 0.0)
            d = (self.xm[i + 1] + self.xp[i]) + (ym + down(yp, 1, 0)) + (zm + down(zp, step, 1))
            d = d + outer * (half * eps * bernoulli(pot)) + self.cap[i]
            w = OMEGA / d
            self.yp[i], self.ym[i], self.zp[i], self.zm[i] = yp, ym, zp, zm
            self.d[i], self.w[i] = d, w
            return 0

        loop(0, nx, plane, 0)

    def coupled(self, u, i):
        v = u[i + 1]
        s = self.xp[i + 1] * u[i + 2] + self.xm[i] * u[i]
        s = s + (self.yp[i] * up(v, 1, 0) + down(self.ym[i] * v, 1, 0))
        return s + (self.zp[i] * up(v, self.step, 1) + down(self.zm[i] * v, self.step, 1))

    def start(self):
        zero = jnp.zeros((self.ny, LANES), jnp.float32)
        for ref in (self.u, self.v):
            ref[0], ref[self.nx + 1] = zero, zero

        def body(i, _):
            wf = self.w[i] * self.f[i]
            self.wf[i] = wf
            self.u[i + 1] = wf
            return 0

        loop(0, self.nx, body, 0)

    def sweep(self, u, v):
        def body(i, _):
            v[i + 1] = (1.0 - OMEGA) * u[i + 1] + self.wf[i] + self.w[i] * self.coupled(u, i)
            return 0

        loop(0, self.nx, body, 0)

    def halve(self, tmp, v):
        step, ny = self.step, self.ny
        tmp[0:ny] = v
        v = tmp[pl.ds(0, ny // 2, stride=2), :] + tmp[pl.ds(1, ny // 2, stride=2), :]
        other = jnp.where(low_lane(v.shape, step), up(v, step, 1), down(v, step, 1))
        return 0.125 * (v + other)

    def descend_fields(self, coarser, tmp):
        def body(i, _):
            for here, there in ((self.eps, coarser.eps), (self.pot, coarser.pot), (self.cap, coarser.cap)):
                there[i] = self.halve(tmp, here[2 * i] + here[2 * i + 1])
            return 0

        loop(0, coarser.nx, body, 0)

    def descend_residual(self, u, coarser, tmp):
        def residual(i):
            return self.f[i] - self.d[i] * u[i + 1] + self.coupled(u, i)

        def body(i, _):
            coarser.f[i] = self.halve(tmp, residual(2 * i) + residual(2 * i + 1))
            return 0

        loop(0, coarser.nx, body, 0)

    def correct(self, u, coarser_u, tmp):
        half_ny = self.ny // 2

        def body(i, _):
            e = coarser_u(i)
            tmp[pl.ds(0, half_ny, stride=2), :] = e
            tmp[pl.ds(1, half_ny, stride=2), :] = e
            wide = tmp[0 : self.ny]
            u[2 * i + 1] = u[2 * i + 1] + wide
            u[2 * i + 2] = u[2 * i + 2] + wide
            return 0

        loop(0, self.nx // 2, body, 0)


def coarsest(lv):
    nx, step = lv.nx, lv.step
    cxp = [lv.w[i] * lv.xp[i + 1] for i in range(nx)]
    cxm = [lv.w[i] * lv.xm[i] for i in range(nx)]
    cyp = [lv.w[i] * lv.yp[i] for i in range(nx)]
    cym = [lv.w[i] * down(lv.ym[i], 1, 0) for i in range(nx)]
    czp = [lv.w[i] * lv.zp[i] for i in range(nx)]
    czm = [lv.w[i] * down(lv.zm[i], step, 1) for i in range(nx)]
    wf = [lv.w[i] * lv.f[i] for i in range(nx)]

    def body(_, u):
        new = []
        for i in range(nx):
            s = czp[i] * up(u[i], step, 1) + czm[i] * down(u[i], step, 1)
            t = cyp[i] * up(u[i], 1, 0) + cym[i] * down(u[i], 1, 0)
            r = (1.0 - OMEGA) * u[i] + wf[i]
            if i + 1 < nx:
                r = r + cxp[i] * u[i + 1]
            if i > 0:
                r = r + cxm[i] * u[i - 1]
            new.append(r + t + s)
        return tuple(new)

    u = tuple(wf)
    for _ in range(COARSE_ITERS - 1):
        u = body(0, u)
    for i in range(nx):
        lv.u[i + 1] = u[i]


def place(bits, y_bits, ref, flip, x, y, ny, put):
    bx, by = ref.shape[-3], ref.shape[-2]

    def body(m, _):
        b = m // ny
        to_x = x ^ flip
        for k, bit in enumerate(bits[:-1]):
            to_x = to_x ^ (((b >> k) & 1) * bit)
        to_y = y
        for k, bit in enumerate(y_bits):
            to_y = to_y ^ (((m >> k) & 1) * bit)
        row = pl.ds(pl.multiple_of(to_y * by, by), by)
        for i in range(bx):
            put(m, i, to_x * bx + i, row)
        return 0

    loop(0, ref.shape[0], body, 0)


def operators_kernel(bits, y_bits, near, far, *refs):
    x, y, ny = lax.axis_index("gx"), lax.axis_index("gy"), lax.axis_size("gy")
    outs, scratch = refs[: 3 * OPERATOR], refs[3 * OPERATOR :]
    l1, l2, l3 = (
        Level(k + 1, outs[OPERATOR * k : OPERATOR * (k + 1)] + scratch[3 * k : 3 * k + 3]) for k in range(3)
    )
    tmp = scratch[9]
    right = iota((near.shape[-2], LANES), 1) >= LANES // 2
    for ref, flip in ((near, 0), (far, bits[-1])):

        def put(m, i, at, row, ref=ref):
            q = ref[m, 1, i]
            l1.eps[at, row, :] = ref[m, 0, i]
            l1.pot[at, row, :] = jnp.where(right, q, 0.0)
            l1.cap[at, row, :] = jnp.where(right, down(q, LANES // 2, 1), 0.0)

        place(bits, y_bits, ref, flip, x, y, ny, put)
    l1.assemble()
    l1.descend_fields(l2, tmp)
    l2.assemble()
    l2.descend_fields(l3, tmp)
    l3.assemble()


def second_kernel(bits, y_bits, near, far, kept, *refs):
    x, y, ny = lax.axis_index("gx"), lax.axis_index("gy"), lax.axis_size("gy")
    given, (out_p, out_n), scratch = refs[: 3 * OPERATOR], refs[3 * OPERATOR : 3 * OPERATOR + 2], refs[3 * OPERATOR + 2 :]
    l1, l2, l3 = (
        Level(k + 1, given[OPERATOR * k : OPERATOR * (k + 1)] + scratch[4 * k : 4 * k + 4]) for k in range(3)
    )
    sol, tmp, fine_a, fine_b = scratch[12:]
    bx, by = near.shape[-3], near.shape[-2]
    for ref, flip in ((near, 0), (far, bits[-1])):

        def put(m, i, at, row, ref=ref):
            l1.f[at, row, :] = ref[m, i]

        place(bits, y_bits, ref, flip, x, y, ny, put)
    for here, there in ((l1, l2), (l2, l3)):
        here.start()
        here.sweep(here.u, here.v)
        here.descend_residual(here.v, there, tmp)
    coarsest(l3)
    l2.correct(l2.v, lambda i: l3.u[i + 1], tmp)
    l2.sweep(l2.v, l2.u)
    l2.sweep(l2.u, l2.v)
    l1.correct(l1.v, lambda i: l2.v[i + 1], tmp)
    l1.sweep(l1.v, l1.u)
    edge = jnp.zeros((by, LANES), jnp.float32)
    n1x, n1y = l1.nx, l1.ny
    blank = jnp.zeros((n1y + 2 * by, LANES), jnp.float32)
    sol[0], sol[n1x + 1] = blank, blank

    def last(i, _):
        sol[i + 1, 0:by] = edge
        sol[i + 1, by + n1y :] = edge
        sol[i + 1, by : by + n1y] = (
            (1.0 - OMEGA) * l1.u[i + 1] + l1.wf[i] + l1.w[i] * l1.coupled(l1.u, i)
        )
        return 0

    loop(0, n1x, last, 0)

    rows = kept.shape[2]
    own = rows - 2 * RIM
    tile_row = iota((by, LANES), 0)
    spread = iota((by, LANES), 1) // 2

    def widen(v, channel):
        return jnp.take_along_axis(v, spread + channel * (LANES // 2), axis=1)

    def correct(i, _):
        at = x * bx + i
        middle, above, below = (
            sol[at, pl.ds(pl.multiple_of((y + k) * by, by), by), :] for k in (1, 2, 0)
        )
        rim = jnp.where(
            tile_row < 2,
            jnp.broadcast_to(above[0:1], (by, LANES)),
            jnp.where(tile_row >= by - 2, jnp.broadcast_to(below[by - 1 : by], (by, LANES)), 0.0),
        )
        for channel, u in ((0, U_P), (1, U_N)):
            e = widen(middle, channel)
            tmp[pl.ds(0, by, stride=2), :] = e
            tmp[pl.ds(1, by, stride=2), :] = e
            tmp[own:rows] = widen(rim, channel)
            e = tmp[0:rows]
            for k in (0, 1):
                p = RIM - 2 + 2 * i + k
                fine_a[channel, p] = kept[u, p] + e
        return 0

    loop(0, bx + 2, correct, 0)

    def fine(u, channel, i):
        w, wf = ((W_P, WF_P), (W_N, WF_N))[channel]
        s = coupled_fine(kept, lambda j: u[channel, j], i, channel == 0)
        return (1.0 - OMEGA) * u[channel, i] + kept[wf, i] + kept[w, i] * s

    def post_one(i, _):
        for channel in (0, 1):
            fine_b[channel, i] = fine(fine_a, channel, i)
        return 0

    def post_two(i, _):
        out_p[i] = fine(fine_b, 0, i + RIM)[0:own]
        out_n[i] = fine(fine_b, 1, i + RIM)[0:own]
        return 0

    loop(RIM - 1, RIM + 2 * bx + 1, post_one, 0)
    loop(0, 2 * bx, post_two, 0)


def moves(ng, nx, ny):
    def of(partner):
        place = {p: k for k, p in enumerate(itertools.product(range(ng), range(nx), range(ny)))}
        return [(k, place[partner(*p)]) for p, k in place.items()]

    def other(k):
        return k + 1 if k % 2 else k - 1

    return {
        "xa": of(lambda g, a, b: (g, a ^ 1, b)),
        "xb": of(lambda g, a, b: (g, other(a), b) if 0 < a < nx - 1 else (g ^ 1, a, b)),
        "ya": of(lambda g, a, b: (g, a, b ^ 1)),
        "yb": of(lambda g, a, b: (g, a, other(b)) if 0 < b < ny - 1 else (g, a ^ 1, b)),
        **{("x", 1 << k): of(lambda g, a, b, k=k: (g, a ^ (1 << k), b)) for k in range((nx - 1).bit_length())},
        **{("y", 1 << k): of(lambda g, a, b, k=k: (g, a, b ^ (1 << k))) for k in range((ny - 1).bit_length())},
    }


def per_device(ng, nx, ny, layer_class, permittivity, mobility, capture, potential, rhs_psi, rhs_n):
    send = moves(ng, nx, ny)
    f32 = jnp.float32

    def permute(v, name):
        return lax.ppermute(v, ("groups", "gx", "gy"), send[name])

    planes, own = layer_class.shape[0], layer_class.shape[1]
    rows, total = own + 2 * RIM, planes + 2 * RIM
    bx, by = planes // 2, own // 2
    def shape(*dims):
        return jax.ShapeDtypeStruct(dims, f32)

    table = jnp.stack([permittivity, mobility, capture])
    table = jnp.broadcast_to(table[:, :, None], (*table.shape, LANES))
    cell = (planes, own, LANES)
    a, b, fields, *raw = pl.pallas_call(
        rim_y_kernel,
        out_shape=[
            shape(2 * planes, by, LANES),
            shape(2 * planes, by, LANES),
            shape(1, 2, bx, by, LANES),
        ]
        + [shape(*cell)] * 4,
        in_specs=[VMEM] + [HBM] * 4,
        out_specs=[VMEM] * 7,
        scratch_shapes=[
            pltpu.VMEM(cell, jnp.int32),
            pltpu.VMEM((4, bx, own, LANES), f32),
            pltpu.SemaphoreType.DMA((4,)),
        ],
        compiler_params=params(53.5),
    )(table, layer_class, potential, rhs_psi, rhs_n)
    b = permute(b, "yb")
    a = permute(jnp.concatenate([a, fields.reshape(-1, by, LANES)]), "ya")
    fields_y = [fields, a[2 * planes :].reshape(fields.shape)]
    mid, a, b = pl.pallas_call(
        rim_x_kernel,
        out_shape=[shape(4, planes, rows, LANES)] + [shape(4 * RIM - 2, rows, LANES)] * 2,
        in_specs=[VMEM] * 6,
        out_specs=[VMEM] * 3,
        compiler_params=params(16),
    )(*raw, a, b)
    fields_y, _ = lax.optimization_barrier((jnp.concatenate(fields_y), mid))
    b = permute(b, "xb")
    a = permute(a, "xa")
    kept, block = pl.pallas_call(
        first_kernel,
        out_shape=[shape(KEPT, total, rows, LANES), shape(1, bx, by, LANES)],
        in_specs=[VMEM] * 4,
        out_specs=[VMEM] * 2,
        scratch_shapes=[
            pltpu.VMEM((8, total, rows, LANES), f32),
            pltpu.VMEM((2, bx, own, LANES), f32),
        ],
        compiler_params=params(24),
    )(table, mid, a, b)

    bits = [1 << k for k in reversed(range((nx - 1).bit_length()))]

    def over_y(near, line):
        for bit in line:
            near = jnp.concatenate([near, permute(near, ("y", bit))])
        return near

    def over_x(near):
        for bit in bits[:-1]:
            near = jnp.concatenate([near, permute(near, ("x", bit))], axis=0)
        return near, permute(near, ("x", bits[-1]))

    halves = [fields_y, permute(fields_y, ("y", 2))]
    y_bits = tuple(1 << k for k in range((ny - 1).bit_length()))
    y_turn = (2, 1) + y_bits[2:]
    pair = jnp.concatenate([block, permute(block, ("y", 2))])
    halves, _ = lax.optimization_barrier((halves, pair))
    fields_y = over_y(jnp.concatenate(halves), y_bits[2:])
    grids = [(bx * nx >> level, by * ny >> level) for level in range(3)]
    large = grids[0][0] * grids[0][1] > 1024
    operators = pl.pallas_call(
        functools.partial(operators_kernel, tuple(bits), y_bits),
        out_shape=[shape(*s) for g in grids for s in Level.operator(*g)],
        in_specs=[VMEM] * 2,
        out_specs=[VMEM] * (3 * OPERATOR),
        scratch_shapes=[pltpu.VMEM(s, f32) for g in grids for s in Level.fields(*g)]
        + [pltpu.VMEM((grids[0][1], LANES), f32)],
        compiler_params=params(60 if large else 16),
    )(*over_x(fields_y))
    near, far = over_x(over_y(pair, y_turn[1:]))
    return pl.pallas_call(
        functools.partial(second_kernel, tuple(bits), y_turn),
        out_shape=[shape(planes, own, LANES)] * 2,
        in_specs=[VMEM] * (3 + 3 * OPERATOR),
        out_specs=[VMEM] * 2,
        scratch_shapes=[pltpu.VMEM(s, f32) for g in grids for s in Level.iterates(*g)]
        + [
            pltpu.VMEM((grids[0][0] + 2, grids[0][1] + 2 * by, LANES), f32),
            pltpu.VMEM((max(grids[0][1], rows), LANES), f32),
            pltpu.VMEM((2, total, rows, LANES), f32),
            pltpu.VMEM((2, total, rows, LANES), f32),
        ],
        compiler_params=params(60 if large else 16),
    )(near, far, kept, *operators)


def solution(mesh):
    grid = P(("groups", "gx"), "gy", None)
    fn = functools.partial(per_device, *(mesh.shape[a] for a in ("groups", "gx", "gy")))
    return jax.shard_map(
        fn,
        mesh=mesh,
        in_specs=(grid, P(), P(), P(), grid, grid, grid),
        out_specs=(grid, grid),
        check_vma=False,
    )
```

```python
import functools
import itertools
import jax
import jax.numpy as jnp
from jax import lax
from jax.experimental import pallas as pl
from jax.experimental.pallas import tpu as pltpu
from jax.sharding import PartitionSpec as P

OMEGA = 0.8
COARSE_ITERS = 20
RIM = 4
LANES = 128
RIM_PLANES = ((0, RIM), (RIM, RIM), (2 * RIM, RIM - 1), (3 * RIM - 1, RIM - 1))
VMEM = pl.BlockSpec(memory_space=pltpu.VMEM)
HBM = pl.BlockSpec(memory_space=pltpu.HBM)


UNROLL = 16


def loop(first, end, body, init):
    if end - first > UNROLL:
        return lax.fori_loop(first, end, body, init)
    for i in range(first, end):
        body(i, 0)
    return init


def params(mib):
    return pltpu.CompilerParams(vmem_limit_bytes=int(mib * 1024 * 1024))


def bernoulli(x):
    t = x * x
    series = (1.0 - 0.5 * x) + t * (1 / 12 - t * (1 / 720))
    near = t < 0.0625
    return jnp.where(near, series, x / (jnp.exp(x) - 1.0))


def iota(shape, dim):
    return lax.broadcasted_iota(jnp.int32, shape, dim)


def up(v, step, dim):
    return pltpu.roll(v, v.shape[dim] - step, dim)


def down(v, step, dim):
    return pltpu.roll(v, step, dim)


def halve_lanes(a, b):
    lane = iota(a.shape, 1)
    at = (2 * lane) % LANES
    a = jnp.take_along_axis(a + up(a, 1, 1), at, axis=1)
    b = jnp.take_along_axis(b + up(b, 1, 1), at, axis=1)
    return jnp.where(lane < LANES // 2, a, b)


def look_up(table, c, shape):
    found = [jnp.zeros(shape, jnp.float32)] * 3
    for k in range(table.shape[1]):
        same = c == float(k)
        found = [
            jnp.where(same, jnp.broadcast_to(table[f, k : k + 1], shape), found[f]) for f in range(3)
        ]
    return found


def rim_y_kernel(table, c_in, p_in, fp_in, fn_in, out_a, out_b, block, c_out, p_out, fp_out, fn_out, cls, work, sems):
    outs = (c_out, p_out, fp_out, fn_out)
    copies = [
        pltpu.make_async_copy(s, d, sems.at[k])
        for k, (s, d) in enumerate(zip((c_in, p_in, fp_in, fn_in), (cls, *outs[1:])))
    ]
    for c in copies:
        c.start()
    for c in copies:
        c.wait()
    c_out[...] = cls[...].astype(jnp.float32)
    even = lax.axis_index("gy") % 2 == 0
    planes, length = cls.shape[0], cls.shape[1]
    for pair in range(2):
        lo, hi = (
            jnp.concatenate([r[:, at : at + RIM, :] for r in outs[2 * pair : 2 * pair + 2]], axis=1)
            for at in (0, length - RIM)
        )
        out_a[pair * planes : (pair + 1) * planes] = jnp.where(even, hi, lo)
        out_b[pair * planes : (pair + 1) * planes] = jnp.where(even, lo, hi)
    bx = planes // 2
    for i in range(bx):
        one, two = (look_up(table, c_out[2 * i + k], (length, LANES)) for k in (0, 1))
        values = [p + q for p, q in zip(one, two)] + [p_out[2 * i] + p_out[2 * i + 1]]
        for k, v in enumerate(values):
            work[k, i] = v
    for i in range(bx):
        eps, mob, cap, pot = (
            work[k, i, pl.ds(0, length // 2, stride=2), :] + work[k, i, pl.ds(1, length // 2, stride=2), :]
            for k in range(4)
        )
        for f, v in enumerate((halve_lanes(eps, mob), halve_lanes(cap, pot))):
            block[0, f, i] = 0.125 * v


def rim_x_kernel(cls, pot, fp, fn, in_a, in_b, out, out_a, out_b):
    y, ny = lax.axis_index("gy"), lax.axis_size("gy")
    even_x, even_y = lax.axis_index("gx") % 2 == 0, y % 2 == 0
    planes, length = cls.shape[0], cls.shape[1]
    row = iota((planes, 2 * RIM, LANES), 1)
    for pair in range(2):
        a, b = (r[pair * planes : (pair + 1) * planes] for r in (in_a, in_b))
        hi, lo = jnp.where(even_y, a, b), jnp.where(even_y, b, a)
        for slot in range(2):
            field = 2 * pair + slot
            outside = -1.0 if field == 0 else 0.0
            h, l = jnp.where(y == ny - 1, outside, hi), jnp.where(y == 0, outside, lo)
            if slot == 0:
                l = down(l, RIM, 1)
            else:
                h = down(h, RIM, 1)
            out[field, :, 0:length, :] = (cls, pot, fp, fn)[field][...]
            out[field, :, length : length + 2 * RIM, :] = jnp.where(row < RIM, h, l)
        for slot in range(2):
            field = 2 * pair + slot
            at, n = RIM_PLANES[field]
            lo_x, hi_x = out[field, 0:n], out[field, planes - n : planes]
            out_a[at : at + n] = jnp.where(even_x, hi_x, lo_x)
            out_b[at : at + n] = jnp.where(even_x, lo_x, hi_x)


W_P, GX, GY, GZ, W_N, XP, XM, YP, YM, ZP, ZM, WF_P, WF_N, U_P, U_N = range(15)
KEPT = 15


def coupled_fine(kept, u, i, poisson):
    v = u(i)
    if poisson:
        xp, xm, yp, ym, zp, zm = GX, GX, GY, GY, GZ, GZ
    else:
        xp, xm, yp, ym, zp, zm = XP, XM, YP, YM, ZP, ZM
    s = kept[xp, i] * u(i + 1) + kept[xm, i - 1] * u(i - 1)
    s = s + (kept[yp, i] * up(v, 1, 0) + down(kept[ym, i] * v, 1, 0))
    return s + (kept[zp, i] * up(v, 1, 1) + down(kept[zm, i] * v, 1, 1))


def first_kernel(table, mid, in_a, in_b, kept, block, fld, work):
    x, nx = lax.axis_index("gx"), lax.axis_size("gx")
    even = x % 2 == 0
    planes = mid.shape[1]
    rows = mid.shape[2]
    own = rows - 2 * RIM
    total = planes + 2 * RIM
    EPS, MOB, POT, CAP, F_P, F_N, D_P, D_N = range(8)

    def materials(i, c, pot, fp, fn):
        eps, mob, cap = look_up(table, c, (rows, LANES))
        fld[EPS, i], fld[MOB, i], fld[POT, i], fld[CAP, i] = eps, mob, pot, cap
        fld[F_P, i], fld[F_N, i] = fp, fn

    def rim(i, ref_even, ref_odd, skip, outside):
        values = []
        for f, (at, n) in enumerate(RIM_PLANES):
            if n < RIM and i == skip:
                values.append(jnp.zeros((rows, LANES), jnp.float32))
                continue
            k = at + i - (1 if n < RIM and skip == 0 else 0)
            v = jnp.where(even, ref_even[k], ref_odd[k])
            values.append(jnp.where(outside, -1.0 if f == 0 else 0.0, v))
        return values

    def low(i, _):
        materials(i, *rim(i, in_b, in_a, 0, x == 0))
        return 0

    def middle(i, _):
        materials(i + RIM, *[mid[f, i] for f in range(4)])
        return 0

    def high(i, _):
        materials(i + RIM + planes, *rim(i, in_a, in_b, RIM - 1, x == nx - 1))
        return 0

    loop(0, RIM, low, 0)
    loop(0, planes, middle, 0)
    loop(0, RIM, high, 0)

    shape = (rows, LANES)
    lane = iota(shape, 1)
    ends = (lane == 0) | (lane == LANES - 1)
    top = lane == LANES - 1

    def x_faces(i):
        eps, mob, pot = fld[EPS, i], fld[MOB, i], fld[POT, i]
        kept[GX, i] = 0.5 * (eps + fld[EPS, i + 1])
        k = 0.5 * (mob + fld[MOB, i + 1])
        delta = fld[POT, i + 1] - pot
        kb = k * bernoulli(delta)
        kept[XP, i] = kb
        kept[XM, i] = kb + k * delta

    x_faces(0)

    def operators(i, _):
        x_faces(i)
        eps, mob, pot = fld[EPS, i], fld[MOB, i], fld[POT, i]
        gy = 0.5 * (eps + up(eps, 1, 0))
        k = 0.5 * (mob + up(mob, 1, 0))
        delta = up(pot, 1, 0) - pot
        yp = k * bernoulli(delta)
        ym = yp + k * delta
        gz = jnp.where(top, 0.0, 0.5 * (eps + up(eps, 1, 1)))
        k = jnp.where(top, 0.0, 0.5 * (mob + up(mob, 1, 1)))
        delta = up(pot, 1, 1) - pot
        zp = k * bernoulli(delta)
        zm = zp + k * delta
        kept[GY, i], kept[YP, i], kept[YM, i] = gy, yp, ym
        kept[GZ, i], kept[ZP, i], kept[ZM, i] = gz, zp, zm
        d_p = (kept[GX, i] + kept[GX, i - 1]) + (gy + down(gy, 1, 0)) + (gz + down(gz, 1, 1))
        d_p = d_p + jnp.where(ends, 0.5 * eps, 0.0)
        d_n = (kept[XM, i] + kept[XP, i - 1]) + (ym + down(yp, 1, 0)) + (zm + down(zp, 1, 1))
        d_n = d_n + jnp.where(ends, 0.5 * mob * bernoulli(pot), 0.0) + fld[CAP, i]
        inside = eps > 0.0
        w_p = jnp.where(inside, OMEGA / d_p, 0.0)
        w_n = jnp.where(inside, OMEGA / d_n, 0.0)
        kept[W_P, i], kept[W_N, i] = w_p, w_n
        kept[WF_P, i], kept[WF_N, i] = w_p * fld[F_P, i], w_n * fld[F_N, i]
        fld[D_P, i], fld[D_N, i] = d_p, d_n
        return 0

    loop(1, total - 1, operators, 0)

    def sweep(i, _):
        for poisson, w, wf, u in ((True, W_P, WF_P, U_P), (False, W_N, WF_N, U_N)):
            s = coupled_fine(kept, lambda j: kept[wf, j], i, poisson)
            kept[u, i] = (2.0 - OMEGA) * kept[wf, i] + kept[w, i] * s
        return 0

    loop(2, total - 2, sweep, 0)

    def residual(i, poisson, f, d, u):
        s = coupled_fine(kept, lambda j: kept[u, j], i, poisson)
        return fld[f, i] - fld[d, i] * kept[u, i] + s

    def coarse(i, _):
        at = RIM + 2 * i
        r_p = residual(at, True, F_P, D_P, U_P) + residual(at + 1, True, F_P, D_P, U_P)
        r_n = residual(at, False, F_N, D_N, U_N) + residual(at + 1, False, F_N, D_N, U_N)
        work[0, i], work[1, i] = r_p[0:own], r_n[0:own]
        r_p, r_n = (
            work[k, i, pl.ds(0, own // 2, stride=2), :] + work[k, i, pl.ds(1, own // 2, stride=2), :]
            for k in range(2)
        )
        block[0, i] = 0.125 * halve_lanes(r_p, r_n)
        return 0

    loop(0, planes // 2, coarse, 0)


def low_lane(shape, bit):
    return (iota(shape, 1) & bit) == 0


OPERATOR = 8


class Level:
    def __init__(self, level, refs):
        self.level, self.step, self.factor = level, 1 << (level - 1), 0.25**level
        (self.xp, self.xm, self.yp, self.ym, self.zp, self.zm, self.w, self.d) = refs[:OPERATOR]
        if len(refs) == OPERATOR + 3:
            self.eps, self.pot, self.cap = refs[OPERATOR:]
        else:
            self.f, self.wf, self.u, self.v = refs[OPERATOR:]
        self.nx, self.ny = self.w.shape[0], self.w.shape[1]

    @staticmethod
    def operator(nx, ny):
        return [(nx + 1, ny, LANES)] * 2 + [(nx, ny, LANES)] * 6

    @staticmethod
    def fields(nx, ny):
        return [(nx, ny, LANES)] * 3

    @staticmethod
    def iterates(nx, ny):
        return [(nx, ny, LANES)] * 2 + [(nx + 2, ny, LANES)] * 2

    def assemble(self):
        nx, ny, step = self.nx, self.ny, self.step
        shape = (ny, LANES)
        row, spot = iota(shape, 0), iota(shape, 1) % (LANES // 2)
        last_row, top = row == ny - 1, spot >= LANES // 2 - step
        walls = (
            jnp.where(row == 0, 1.0, 0.0)
            + jnp.where(last_row, 1.0, 0.0)
            + jnp.where(spot < step, 1.0, 0.0)
            + jnp.where(top, 1.0, 0.0)
        )
        zero = jnp.zeros(shape, jnp.float32)
        half = 0.5 * self.factor
        for ref in (self.xp, self.xm):
            ref[0], ref[nx] = zero, zero

        def x_face(i, _):
            k = half * (self.eps[i - 1] + self.eps[i])
            delta = self.pot[i] - self.pot[i - 1]
            kb = k * bernoulli(delta)
            self.xp[i], self.xm[i] = kb, kb + k * delta
            return 0

        loop(1, nx, x_face, 0)

        def plane(i, _):
            eps, pot = self.eps[i], self.pot[i]
            k = jnp.where(last_row, 0.0, half * (eps + up(eps, 1, 0)))
            delta = up(pot, 1, 0) - pot
            yp = k * bernoulli(delta)
            ym = yp + k * delta
            k = jnp.where(top, 0.0, half * (eps + up(eps, step, 1)))
            delta = up(pot, step, 1) - pot
            zp = k * bernoulli(delta)
            zm = zp + k * delta
            outer = walls + jnp.where(i == 0, 1.0, 0.0) + jnp.where(i == nx - 1, 1.0, 0.0)
            d = (self.xm[i + 1] + self.xp[i]) + (ym + down(yp, 1, 0)) + (zm + down(zp, step, 1))
            d = d + outer * (half * eps * bernoulli(pot)) + self.cap[i]
            w = OMEGA / d
            self.yp[i], self.ym[i], self.zp[i], self.zm[i] = yp, ym, zp, zm
            self.d[i], self.w[i] = d, w
            return 0

        loop(0, nx, plane, 0)

    def coupled(self, u, i):
        v = u[i + 1]
        s = self.xp[i + 1] * u[i + 2] + self.xm[i] * u[i]
        s = s + (self.yp[i] * up(v, 1, 0) + down(self.ym[i] * v, 1, 0))
        return s + (self.zp[i] * up(v, self.step, 1) + down(self.zm[i] * v, self.step, 1))

    def start(self):
        zero = jnp.zeros((self.ny, LANES), jnp.float32)
        for ref in (self.u, self.v):
            ref[0], ref[self.nx + 1] = zero, zero

        def body(i, _):
            wf = self.w[i] * self.f[i]
            self.wf[i] = wf
            self.u[i + 1] = wf
            return 0

        loop(0, self.nx, body, 0)

    def sweep(self, u, v):
        def body(i, _):
            v[i + 1] = (1.0 - OMEGA) * u[i + 1] + self.wf[i] + self.w[i] * self.coupled(u, i)
            return 0

        loop(0, self.nx, body, 0)

    def halve(self, tmp, v):
        step, ny = self.step, self.ny
        tmp[0:ny] = v
        v = tmp[pl.ds(0, ny // 2, stride=2), :] + tmp[pl.ds(1, ny // 2, stride=2), :]
        other = jnp.where(low_lane(v.shape, step), up(v, step, 1), down(v, step, 1))
        return 0.125 * (v + other)

    def descend_fields(self, coarser, tmp):
        def body(i, _):
            for here, there in ((self.eps, coarser.eps), (self.pot, coarser.pot), (self.cap, coarser.cap)):
                there[i] = self.halve(tmp, here[2 * i] + here[2 * i + 1])
            return 0

        loop(0, coarser.nx, body, 0)

    def descend_residual(self, u, coarser, tmp):
        def residual(i):
            return self.f[i] - self.d[i] * u[i + 1] + self.coupled(u, i)

        def body(i, _):
            coarser.f[i] = self.halve(tmp, residual(2 * i) + residual(2 * i + 1))
            return 0

        loop(0, coarser.nx, body, 0)

    def correct(self, u, coarser_u, tmp):
        half_ny = self.ny // 2

        def body(i, _):
            e = coarser_u(i)
            tmp[pl.ds(0, half_ny, stride=2), :] = e
            tmp[pl.ds(1, half_ny, stride=2), :] = e
            wide = tmp[0 : self.ny]
            u[2 * i + 1] = u[2 * i + 1] + wide
            u[2 * i + 2] = u[2 * i + 2] + wide
            return 0

        loop(0, self.nx // 2, body, 0)


def coarsest(lv):
    nx, step = lv.nx, lv.step
    cxp = [lv.w[i] * lv.xp[i + 1] for i in range(nx)]
    cxm = [lv.w[i] * lv.xm[i] for i in range(nx)]
    cyp = [lv.w[i] * lv.yp[i] for i in range(nx)]
    cym = [lv.w[i] * down(lv.ym[i], 1, 0) for i in range(nx)]
    czp = [lv.w[i] * lv.zp[i] for i in range(nx)]
    czm = [lv.w[i] * down(lv.zm[i], step, 1) for i in range(nx)]
    wf = [lv.w[i] * lv.f[i] for i in range(nx)]

    def body(_, u):
        new = []
        for i in range(nx):
            s = czp[i] * up(u[i], step, 1) + czm[i] * down(u[i], step, 1)
            t = cyp[i] * up(u[i], 1, 0) + cym[i] * down(u[i], 1, 0)
            r = (1.0 - OMEGA) * u[i] + wf[i]
            if i + 1 < nx:
                r = r + cxp[i] * u[i + 1]
            if i > 0:
                r = r + cxm[i] * u[i - 1]
            new.append(r + t + s)
        return tuple(new)

    u = tuple(wf)
    for _ in range(COARSE_ITERS - 1):
        u = body(0, u)
    for i in range(nx):
        lv.u[i + 1] = u[i]


def place(bits, y_bits, ref, flip, x, y, ny, put):
    bx, by = ref.shape[-3], ref.shape[-2]

    def body(m, _):
        b = m // ny
        to_x = x ^ flip
        for k, bit in enumerate(bits[:-1]):
            to_x = to_x ^ (((b >> k) & 1) * bit)
        to_y = y
        for k, bit in enumerate(y_bits):
            to_y = to_y ^ (((m >> k) & 1) * bit)
        row = pl.ds(pl.multiple_of(to_y * by, by), by)
        for i in range(bx):
            put(m, i, to_x * bx + i, row)
        return 0

    loop(0, ref.shape[0], body, 0)


def operators_kernel(bits, y_bits, near, far, *refs):
    x, y, ny = lax.axis_index("gx"), lax.axis_index("gy"), lax.axis_size("gy")
    outs, scratch = refs[: 3 * OPERATOR], refs[3 * OPERATOR :]
    l1, l2, l3 = (
        Level(k + 1, outs[OPERATOR * k : OPERATOR * (k + 1)] + scratch[3 * k : 3 * k + 3]) for k in range(3)
    )
    tmp = scratch[9]
    right = iota((near.shape[-2], LANES), 1) >= LANES // 2
    for ref, flip in ((near, 0), (far, bits[-1])):

        def put(m, i, at, row, ref=ref):
            q = ref[m, 1, i]
            l1.eps[at, row, :] = ref[m, 0, i]
            l1.pot[at, row, :] = jnp.where(right, q, 0.0)
            l1.cap[at, row, :] = jnp.where(right, down(q, LANES // 2, 1), 0.0)

        place(bits, y_bits, ref, flip, x, y, ny, put)
    l1.assemble()
    l1.descend_fields(l2, tmp)
    l2.assemble()
    l2.descend_fields(l3, tmp)
    l3.assemble()


def second_kernel(bits, y_bits, near, far, kept, *refs):
    x, y, ny = lax.axis_index("gx"), lax.axis_index("gy"), lax.axis_size("gy")
    given, (out_p, out_n), scratch = refs[: 3 * OPERATOR], refs[3 * OPERATOR : 3 * OPERATOR + 2], refs[3 * OPERATOR + 2 :]
    l1, l2, l3 = (
        Level(k + 1, given[OPERATOR * k : OPERATOR * (k + 1)] + scratch[4 * k : 4 * k + 4]) for k in range(3)
    )
    sol, tmp, fine_a, fine_b = scratch[12:]
    bx, by = near.shape[-3], near.shape[-2]
    for ref, flip in ((near, 0), (far, bits[-1])):

        def put(m, i, at, row, ref=ref):
            l1.f[at, row, :] = ref[m, i]

        place(bits, y_bits, ref, flip, x, y, ny, put)
    for here, there in ((l1, l2), (l2, l3)):
        here.start()
        here.sweep(here.u, here.v)
        here.descend_residual(here.v, there, tmp)
    coarsest(l3)
    l2.correct(l2.v, lambda i: l3.u[i + 1], tmp)
    l2.sweep(l2.v, l2.u)
    l2.sweep(l2.u, l2.v)
    l1.correct(l1.v, lambda i: l2.v[i + 1], tmp)
    l1.sweep(l1.v, l1.u)
    edge = jnp.zeros((by, LANES), jnp.float32)
    n1x, n1y = l1.nx, l1.ny
    blank = jnp.zeros((n1y + 2 * by, LANES), jnp.float32)
    sol[0], sol[n1x + 1] = blank, blank

    def last(i, _):
        sol[i + 1, 0:by] = edge
        sol[i + 1, by + n1y :] = edge
        sol[i + 1, by : by + n1y] = (
            (1.0 - OMEGA) * l1.u[i + 1] + l1.wf[i] + l1.w[i] * l1.coupled(l1.u, i)
        )
        return 0

    loop(0, n1x, last, 0)

    rows = kept.shape[2]
    own = rows - 2 * RIM
    tile_row = iota((by, LANES), 0)
    spread = iota((by, LANES), 1) // 2

    def widen(v, channel):
        return jnp.take_along_axis(v, spread + channel * (LANES // 2), axis=1)

    def correct(i, _):
        at = x * bx + i
        middle, above, below = (
            sol[at, pl.ds(pl.multiple_of((y + k) * by, by), by), :] for k in (1, 2, 0)
        )
        rim = jnp.where(
            tile_row < 2,
            jnp.broadcast_to(above[0:1], (by, LANES)),
            jnp.where(tile_row >= by - 2, jnp.broadcast_to(below[by - 1 : by], (by, LANES)), 0.0),
        )
        for channel, u in ((0, U_P), (1, U_N)):
            e = widen(middle, channel)
            tmp[pl.ds(0, by, stride=2), :] = e
            tmp[pl.ds(1, by, stride=2), :] = e
            tmp[own:rows] = widen(rim, channel)
            e = tmp[0:rows]
            for k in (0, 1):
                p = RIM - 2 + 2 * i + k
                fine_a[channel, p] = kept[u, p] + e
        return 0

    loop(0, bx + 2, correct, 0)

    def fine(u, channel, i):
        w, wf = ((W_P, WF_P), (W_N, WF_N))[channel]
        s = coupled_fine(kept, lambda j: u[channel, j], i, channel == 0)
        return (1.0 - OMEGA) * u[channel, i] + kept[wf, i] + kept[w, i] * s

    def post_one(i, _):
        for channel in (0, 1):
            fine_b[channel, i] = fine(fine_a, channel, i)
        return 0

    def post_two(i, _):
        out_p[i] = fine(fine_b, 0, i + RIM)[0:own]
        out_n[i] = fine(fine_b, 1, i + RIM)[0:own]
        return 0

    loop(RIM - 1, RIM + 2 * bx + 1, post_one, 0)
    loop(0, 2 * bx, post_two, 0)


def moves(ng, nx, ny):
    def of(partner):
        place = {p: k for k, p in enumerate(itertools.product(range(ng), range(nx), range(ny)))}
        return [(k, place[partner(*p)]) for p, k in place.items()]

    def other(k):
        return k + 1 if k % 2 else k - 1

    return {
        "xa": of(lambda g, a, b: (g, a ^ 1, b)),
        "xb": of(lambda g, a, b: (g, other(a), b) if 0 < a < nx - 1 else (g ^ 1, a, b)),
        "ya": of(lambda g, a, b: (g, a, b ^ 1)),
        "yb": of(lambda g, a, b: (g, a, other(b)) if 0 < b < ny - 1 else (g, a ^ 1, b)),
        **{("x", 1 << k): of(lambda g, a, b, k=k: (g, a ^ (1 << k), b)) for k in range((nx - 1).bit_length())},
        **{("y", 1 << k): of(lambda g, a, b, k=k: (g, a, b ^ (1 << k))) for k in range((ny - 1).bit_length())},
    }


def per_device(ng, nx, ny, layer_class, permittivity, mobility, capture, potential, rhs_psi, rhs_n):
    send = moves(ng, nx, ny)
    f32 = jnp.float32

    def permute(v, name):
        return lax.ppermute(v, ("groups", "gx", "gy"), send[name])

    planes, own = layer_class.shape[0], layer_class.shape[1]
    rows, total = own + 2 * RIM, planes + 2 * RIM
    bx, by = planes // 2, own // 2
    def shape(*dims):
        return jax.ShapeDtypeStruct(dims, f32)

    table = jnp.stack([permittivity, mobility, capture])
    table = jnp.broadcast_to(table[:, :, None], (*table.shape, LANES))
    cell = (planes, own, LANES)
    a, b, fields, *raw = pl.pallas_call(
        rim_y_kernel,
        out_shape=[
            shape(2 * planes, by, LANES),
            shape(2 * planes, by, LANES),
            shape(1, 2, bx, by, LANES),
        ]
        + [shape(*cell)] * 4,
        in_specs=[VMEM] + [HBM] * 4,
        out_specs=[VMEM] * 7,
        scratch_shapes=[
            pltpu.VMEM(cell, jnp.int32),
            pltpu.VMEM((4, bx, own, LANES), f32),
            pltpu.SemaphoreType.DMA((4,)),
        ],
        compiler_params=params(53.5),
    )(table, layer_class, potential, rhs_psi, rhs_n)
    b = permute(b, "yb")
    a = permute(jnp.concatenate([a, fields.reshape(-1, by, LANES)]), "ya")
    fields_y = [fields, a[2 * planes :].reshape(fields.shape)]
    mid, a, b = pl.pallas_call(
        rim_x_kernel,
        out_shape=[shape(4, planes, rows, LANES)] + [shape(4 * RIM - 2, rows, LANES)] * 2,
        in_specs=[VMEM] * 6,
        out_specs=[VMEM] * 3,
        compiler_params=params(16),
    )(*raw, a, b)
    fields_y, _ = lax.optimization_barrier((jnp.concatenate(fields_y), mid))
    b = permute(b, "xb")
    a = permute(a, "xa")
    kept, block = pl.pallas_call(
        first_kernel,
        out_shape=[shape(KEPT, total, rows, LANES), shape(1, bx, by, LANES)],
        in_specs=[VMEM] * 4,
        out_specs=[VMEM] * 2,
        scratch_shapes=[
            pltpu.VMEM((8, total, rows, LANES), f32),
            pltpu.VMEM((2, bx, own, LANES), f32),
        ],
        compiler_params=params(24),
    )(table, mid, a, b)

    bits = [1 << k for k in reversed(range((nx - 1).bit_length()))]

    def over_y(near, line):
        for bit in line:
            near = jnp.concatenate([near, permute(near, ("y", bit))])
        return near

    def over_x(near):
        for bit in bits[:-1]:
            near = jnp.concatenate([near, permute(near, ("x", bit))], axis=0)
        return near, permute(near, ("x", bits[-1]))

    halves = [fields_y, permute(fields_y, ("y", 2))]
    y_bits = tuple(1 << k for k in range((ny - 1).bit_length()))
    y_turn = (2, 1) + y_bits[2:]
    pair = jnp.concatenate([block, permute(block, ("y", 2))])
    halves, _ = lax.optimization_barrier((halves, pair))
    fields_y = over_y(jnp.concatenate(halves), y_bits[2:])
    grids = [(bx * nx >> level, by * ny >> level) for level in range(3)]
    large = grids[0][0] * grids[0][1] > 1024
    operators = pl.pallas_call(
        functools.partial(operators_kernel, tuple(bits), y_bits),
        out_shape=[shape(*s) for g in grids for s in Level.operator(*g)],
        in_specs=[VMEM] * 2,
        out_specs=[VMEM] * (3 * OPERATOR),
        scratch_shapes=[pltpu.VMEM(s, f32) for g in grids for s in Level.fields(*g)]
        + [pltpu.VMEM((grids[0][1], LANES), f32)],
        compiler_params=params(60 if large else 16),
    )(*over_x(fields_y))
    near, far = over_x(over_y(pair, y_turn[1:]))
    return pl.pallas_call(
        functools.partial(second_kernel, tuple(bits), y_turn),
        out_shape=[shape(planes, own, LANES)] * 2,
        in_specs=[VMEM] * (3 + 3 * OPERATOR),
        out_specs=[VMEM] * 2,
        scratch_shapes=[pltpu.VMEM(s, f32) for g in grids for s in Level.iterates(*g)]
        + [
            pltpu.VMEM((grids[0][0] + 2, grids[0][1] + 2 * by, LANES), f32),
            pltpu.VMEM((max(grids[0][1], rows), LANES), f32),
            pltpu.VMEM((2, total, rows, LANES), f32),
            pltpu.VMEM((2, total, rows, LANES), f32),
        ],
        compiler_params=params(60 if large else 16),
    )(near, far, kept, *operators)


def solution(mesh):
    grid = P(("groups", "gx"), "gy", None)
    fn = functools.partial(per_device, *(mesh.shape[a] for a in ("groups", "gx", "gy")))
    return jax.shard_map(
        fn,
        mesh=mesh,
        in_specs=(grid, P(), P(), P(), grid, grid, grid),
        out_specs=(grid, grid),
        check_vma=False,
    )
```

```python
import functools
import itertools
import jax
import jax.numpy as jnp
from jax import lax
from jax.experimental import pallas as pl
from jax.experimental.pallas import tpu as pltpu
from jax.sharding import PartitionSpec as P

OMEGA = 0.8
COARSE_ITERS = 20
RIM = 4
LANES = 128
RIM_PLANES = ((0, RIM), (RIM, RIM), (2 * RIM, RIM - 1), (3 * RIM - 1, RIM - 1))
VMEM = pl.BlockSpec(memory_space=pltpu.VMEM)
HBM = pl.BlockSpec(memory_space=pltpu.HBM)


UNROLL = 16


def loop(first, end, body, init):
    if end - first > UNROLL:
        return lax.fori_loop(first, end, body, init)
    for i in range(first, end):
        body(i, 0)
    return init


def params(mib):
    return pltpu.CompilerParams(vmem_limit_bytes=int(mib * 1024 * 1024))


def bernoulli(x):
    t = x * x
    series = (1.0 - 0.5 * x) + t * (1 / 12 - t * (1 / 720))
    near = t < 0.0625
    guarded = jnp.where(near, 1.0, x)
    return jnp.where(near, series, guarded / (jnp.exp(guarded) - 1.0))


def iota(shape, dim):
    return lax.broadcasted_iota(jnp.int32, shape, dim)


def up(v, step, dim):
    return pltpu.roll(v, v.shape[dim] - step, dim)


def down(v, step, dim):
    return pltpu.roll(v, step, dim)


def halve_lanes(a, b):
    lane = iota(a.shape, 1)
    at = (2 * lane) % LANES
    a = jnp.take_along_axis(a + up(a, 1, 1), at, axis=1)
    b = jnp.take_along_axis(b + up(b, 1, 1), at, axis=1)
    return jnp.where(lane < LANES // 2, a, b)


def look_up(table, c, shape):
    found = [jnp.zeros(shape, jnp.float32)] * 3
    for k in range(table.shape[1]):
        same = c == float(k)
        found = [
            jnp.where(same, jnp.broadcast_to(table[f, k : k + 1], shape), found[f]) for f in range(3)
        ]
    return found


def rim_y_kernel(table, c_in, p_in, fp_in, fn_in, out_a, out_b, block, c_out, p_out, fp_out, fn_out, cls, work, sems):
    outs = (c_out, p_out, fp_out, fn_out)
    copies = [
        pltpu.make_async_copy(s, d, sems.at[k])
        for k, (s, d) in enumerate(zip((c_in, p_in, fp_in, fn_in), (cls, *outs[1:])))
    ]
    for c in copies:
        c.start()
    for c in copies:
        c.wait()
    c_out[...] = cls[...].astype(jnp.float32)
    even = lax.axis_index("gy") % 2 == 0
    planes, length = cls.shape[0], cls.shape[1]
    for pair in range(2):
        lo, hi = (
            jnp.concatenate([r[:, at : at + RIM, :] for r in outs[2 * pair : 2 * pair + 2]], axis=1)
            for at in (0, length - RIM)
        )
        out_a[pair * planes : (pair + 1) * planes] = jnp.where(even, hi, lo)
        out_b[pair * planes : (pair + 1) * planes] = jnp.where(even, lo, hi)
    bx = planes // 2
    for i in range(bx):
        one, two = (look_up(table, c_out[2 * i + k], (length, LANES)) for k in (0, 1))
        values = [p + q for p, q in zip(one, two)] + [p_out[2 * i] + p_out[2 * i + 1]]
        for k, v in enumerate(values):
            work[k, i] = v
    for i in range(bx):
        eps, mob, cap, pot = (
            work[k, i, pl.ds(0, length // 2, stride=2), :] + work[k, i, pl.ds(1, length // 2, stride=2), :]
            for k in range(4)
        )
        for f, v in enumerate((halve_lanes(eps, mob), halve_lanes(cap, pot))):
            block[0, f, i] = 0.125 * v


def rim_x_kernel(cls, pot, fp, fn, in_a, in_b, out, out_a, out_a2, out_b):
    y, ny = lax.axis_index("gy"), lax.axis_size("gy")
    even_x, even_y = lax.axis_index("gx") % 2 == 0, y % 2 == 0
    planes, length = cls.shape[0], cls.shape[1]
    row = iota((planes, 2 * RIM, LANES), 1)
    for pair in range(2):
        a, b = (r[pair * planes : (pair + 1) * planes] for r in (in_a, in_b))
        hi, lo = jnp.where(even_y, a, b), jnp.where(even_y, b, a)
        for slot in range(2):
            field = 2 * pair + slot
            outside = -1.0 if field == 0 else 0.0
            h, l = jnp.where(y == ny - 1, outside, hi), jnp.where(y == 0, outside, lo)
            if slot == 0:
                l = down(l, RIM, 1)
            else:
                h = down(h, RIM, 1)
            out[field, :, 0:length, :] = (cls, pot, fp, fn)[field][...]
            out[field, :, length : length + 2 * RIM, :] = jnp.where(row < RIM, h, l)
        for slot in range(2):
            field = 2 * pair + slot
            at, n = RIM_PLANES[field]
            lo_x, hi_x = out[field, 0:n], out[field, planes - n : planes]
            half, start = (out_a, at) if pair == 0 else (out_a2, at - 2 * RIM)
            half[start : start + n] = jnp.where(even_x, hi_x, lo_x)
            out_b[at : at + n] = jnp.where(even_x, lo_x, hi_x)


W_P, GX, GY, GZ, W_N, XP, XM, YP, YM, ZP, ZM, WF_P, WF_N, U_P, U_N = range(15)
KEPT = 15


def coupled_fine(kept, u, i, poisson):
    v = u(i)
    if poisson:
        xp, xm, yp, ym, zp, zm = GX, GX, GY, GY, GZ, GZ
    else:
        xp, xm, yp, ym, zp, zm = XP, XM, YP, YM, ZP, ZM
    s = kept[xp, i] * u(i + 1) + kept[xm, i - 1] * u(i - 1)
    s = s + (kept[yp, i] * up(v, 1, 0) + down(kept[ym, i] * v, 1, 0))
    return s + (kept[zp, i] * up(v, 1, 1) + down(kept[zm, i] * v, 1, 1))


def first_kernel(table, mid, in_a, in_b, kept, block, fld, work):
    x, nx = lax.axis_index("gx"), lax.axis_size("gx")
    even = x % 2 == 0
    planes = mid.shape[1]
    rows = mid.shape[2]
    own = rows - 2 * RIM
    total = planes + 2 * RIM
    EPS, MOB, POT, CAP, F_P, F_N, D_P, D_N = range(8)

    def materials(i, c, pot, fp, fn):
        eps, mob, cap = look_up(table, c, (rows, LANES))
        fld[EPS, i], fld[MOB, i], fld[POT, i], fld[CAP, i] = eps, mob, pot, cap
        fld[F_P, i], fld[F_N, i] = fp, fn

    def rim(i, ref_even, ref_odd, skip, outside):
        values = []
        for f, (at, n) in enumerate(RIM_PLANES):
            if n < RIM and i == skip:
                values.append(jnp.zeros((rows, LANES), jnp.float32))
                continue
            k = at + i - (1 if n < RIM and skip == 0 else 0)
            v = jnp.where(even, ref_even[k], ref_odd[k])
            values.append(jnp.where(outside, -1.0 if f == 0 else 0.0, v))
        return values

    def low(i, _):
        materials(i, *rim(i, in_b, in_a, 0, x == 0))
        return 0

    def middle(i, _):
        materials(i + RIM, *[mid[f, i] for f in range(4)])
        return 0

    def high(i, _):
        materials(i + RIM + planes, *rim(i, in_a, in_b, RIM - 1, x == nx - 1))
        return 0

    loop(0, RIM, low, 0)
    loop(0, planes, middle, 0)
    loop(0, RIM, high, 0)

    shape = (rows, LANES)
    lane = iota(shape, 1)
    ends = (lane == 0) | (lane == LANES - 1)
    top = lane == LANES - 1

    def x_faces(i):
        eps, mob, pot = fld[EPS, i], fld[MOB, i], fld[POT, i]
        kept[GX, i] = 0.5 * (eps + fld[EPS, i + 1])
        k = 0.5 * (mob + fld[MOB, i + 1])
        delta = fld[POT, i + 1] - pot
        kb = k * bernoulli(delta)
        kept[XP, i] = kb
        kept[XM, i] = kb + k * delta

    x_faces(0)

    def operators(i, _):
        x_faces(i)
        eps, mob, pot = fld[EPS, i], fld[MOB, i], fld[POT, i]
        gy = 0.5 * (eps + up(eps, 1, 0))
        k = 0.5 * (mob + up(mob, 1, 0))
        delta = up(pot, 1, 0) - pot
        yp = k * bernoulli(delta)
        ym = yp + k * delta
        gz = jnp.where(top, 0.0, 0.5 * (eps + up(eps, 1, 1)))
        k = jnp.where(top, 0.0, 0.5 * (mob + up(mob, 1, 1)))
        delta = up(pot, 1, 1) - pot
        zp = k * bernoulli(delta)
        zm = zp + k * delta
        kept[GY, i], kept[YP, i], kept[YM, i] = gy, yp, ym
        kept[GZ, i], kept[ZP, i], kept[ZM, i] = gz, zp, zm
        d_p = (kept[GX, i] + kept[GX, i - 1]) + (gy + down(gy, 1, 0)) + (gz + down(gz, 1, 1))
        d_p = d_p + jnp.where(ends, 0.5 * eps, 0.0)
        d_n = (kept[XM, i] + kept[XP, i - 1]) + (ym + down(yp, 1, 0)) + (zm + down(zp, 1, 1))
        d_n = d_n + jnp.where(ends, 0.5 * mob * bernoulli(pot), 0.0) + fld[CAP, i]
        inside = eps > 0.0
        w_p = jnp.where(inside, OMEGA / jnp.where(inside, d_p, 1.0), 0.0)
        w_n = jnp.where(inside, OMEGA / jnp.where(inside, d_n, 1.0), 0.0)
        kept[W_P, i], kept[W_N, i] = w_p, w_n
        kept[WF_P, i], kept[WF_N, i] = w_p * fld[F_P, i], w_n * fld[F_N, i]
        fld[D_P, i], fld[D_N, i] = d_p, d_n
        return 0

    loop(1, total - 1, operators, 0)

    def sweep(i, _):
        for poisson, w, wf, u in ((True, W_P, WF_P, U_P), (False, W_N, WF_N, U_N)):
            s = coupled_fine(kept, lambda j: kept[wf, j], i, poisson)
            kept[u, i] = (2.0 - OMEGA) * kept[wf, i] + kept[w, i] * s
        return 0

    loop(2, total - 2, sweep, 0)

    def residual(i, poisson, f, d, u):
        s = coupled_fine(kept, lambda j: kept[u, j], i, poisson)
        return fld[f, i] - fld[d, i] * kept[u, i] + s

    def coarse(i, _):
        at = RIM + 2 * i
        r_p = residual(at, True, F_P, D_P, U_P) + residual(at + 1, True, F_P, D_P, U_P)
        r_n = residual(at, False, F_N, D_N, U_N) + residual(at + 1, False, F_N, D_N, U_N)
        work[0, i], work[1, i] = r_p[0:own], r_n[0:own]
        r_p, r_n = (
            work[k, i, pl.ds(0, own // 2, stride=2), :] + work[k, i, pl.ds(1, own // 2, stride=2), :]
            for k in range(2)
        )
        block[0, i] = 0.125 * halve_lanes(r_p, r_n)
        return 0

    loop(0, planes // 2, coarse, 0)


def low_lane(shape, bit):
    return (iota(shape, 1) & bit) == 0


OPERATOR = 8


class Level:
    def __init__(self, level, refs):
        self.level, self.step, self.factor = level, 1 << (level - 1), 0.25**level
        (self.xp, self.xm, self.yp, self.ym, self.zp, self.zm, self.w, self.d) = refs[:OPERATOR]
        if len(refs) == OPERATOR + 3:
            self.eps, self.pot, self.cap = refs[OPERATOR:]
        else:
            self.f, self.wf, self.u, self.v = refs[OPERATOR:]
        self.nx, self.ny = self.w.shape[0], self.w.shape[1]

    @staticmethod
    def operator(nx, ny):
        return [(nx + 1, ny, LANES)] * 2 + [(nx, ny, LANES)] * 6

    @staticmethod
    def fields(nx, ny):
        return [(nx, ny, LANES)] * 3

    @staticmethod
    def iterates(nx, ny):
        return [(nx, ny, LANES)] * 2 + [(nx + 2, ny, LANES)] * 2

    def assemble(self):
        nx, ny, step = self.nx, self.ny, self.step
        shape = (ny, LANES)
        row, spot = iota(shape, 0), iota(shape, 1) % (LANES // 2)
        last_row, top = row == ny - 1, spot >= LANES // 2 - step
        walls = (
            jnp.where(row == 0, 1.0, 0.0)
            + jnp.where(last_row, 1.0, 0.0)
            + jnp.where(spot < step, 1.0, 0.0)
            + jnp.where(top, 1.0, 0.0)
        )
        zero = jnp.zeros(shape, jnp.float32)
        half = 0.5 * self.factor
        for ref in (self.xp, self.xm):
            ref[0], ref[nx] = zero, zero

        def x_face(i, _):
            k = half * (self.eps[i - 1] + self.eps[i])
            delta = self.pot[i] - self.pot[i - 1]
            kb = k * bernoulli(delta)
            self.xp[i], self.xm[i] = kb, kb + k * delta
            return 0

        loop(1, nx, x_face, 0)

        def plane(i, _):
            eps, pot = self.eps[i], self.pot[i]
            k = jnp.where(last_row, 0.0, half * (eps + up(eps, 1, 0)))
            delta = up(pot, 1, 0) - pot
            yp = k * bernoulli(delta)
            ym = yp + k * delta
            k = jnp.where(top, 0.0, half * (eps + up(eps, step, 1)))
            delta = up(pot, step, 1) - pot
            zp = k * bernoulli(delta)
            zm = zp + k * delta
            outer = walls + jnp.where(i == 0, 1.0, 0.0) + jnp.where(i == nx - 1, 1.0, 0.0)
            d = (self.xm[i + 1] + self.xp[i]) + (ym + down(yp, 1, 0)) + (zm + down(zp, step, 1))
            d = d + outer * (half * eps * bernoulli(pot)) + self.cap[i]
            w = OMEGA / d
            self.yp[i], self.ym[i], self.zp[i], self.zm[i] = yp, ym, zp, zm
            self.d[i], self.w[i] = d, w
            return 0

        loop(0, nx, plane, 0)

    def coupled(self, u, i):
        v = u[i + 1]
        s = self.xp[i + 1] * u[i + 2] + self.xm[i] * u[i]
        s = s + (self.yp[i] * up(v, 1, 0) + down(self.ym[i] * v, 1, 0))
        return s + (self.zp[i] * up(v, self.step, 1) + down(self.zm[i] * v, self.step, 1))

    def start(self):
        zero = jnp.zeros((self.ny, LANES), jnp.float32)
        for ref in (self.u, self.v):
            ref[0], ref[self.nx + 1] = zero, zero

        def body(i, _):
            wf = self.w[i] * self.f[i]
            self.wf[i] = wf
            self.u[i + 1] = wf
            return 0

        loop(0, self.nx, body, 0)

    def sweep(self, u, v):
        def body(i, _):
            v[i + 1] = (1.0 - OMEGA) * u[i + 1] + self.wf[i] + self.w[i] * self.coupled(u, i)
            return 0

        loop(0, self.nx, body, 0)

    def halve(self, tmp, v):
        step, ny = self.step, self.ny
        tmp[0:ny] = v
        v = tmp[pl.ds(0, ny // 2, stride=2), :] + tmp[pl.ds(1, ny // 2, stride=2), :]
        other = jnp.where(low_lane(v.shape, step), up(v, step, 1), down(v, step, 1))
        return 0.125 * (v + other)

    def descend_fields(self, coarser, tmp):
        def body(i, _):
            for here, there in ((self.eps, coarser.eps), (self.pot, coarser.pot), (self.cap, coarser.cap)):
                there[i] = self.halve(tmp, here[2 * i] + here[2 * i + 1])
            return 0

        loop(0, coarser.nx, body, 0)

    def descend_residual(self, u, coarser, tmp):
        def residual(i):
            return self.f[i] - self.d[i] * u[i + 1] + self.coupled(u, i)

        def body(i, _):
            coarser.f[i] = self.halve(tmp, residual(2 * i) + residual(2 * i + 1))
            return 0

        loop(0, coarser.nx, body, 0)

    def correct(self, u, coarser_u, tmp):
        half_ny = self.ny // 2

        def body(i, _):
            e = coarser_u(i)
            tmp[pl.ds(0, half_ny, stride=2), :] = e
            tmp[pl.ds(1, half_ny, stride=2), :] = e
            wide = tmp[0 : self.ny]
            u[2 * i + 1] = u[2 * i + 1] + wide
            u[2 * i + 2] = u[2 * i + 2] + wide
            return 0

        loop(0, self.nx // 2, body, 0)


def coarsest(lv):
    nx, step = lv.nx, lv.step
    cxp = [lv.w[i] * lv.xp[i + 1] for i in range(nx)]
    cxm = [lv.w[i] * lv.xm[i] for i in range(nx)]
    cyp = [lv.w[i] * lv.yp[i] for i in range(nx)]
    cym = [lv.w[i] * down(lv.ym[i], 1, 0) for i in range(nx)]
    czp = [lv.w[i] * lv.zp[i] for i in range(nx)]
    czm = [lv.w[i] * down(lv.zm[i], step, 1) for i in range(nx)]
    wf = [lv.w[i] * lv.f[i] for i in range(nx)]

    def body(_, u):
        new = []
        for i in range(nx):
            s = czp[i] * up(u[i], step, 1) + czm[i] * down(u[i], step, 1)
            t = cyp[i] * up(u[i], 1, 0) + cym[i] * down(u[i], 1, 0)
            r = (1.0 - OMEGA) * u[i] + wf[i]
            if i + 1 < nx:
                r = r + cxp[i] * u[i + 1]
            if i > 0:
                r = r + cxm[i] * u[i - 1]
            new.append(r + t + s)
        return tuple(new)

    u = tuple(wf)
    for _ in range(COARSE_ITERS - 1):
        u = body(0, u)
    for i in range(nx):
        lv.u[i + 1] = u[i]


def place(bits, y_bits, ref, flip, x, y, ny, put):
    bx, by = ref.shape[-3], ref.shape[-2]

    def body(m, _):
        b = m // ny
        to_x = x ^ flip
        for k, bit in enumerate(bits[:-1]):
            to_x = to_x ^ (((b >> k) & 1) * bit)
        to_y = y
        for k, bit in enumerate(y_bits):
            to_y = to_y ^ (((m >> k) & 1) * bit)
        row = pl.ds(pl.multiple_of(to_y * by, by), by)
        for i in range(bx):
            put(m, i, to_x * bx + i, row)
        return 0

    loop(0, ref.shape[0], body, 0)


def operators_kernel(bits, y_bits, near, far, *refs):
    x, y, ny = lax.axis_index("gx"), lax.axis_index("gy"), lax.axis_size("gy")
    outs, scratch = refs[: 3 * OPERATOR], refs[3 * OPERATOR :]
    l1, l2, l3 = (
        Level(k + 1, outs[OPERATOR * k : OPERATOR * (k + 1)] + scratch[3 * k : 3 * k + 3]) for k in range(3)
    )
    tmp = scratch[9]
    right = iota((near.shape[-2], LANES), 1) >= LANES // 2
    for ref, flip in ((near, 0), (far, bits[-1])):

        def put(m, i, at, row, ref=ref):
            q = ref[m, 1, i]
            l1.eps[at, row, :] = ref[m, 0, i]
            l1.pot[at, row, :] = jnp.where(right, q, 0.0)
            l1.cap[at, row, :] = jnp.where(right, down(q, LANES // 2, 1), 0.0)

        place(bits, y_bits, ref, flip, x, y, ny, put)
    l1.assemble()
    l1.descend_fields(l2, tmp)
    l2.assemble()
    l2.descend_fields(l3, tmp)
    l3.assemble()


def second_kernel(bits, y_bits, near, far, kept, *refs):
    x, y, ny = lax.axis_index("gx"), lax.axis_index("gy"), lax.axis_size("gy")
    given, (out_p, out_n), scratch = refs[: 3 * OPERATOR], refs[3 * OPERATOR : 3 * OPERATOR + 2], refs[3 * OPERATOR + 2 :]
    l1, l2, l3 = (
        Level(k + 1, given[OPERATOR * k : OPERATOR * (k + 1)] + scratch[4 * k : 4 * k + 4]) for k in range(3)
    )
    sol, tmp, fine_a, fine_b = scratch[12:]
    bx, by = near.shape[-3], near.shape[-2]
    for ref, flip in ((near, 0), (far, bits[-1])):

        def put(m, i, at, row, ref=ref):
            l1.f[at, row, :] = ref[m, i]

        place(bits, y_bits, ref, flip, x, y, ny, put)
    for here, there in ((l1, l2), (l2, l3)):
        here.start()
        here.sweep(here.u, here.v)
        here.descend_residual(here.v, there, tmp)
    coarsest(l3)
    l2.correct(l2.v, lambda i: l3.u[i + 1], tmp)
    l2.sweep(l2.v, l2.u)
    l2.sweep(l2.u, l2.v)
    l1.correct(l1.v, lambda i: l2.v[i + 1], tmp)
    l1.sweep(l1.v, l1.u)
    edge = jnp.zeros((by, LANES), jnp.float32)
    n1x, n1y = l1.nx, l1.ny
    blank = jnp.zeros((n1y + 2 * by, LANES), jnp.float32)
    sol[0], sol[n1x + 1] = blank, blank

    def last(i, _):
        sol[i + 1, 0:by] = edge
        sol[i + 1, by + n1y :] = edge
        sol[i + 1, by : by + n1y] = (
            (1.0 - OMEGA) * l1.u[i + 1] + l1.wf[i] + l1.w[i] * l1.coupled(l1.u, i)
        )
        return 0

    loop(0, n1x, last, 0)

    rows = kept.shape[2]
    own = rows - 2 * RIM
    tile_row = iota((by, LANES), 0)
    spread = iota((by, LANES), 1) // 2

    def widen(v, channel):
        return jnp.take_along_axis(v, spread + channel * (LANES // 2), axis=1)

    def correct(i, _):
        at = x * bx + i
        middle, above, below = (
            sol[at, pl.ds(pl.multiple_of((y + k) * by, by), by), :] for k in (1, 2, 0)
        )
        rim = jnp.where(
            tile_row < 2,
            jnp.broadcast_to(above[0:1], (by, LANES)),
            jnp.where(tile_row >= by - 2, jnp.broadcast_to(below[by - 1 : by], (by, LANES)), 0.0),
        )
        for channel, u in ((0, U_P), (1, U_N)):
            e = widen(middle, channel)
            tmp[pl.ds(0, by, stride=2), :] = e
            tmp[pl.ds(1, by, stride=2), :] = e
            tmp[own:rows] = widen(rim, channel)
            e = tmp[0:rows]
            for k in (0, 1):
                p = RIM - 2 + 2 * i + k
                fine_a[channel, p] = kept[u, p] + e
        return 0

    loop(0, bx + 2, correct, 0)

    def fine(u, channel, i):
        w, wf = ((W_P, WF_P), (W_N, WF_N))[channel]
        s = coupled_fine(kept, lambda j: u[channel, j], i, channel == 0)
        return (1.0 - OMEGA) * u[channel, i] + kept[wf, i] + kept[w, i] * s

    def post_one(i, _):
        for channel in (0, 1):
            fine_b[channel, i] = fine(fine_a, channel, i)
        return 0

    def post_two(i, _):
        out_p[i] = fine(fine_b, 0, i + RIM)[0:own]
        out_n[i] = fine(fine_b, 1, i + RIM)[0:own]
        return 0

    loop(RIM - 1, RIM + 2 * bx + 1, post_one, 0)
    loop(0, 2 * bx, post_two, 0)


def moves(ng, nx, ny):
    def of(partner):
        place = {p: k for k, p in enumerate(itertools.product(range(ng), range(nx), range(ny)))}
        return [(k, place[partner(*p)]) for p, k in place.items()]

    def other(k):
        return k + 1 if k % 2 else k - 1

    return {
        "xa": of(lambda g, a, b: (g, a ^ 1, b)),
        "xb": of(lambda g, a, b: (g, other(a), b) if 0 < a < nx - 1 else (g ^ 1, a, b)),
        "ya": of(lambda g, a, b: (g, a, b ^ 1)),
        "yb": of(lambda g, a, b: (g, a, other(b)) if 0 < b < ny - 1 else (g, a ^ 1, b)),
        **{("x", 1 << k): of(lambda g, a, b, k=k: (g, a ^ (1 << k), b)) for k in range((nx - 1).bit_length())},
        **{("y", 1 << k): of(lambda g, a, b, k=k: (g, a, b ^ (1 << k))) for k in range((ny - 1).bit_length())},
    }


def per_device(ng, nx, ny, layer_class, permittivity, mobility, capture, potential, rhs_psi, rhs_n):
    send = moves(ng, nx, ny)
    f32 = jnp.float32

    def permute(v, name):
        return lax.ppermute(v, ("groups", "gx", "gy"), send[name])

    planes, own = layer_class.shape[0], layer_class.shape[1]
    rows, total = own + 2 * RIM, planes + 2 * RIM
    bx, by = planes // 2, own // 2
    def shape(*dims):
        return jax.ShapeDtypeStruct(dims, f32)

    table = jnp.stack([permittivity, mobility, capture])
    table = jnp.broadcast_to(table[:, :, None], (*table.shape, LANES))
    cell = (planes, own, LANES)
    a, b, fields, *raw = pl.pallas_call(
        rim_y_kernel,
        out_shape=[
            shape(2 * planes, by, LANES),
            shape(2 * planes, by, LANES),
            shape(1, 2, bx, by, LANES),
        ]
        + [shape(*cell)] * 4,
        in_specs=[VMEM] + [HBM] * 4,
        out_specs=[VMEM] * 7,
        scratch_shapes=[
            pltpu.VMEM(cell, jnp.int32),
            pltpu.VMEM((4, bx, own, LANES), f32),
            pltpu.SemaphoreType.DMA((4,)),
        ],
        compiler_params=params(53.5),
    )(table, layer_class, potential, rhs_psi, rhs_n)
    b = permute(b, "yb")
    a = permute(jnp.concatenate([a, fields.reshape(-1, by, LANES)]), "ya")
    fields_y = [fields, a[2 * planes :].reshape(fields.shape)]
    mid, a, a2, b = pl.pallas_call(
        rim_x_kernel,
        out_shape=[shape(4, planes, rows, LANES)] + [shape(k, rows, LANES) for k in (2 * RIM, 2 * RIM - 2, 4 * RIM - 2)],
        in_specs=[VMEM] * 6,
        out_specs=[VMEM] * 4,
        compiler_params=params(16),
    )(*raw, a, b)
    fields_y, _ = lax.optimization_barrier((jnp.concatenate(fields_y), mid))
    b = permute(b, "xb")
    a = permute(jnp.concatenate([a, a2]), "xa")
    kept, block = pl.pallas_call(
        first_kernel,
        out_shape=[shape(KEPT, total, rows, LANES), shape(1, bx, by, LANES)],
        in_specs=[VMEM] * 4,
        out_specs=[VMEM] * 2,
        scratch_shapes=[
            pltpu.VMEM((8, total, rows, LANES), f32),
            pltpu.VMEM((2, bx, own, LANES), f32),
        ],
        compiler_params=params(24),
    )(table, mid, a, b)

    bits = [1 << k for k in reversed(range((nx - 1).bit_length()))]

    def over_y(near, line):
        for bit in line:
            near = jnp.concatenate([near, permute(near, ("y", bit))])
        return near

    def over_x(near):
        for bit in bits[:-1]:
            near = jnp.concatenate([near, permute(near, ("x", bit))], axis=0)
        return near, permute(near, ("x", bits[-1]))

    halves = [fields_y, permute(fields_y, ("y", 2))]
    y_bits = tuple(1 << k for k in range((ny - 1).bit_length()))
    y_turn = (2, 1) + y_bits[2:]
    pair = jnp.concatenate([block, permute(block, ("y", 2))])
    halves, _ = lax.optimization_barrier((halves, pair))
    fields_y = over_y(jnp.concatenate(halves), y_bits[2:])
    grids = [(bx * nx >> level, by * ny >> level) for level in range(3)]
    large = grids[0][0] * grids[0][1] > 1024
    operators = pl.pallas_call(
        functools.partial(operators_kernel, tuple(bits), y_bits),
        out_shape=[shape(*s) for g in grids for s in Level.operator(*g)],
        in_specs=[VMEM] * 2,
        out_specs=[VMEM] * (3 * OPERATOR),
        scratch_shapes=[pltpu.VMEM(s, f32) for g in grids for s in Level.fields(*g)]
        + [pltpu.VMEM((grids[0][1], LANES), f32)],
        compiler_params=params(60 if large else 16),
    )(*over_x(fields_y))
    near, far = over_x(over_y(pair, y_turn[1:]))
    return pl.pallas_call(
        functools.partial(second_kernel, tuple(bits), y_turn),
        out_shape=[shape(planes, own, LANES)] * 2,
        in_specs=[VMEM] * (3 + 3 * OPERATOR),
        out_specs=[VMEM] * 2,
        scratch_shapes=[pltpu.VMEM(s, f32) for g in grids for s in Level.iterates(*g)]
        + [
            pltpu.VMEM((grids[0][0] + 2, grids[0][1] + 2 * by, LANES), f32),
            pltpu.VMEM((max(grids[0][1], rows), LANES), f32),
            pltpu.VMEM((2, total, rows, LANES), f32),
            pltpu.VMEM((2, total, rows, LANES), f32),
        ],
        compiler_params=params(60 if large else 16),
    )(near, far, kept, *operators)


def solution(mesh):
    grid = P(("groups", "gx"), "gy", None)
    fn = functools.partial(per_device, *(mesh.shape[a] for a in ("groups", "gx", "gy")))
    return jax.shard_map(
        fn,
        mesh=mesh,
        in_specs=(grid, P(), P(), P(), grid, grid, grid),
        out_specs=(grid, grid),
        check_vma=False,
    )
```
